32 devices in a mesh: groups: 1, slab: 32 (over z, y, x, core).
Axes of the slice: x: 2, y: 2, z: 4, core: 2. Of those that a mesh axis runs over, the one named last changes fastest.
Arguments:
- velocity: float32 [3, 128, 64, 256], P(None, ('groups', 'slab')), may hold values from -6 to 6
- pressure_shift: float32 [128, 64, 256], P(('groups', 'slab')), may hold values from 0.02 to 0.5
- owner_rank: int32 [32768, 1], P(('groups', 'slab')), may hold values from 0 to 31; in each aligned block of 1024 rows (0 to 1023, 1024 to 2047, ...) at most 32 rows name the same one
- node_index: int32 [32768], P(('groups', 'slab')), may hold values from 0 to 8191
- map_weight: int32 [32768], P(('groups', 'slab')), may hold values from 1 to 8
- shell_load: float32 [3, 256, 1024], P(None, ('groups', 'slab')), may hold values from -4 to 4
- shell_stiffness: float32 [256, 1024], P(('groups', 'slab')), may hold values from 0.02 to 0.5
- displacement: float32 [3, 256, 1024], P(None, ('groups', 'slab')), may hold values from -6 to 6
- residual_prev: float32 [3, 256, 1024], P(None, ('groups', 'slab')), may hold values from -6 to 6
- solved_prev: float32 [3, 256, 1024], P(None, ('groups', 'slab')), may hold values from -6 to 6
- residual_history: float32 [4, 3, 256, 1024], P(None, None, ('groups', 'slab')), may hold values from -12 to 12, as said below
- solved_history: float32 [4, 3, 256, 1024], P(None, None, ('groups', 'slab')), may hold values from -6 to 6
Outputs:
- pressure: float32 [128, 64, 256], P(('groups', 'slab'))
- new_displacement: float32 [3, 256, 1024], P(None, ('groups', 'slab'))
- wall_displacement: float32 [3, 32768], P(None, ('groups', 'slab'))
The draws below stay inside these ranges and needn't reach their ends.
Inputs may be any that keep to these rules, and one draw needn't show every extreme that they name: `owner_rank`: among the 1024 wall cells of one device at most 32 name the same owner, and some device has exactly 32 cells with one owner. `residual_history`: independent entries.
All inputs are finite; a program needn't handle non-finite values.
Results may differ from the reference program's by a relative error of at most 0.0001.
Values sent between devices are 32-bit elements; how exact they have to be, the bound alone decides.
No kernel may reach another device: no remote copies, remote signals or barrier semaphores. Data moves between devices by JAX's collectives and lax.ppermute only.
A program may use at most 320 MiB of HBM per device.

```python
import math
import jax
import jax.numpy as jnp
import numpy as np
from jax import lax

NY = 64
NZ = 256
SC = 1024
CAP = 32
PITERS = 5
SITERS = 8
KOLD = 4
KALL = 5
NX = 128
IFACE_DEV = 1024
IFACE = 32768
NODE_DEV = 8192
SROWS = 256
NODES = 262144
N_SLAB = 32


def draw_residual_history(key, part):
    key = jax.random.fold_in(key, 11)
    row_pos = jnp.arange(SROWS, dtype=jnp.float32)
    rising = jnp.exp(jnp.log(3.0) * row_pos / SROWS)[None, None, :, None]
    base = jax.random.truncated_normal(key, -4.0, 4.0, (KOLD, 3, SROWS, SC), jnp.float32)
    return base * rising


def touch_ends(values, rng, smallest, high):
    index_at = [jax.random.randint(jax.random.fold_in(rng, axis), (), 0, length) for axis, length in enumerate(values.shape)]
    main_axis = values.shape.index(max(values.shape))
    beside = index_at[:main_axis] + [(index_at[main_axis] + 1) % values.shape[main_axis]] + index_at[main_axis + 1:]
    return values.at[tuple(index_at)].set(smallest).at[tuple(beside)].set(high)


def block_levels(stream_key, extent, cuts, least, top_value):
    level, own = 1.0, jax.random.fold_in(stream_key, 6)
    for position, shards_of in cuts:
        heights = jnp.exp(jax.random.uniform(jax.random.fold_in(own, position), (shards_of,), jnp.float32, least / len(cuts), top_value / len(cuts)))
        level = level * jnp.repeat(heights, extent[position] // shards_of).reshape([-1 if axis == position else 1 for axis in range(len(extent))])
    return level


def assign_block(own_key, own, number, rows, count, top, most, slope):
    sequence = jax.random.permutation(own_key, count)
    packed, usual = portions_of(count, rows * top, most, slope, True), portions_of(count, rows * top, most, slope, False)
    places = jnp.arange(count)

    def named(sizes, offset_by):
        used = int((sizes > 0).sum())
        fixed = max(1, used // 4)
        passed = fixed + (places - fixed + offset_by * (used - fixed)) % max(1, count - fixed)
        return jnp.zeros((count,), jnp.int32).at[sequence[jnp.where(places < fixed, places, passed)]].set(jnp.asarray(sizes, jnp.int32))

    sizes = jnp.where(number % 4 == 0, named(packed, number // 4), named(usual, number - number // 4 - 1))
    mixed = jax.random.permutation(jax.random.fold_in(own, 3), count)
    giver, taker = mixed[0:count // 2 * 2:2], mixed[1:count // 2 * 2:2]
    room = jnp.minimum(sizes[giver] - 1, most - sizes[taker]) // 2
    room = jnp.where((giver == sequence[0]) | (taker == sequence[0]) | (sizes[taker] == 0), 0, jnp.maximum(room, 0))
    passed = jax.random.randint(jax.random.fold_in(own, 4), (count // 2,), 0, 1 << 20) % (room + 1)
    sizes = sizes.at[giver].add(-passed).at[taker].add(passed)
    members = jnp.searchsorted(jnp.cumsum(sizes), jnp.arange(rows * top), side="right").astype(jnp.int32)
    table = members.reshape(top, rows).T
    table = table[jax.random.permutation(jax.random.fold_in(own, 1), rows)]
    offset_by = jax.random.randint(jax.random.fold_in(own, 2), (rows, 1), 0, top)
    return jnp.take_along_axis(table, (jnp.arange(top)[None, :] + offset_by) % top, axis=1)


def portions_of(number_of, total, reach, skew, full):
    portions = [(1 << 20) // math.isqrt(standing ** skew) + 1 for standing in range(1, number_of + 1)]
    largest = reach if full else min(reach, max(-(-total // number_of), total * portions[0] // sum(portions)))
    least = 1 if total - largest >= number_of - 1 else 0
    holding, surplus = [largest] + [least] * (number_of - 1), total - largest - least * (number_of - 1)
    while surplus > 0:
        movable = [i for i in range(1, number_of) if holding[i] < largest] or [i for i in range(1, number_of) if holding[i] < reach]
        whole, remaining = sum([portions[i] for i in movable]), surplus
        for i in movable:
            addition = min(reach - holding[i], max(1, remaining * portions[i] // whole), surplus)
            holding[i] = holding[i] + addition
            surplus = surplus - addition
    return np.array(holding)


def gaussian(rng, shape, scale, reach, pieces=(), held_as=jnp.bfloat16):
    result = scale * jax.random.normal(rng, shape, jnp.float32)
    if pieces:
        result = result * block_levels(rng, shape, pieces, -0.22, 0.18)
    return jnp.clip(result, -reach, reach).astype(held_as)


def setup_inputs(seed: int = 0, part: int = 0) -> dict:
    arg_keys = jax.random.split(jax.random.key(seed), 13)
    part_keys = jax.random.split(jax.random.fold_in(arg_keys[12], part), 13)
    velocity = gaussian(part_keys[0], (3, NX, NY, NZ), 1.0, 6.0, ((1, 32),), jnp.float32)
    pressure_shift = jnp.clip(jnp.exp(math.log(0.5) - 3.218876 * jax.random.uniform(part_keys[1], (NX, NY, NZ), jnp.float32) ** block_levels(part_keys[1], (NX, NY, NZ), ((0, 32),), -0.2, 0.2)), 0.02, 0.5)
    owner_rank_keys = jax.random.split(jax.random.fold_in(part_keys[2], 1), IFACE // IFACE_DEV)
    owner_rank_turns = jax.random.permutation(jax.random.fold_in(part_keys[2], 3), IFACE // IFACE_DEV)
    owner_rank = jax.vmap(lambda own, number: assign_block(jax.random.fold_in(part_keys[2], 2), own, number, IFACE_DEV, N_SLAB, 1, CAP, 2))(owner_rank_keys, owner_rank_turns).reshape((IFACE, 1))
    node_index = touch_ends(jax.random.randint(part_keys[3], (IFACE,), 0, NODE_DEV), jax.random.fold_in(part_keys[3], 1), 0, NODE_DEV - 1).astype(jnp.int32)
    map_weight = touch_ends(jax.random.randint(part_keys[4], (IFACE,), 1, 9), jax.random.fold_in(part_keys[4], 1), 1, 8).astype(jnp.int32)
    shell_load = gaussian(part_keys[5], (3, SROWS, SC), 0.5, 4.0, ((1, 32),), jnp.float32)
    shell_stiffness = jnp.clip(jnp.exp(math.log(0.5) - 3.218876 * jax.random.uniform(part_keys[6], (SROWS, SC), jnp.float32) ** block_levels(part_keys[6], (SROWS, SC), ((0, 32),), -0.2, 0.2)), 0.02, 0.5)
    displacement = gaussian(part_keys[7], (3, SROWS, SC), 1.0, 6.0, ((1, 32),), jnp.float32)
    residual_prev = gaussian(part_keys[8], (3, SROWS, SC), 1.0, 6.0, ((1, 32),), jnp.float32)
    solved_prev = gaussian(part_keys[9], (3, SROWS, SC), 1.0, 6.0, ((1, 32),), jnp.float32)
    residual_history = draw_residual_history(jax.random.fold_in(jax.random.fold_in(arg_keys[12], part), 71), part)
    solved_history = gaussian(part_keys[11], (KOLD, 3, SROWS, SC), 1.0, 6.0, ((2, 32),), jnp.float32)
    return dict(velocity=velocity, pressure_shift=pressure_shift, owner_rank=owner_rank, node_index=node_index, map_weight=map_weight, shell_load=shell_load, shell_stiffness=shell_stiffness, displacement=displacement, residual_prev=residual_prev, solved_prev=solved_prev, residual_history=residual_history, solved_history=solved_history)


NU = 0.15
MU = 0.5
WALL = 4.0

def fluid_beside(field):
    padded = jnp.pad(field, [(0, 0)] * (field.ndim - 3) + [(1, 1), (1, 1), (1, 1)])
    total = padded[..., 2:, 1:-1, 1:-1] + padded[..., :-2, 1:-1, 1:-1]
    total = total + padded[..., 1:-1, 2:, 1:-1] + padded[..., 1:-1, :-2, 1:-1]
    return total + padded[..., 1:-1, 1:-1, 2:] + padded[..., 1:-1, 1:-1, :-2]

def shell_apply(field, stiffness):
    padded = jnp.pad(field, ((0, 0), (1, 1), (1, 1)))
    beside = padded[:, 2:, 1:-1] + padded[:, :-2, 1:-1] + padded[:, 1:-1, 2:] + padded[:, 1:-1, :-2]
    return (4.0 + stiffness) * field - beside

def small_solve(gram, target):
    factor = jnp.linalg.cholesky(gram)
    gram_size = gram.shape[0]
    forward = []
    for across in range(gram_size):
        partial_sum = target[across] - sum((factor[across, within] * forward[within] for within in range(across)))
        forward.append(partial_sum / factor[across, across])
    backward = [None] * gram_size
    for across in reversed(range(gram_size)):
        partial_sum = forward[across] - sum((factor[within, across] * backward[within] for within in range(across + 1, gram_size)))
        backward[across] = partial_sum / factor[across, across]
    return jnp.stack(backward)

def reference(velocity, pressure_shift, owner_rank, node_index, map_weight, shell_load, shell_stiffness, displacement, residual_prev, solved_prev, residual_history, solved_history):
    predicted = velocity + NU * (fluid_beside(velocity) - 6.0 * velocity)
    padded = jnp.pad(predicted, ((0, 0), (1, 1), (1, 1), (1, 1)))
    spread = padded[0, 2:, 1:-1, 1:-1] - padded[0, :-2, 1:-1, 1:-1]
    spread = spread + padded[1, 1:-1, 2:, 1:-1] - padded[1, 1:-1, :-2, 1:-1]
    spread = spread + padded[2, 1:-1, 1:-1, 2:] - padded[2, 1:-1, 1:-1, :-2]
    source = -0.5 * spread
    pressure = jnp.zeros_like(source)
    residual = source
    direction = source
    norm_now = jnp.sum(residual * residual)
    for sweep in range(PITERS):
        image = (6.0 + pressure_shift) * direction - fluid_beside(direction)
        step_size = norm_now / jnp.sum(direction * image)
        pressure = pressure + step_size * direction
        residual = residual - step_size * image
        norm_next = jnp.sum(residual * residual)
        direction = residual + norm_next / norm_now * direction
        norm_now = norm_next
    traction = jnp.stack([MU * (predicted[0, :, 1, :] - predicted[0, :, 0, :]), WALL * pressure[:, 0, :], MU * (predicted[2, :, 1, :] - predicted[2, :, 0, :])]).reshape(3, IFACE)
    nodes = owner_rank[:, 0] * NODE_DEV + node_index
    scaled = map_weight.astype(jnp.float32)
    totals = jax.ops.segment_sum((traction * scaled[None, :]).T, nodes, num_segments=NODES)
    weights_sum = jax.ops.segment_sum(scaled, nodes, num_segments=NODES)
    force = (totals / jnp.maximum(weights_sum, 1.0)[:, None]).T.reshape(3, SROWS, SC)
    shell_source = force + shell_load
    solved = displacement
    residual = shell_source - shell_apply(solved, shell_stiffness)
    direction = residual
    norm_now = jnp.sum(residual * residual)
    for sweep in range(SITERS):
        image = shell_apply(direction, shell_stiffness)
        step_size = norm_now / jnp.sum(direction * image)
        solved = solved + step_size * direction
        residual = residual - step_size * image
        norm_next = jnp.sum(residual * residual)
        direction = residual + norm_next / norm_now * direction
        norm_now = norm_next
    moved = solved - displacement
    newest_v = moved - residual_prev
    newest_w = solved - solved_prev
    columns = jnp.concatenate([newest_v[None], residual_history], 0).reshape(KALL, -1)
    outputs_w = jnp.concatenate([newest_w[None], solved_history], 0)
    gram = jnp.dot(columns, columns.T, precision=lax.Precision.HIGHEST)
    target = jnp.dot(columns, moved.reshape(-1), precision=lax.Precision.HIGHEST)
    coefficients = -small_solve(gram, target)
    new_displacement = solved + jnp.einsum('k,kabc->abc', coefficients, outputs_w, precision=lax.Precision.HIGHEST)
    wall_displacement = new_displacement.reshape(3, NODES)[:, nodes]
    return (pressure, new_displacement, wall_displacement)
```

```python
import jax
import jax.numpy as jnp
from jax import lax
from jax.experimental import pallas as pl
from jax.experimental.pallas import tpu as pltpu
from jax.sharding import PartitionSpec as P

CAP = 32
PITERS = 5
SITERS = 8

NU = 0.15
MU = 0.5
WALL = 4.0

P_SHIFT, P_BACK = (4.93, 7.29, 5.13, 7.05, 5.38), (10.17, 6.01, 8.86, 8.24)
S_SHIFT = (5.7, 5.09, 4.26, 4.26, 4.08, 4.17, 4.1, 4.18)
S_BACK = (2.53, 3.17, 4.07, 3.95, 4.22, 4.01, 4.14)
TINY = 1e-7

VMEM = pl.BlockSpec(memory_space=pltpu.VMEM)
F32 = jnp.float32
BF16 = jnp.bfloat16

H2_AT, ROW_AT, DISP_AT, HALO_ROWS = 128, 256, 264, 288
SHELL_AT, FIELD_ROWS = 512, 704


def call(kernel, outs, args, scratch=(), flops=1000000, limit=48):
    return pl.pallas_call(
        kernel,
        out_shape=outs,
        in_specs=[VMEM] * len(args),
        out_specs=jax.tree.map(lambda _: VMEM, outs),
        scratch_shapes=list(scratch),
        compiler_params=pltpu.CompilerParams(vmem_limit_bytes=limit * 1024 * 1024),
        cost_estimate=pl.CostEstimate(flops=flops, bytes_accessed=1000000, transcendentals=0),
    )(*args)


def shape(*dims, dtype=F32):
    return jax.ShapeDtypeStruct(dims, dtype)


def at(values, axis):
    return lax.broadcasted_iota(jnp.int32, values.shape, axis)


def ahead(values, axis):
    size = values.shape[axis]
    return jnp.where(at(values, axis) == size - 1, 0.0, pltpu.roll(values, size - 1, axis))


def behind(values, axis):
    return jnp.where(at(values, axis) == 0, 0.0, pltpu.roll(values, 1, axis))


def plane_sum(plane):
    return ahead(plane, 0) + behind(plane, 0) + ahead(plane, 1) + behind(plane, 1)


def difference(plane, axis):
    return ahead(plane, axis) - behind(plane, axis)


def halves(ref, start):
    return jnp.concatenate([ref[start : start + 64, :], ref[start + 64 : start + 128, :]], axis=1)


def put_halves(ref, start, plane):
    ref[start : start + 64, :] = plane[:, :128]
    ref[start + 64 : start + 128, :] = plane[:, 128:]


def parts(values, count):
    pieces = []
    for _ in range(count - 1):
        piece = values.astype(BF16)
        pieces.append(piece)
        values = values - piece.astype(F32)
    pieces.append(values.astype(BF16))
    return pieces


def dot(left, right, transposed=False):
    dims = (((1,), (1 if transposed else 0,)), ((), ()))
    return lax.dot_general(left, right, dims, preferred_element_type=F32)


def split_dot(left, right, count, transposed=False):
    rows = left.shape[0]
    product = dot(jnp.concatenate(parts(left, count), 0), right, transposed)
    return sum(product[i * rows : (i + 1) * rows] for i in range(count))


def fluid_kernel(velocity, displacement, to_left, to_right, source, wall):
    layers = velocity.shape[1]
    last = layers - 1
    field = [[velocity[c, x] for x in range(layers)] for c in range(3)]
    own = [[(1.0 - 6.0 * NU) * f + NU * plane_sum(f) for f in rows] for rows in field]
    spread = {
        x: NU * (difference(field[1][x], 0) + difference(field[2][x], 1)) for x in (0, last)
    }
    put_halves(to_left, 0, own[0][0] + NU * field[0][1] + spread[0])
    put_halves(to_left, H2_AT, NU * field[0][0])
    put_halves(to_right, 0, spread[last] - own[0][last] - NU * field[0][last - 1])
    put_halves(to_right, H2_AT, NU * field[0][last])
    for ref, x, row in ((to_left, 0, 0), (to_right, last, 7)):
        edge = (MU * NU) * (velocity[2, x, 1:2, :] - velocity[2, x, 0:1, :])
        ref[ROW_AT : DISP_AT, :] = jnp.zeros((8, 128), F32)
        ref[ROW_AT : ROW_AT + 1, :] = edge[:, :128]
        ref[ROW_AT + 1 : ROW_AT + 2, :] = edge[:, 128:]
        ref[ROW_AT + 2 : ROW_AT + 3, :] = jnp.ones((1, 128), F32)
        for c in range(3):
            for k in range(8):
                place = DISP_AT + c * 8 + k
                ref[place : place + 1, :] = displacement[c, row : row + 1, k * 128 : k * 128 + 128]
    zero = jnp.zeros_like(field[0][0])
    predicted = [
        [
            own[c][x]
            + NU
            * (
                (field[c][x + 1] if x < last else zero)
                + (field[c][x - 1] if x > 0 else zero)
            )
            for x in range(layers)
        ]
        for c in range(3)
    ]
    for x in range(layers):
        after = predicted[0][x + 1] if x < last else zero
        before = predicted[0][x - 1] if x > 0 else zero
        source[x] = -0.5 * (
            after - before + difference(predicted[1][x], 0) + difference(predicted[2][x], 1)
        )
        wall[x : x + 1, :] = MU * (predicted[0][x][1:2, :] - predicted[0][x][0:1, :])
        wall[4 + x : 5 + x, :] = MU * (predicted[2][x][1:2, :] - predicted[2][x][0:1, :])


def shell_beside(field):
    return ahead(field, 0) + behind(field, 0) + ahead(field, 1) + behind(field, 1)


def source_kernel(
    source, wall, to_left, to_right, from_left, from_right, displacement, load, stiffness, fields, first, wall_out
):
    layers = source.shape[0]
    last = layers - 1
    left1, left2 = halves(from_left, 0), halves(from_left, H2_AT)
    right1, right2 = halves(from_right, 0), halves(from_right, H2_AT)
    has_left = from_left[ROW_AT + 2 : ROW_AT + 3, 0:1]
    has_right = from_right[ROW_AT + 2 : ROW_AT + 3, 0:1]
    left1 = left1 - has_left * halves(to_left, H2_AT)
    right1 = right1 + has_right * halves(to_right, H2_AT)
    for x in range(layers):
        plane = source[x]
        if x == 0:
            plane = plane - 0.5 * left1
        if x == 1:
            plane = plane + 0.5 * left2
        if x == last - 1:
            plane = plane - 0.5 * right2
        if x == last:
            plane = plane - 0.5 * right1
        put_halves(fields, x * 128, plane)
        if x == 0:
            put_halves(first, 0, plane)
    wall_out[...] = wall[...]
    for x, ref, plane in ((0, from_left, left2), (last, from_right, right2)):
        edge = jnp.concatenate([ref[ROW_AT : ROW_AT + 1, :], ref[ROW_AT + 1 : ROW_AT + 2, :]], 1)
        wall_out[x : x + 1, :] = wall[x : x + 1, :] + MU * (plane[1:2, :] - plane[0:1, :])
        wall_out[4 + x : 5 + x, :] = wall[4 + x : 5 + x, :] + edge
    for c in range(3):
        field = displacement[c]
        above = jnp.concatenate(
            [from_left[DISP_AT + c * 8 + k : DISP_AT + c * 8 + k + 1, :] for k in range(8)], 1
        )
        below = jnp.concatenate(
            [from_right[DISP_AT + c * 8 + k : DISP_AT + c * 8 + k + 1, :] for k in range(8)], 1
        )
        row = at(field, 0)
        beside = jnp.where(row == 0, above, pltpu.roll(field, 1, 0))
        beside = beside + jnp.where(row == 7, below, pltpu.roll(field, 7, 0))
        beside = beside + ahead(field, 1) + behind(field, 1)
        start = load[c] - ((4.0 + stiffness[...]) * field - beside)
        for k in range(8):
            place = SHELL_AT + (c * 8 + k) * 8
            fields[place : place + 8, :] = start[:, k * 128 : k * 128 + 128]


def slots_kernel(owner, slots, *, ranks):
    width = owner.shape[1]
    down = lax.broadcasted_iota(jnp.int32, (width, width), 0)
    across = lax.broadcasted_iota(jnp.int32, (width, width), 1)
    earlier = jnp.where(down < across, 1.0, 0.0).astype(BF16)
    rank = lax.broadcasted_iota(jnp.int32, (ranks, width), 0)
    seen = jnp.zeros((ranks, 1), F32)
    for x in range(owner.shape[0]):
        member = jnp.where(rank == owner[x : x + 1, :], 1.0, 0.0)
        before = dot(member.astype(BF16), earlier) + seen
        slots[x : x + 1, :] = jnp.sum(before * member, 0, keepdims=True).astype(jnp.int32)
        seen = seen + jnp.sum(member, 1, keepdims=True)


def fold(product):
    rows, columns = product.shape
    tall = product[0:8]
    for a in range(1, rows // 8):
        tall = tall + product[a * 8 : a * 8 + 8]
    total = tall[:, :128]
    for b in range(1, columns // 128):
        total = total + tall[:, b * 128 : b * 128 + 128]
    return total


def whole(tile):
    return jnp.sum(jnp.sum(tile, 0, keepdims=True), 1, keepdims=True)


def place_pair(tile, i, j, value):
    row, lane = at(tile, 0), at(tile, 1)
    here = (row == i) & (lane == j[0])
    if j[1] is not None:
        here = here | ((row == j[1]) & (lane == j[2]))
    return jnp.where(here, value, tile)


def pressure_kernel(
    own, left, right, beyond, shift, shift_left, shift_right,
    wall, owner, slots, node, weight,
    payload, basis, work, diagonal, off, *, ranks,
):
    layers = shift.shape[0]
    for x in range(layers):
        work[0, x] = halves(left, x * 128)
        work[0, x + 4] = halves(own, x * 128)
        work[0, x + 8] = halves(right, x * 128)
    work[0, 12] = halves(beyond, 0)
    for x in range(1, 12):
        ref = (shift_left, shift, shift_right)[x // 4]
        values = ref[x % 4]
        inside = values > 0.0
        diagonal[x] = jnp.where(inside, values + 6.0, 0.0)
        off[x] = jnp.where(inside, 1.0, 0.0)
    for step in range(1, PITERS):
        for x in range(step, 13 - step):
            now = work[step - 1, x]
            beside = work[step - 1, x - 1] + work[step - 1, x + 1] + plane_sum(now)
            if x < 4 or x >= 8:
                beside = off[x] * beside
            value = (diagonal[x] - P_SHIFT[step - 1]) * now - beside
            if step > 1:
                value = value - P_BACK[step - 2] * work[step - 2, x]
            work[step, x] = value
    tile = jnp.zeros((8, 128), F32)
    for i in range(PITERS):
        for j in range(i, PITERS):
            total = sum(work[i, x] * work[j, x] for x in range(4, 8))
            value = whole(fold(total))
            tile = place_pair(tile, 3 + i, (96 + j, 3 + j, 96 + i), value)
    top = PITERS - 1
    total = 0.0
    for x in range(4, 8):
        now = work[top, x]
        image = (6.0 + shift[x - 4]) * now - plane_sum(now) - 2.0 * work[top, x + 1]
        total = total + now * image
    tile = place_pair(tile, 3 + top, (96 + PITERS, None, None), whole(fold(total)))
    for k in range(PITERS):
        for x in range(layers):
            basis[k, x] = work[k, x + 4]
    lanes = lax.broadcasted_iota(jnp.int32, (128, 256), 0)
    field_row = lax.broadcasted_iota(jnp.int32, (8, 256), 0)
    packed = jnp.zeros((ranks * 8, 128), F32)
    weights = jnp.zeros((ranks * 8, 128), F32)
    for x in range(layers):
        scale = weight[x : x + 1, :].astype(F32)
        rows = [wall[x : x + 1, :] * scale, wall[4 + x : 5 + x, :] * scale]
        rows.append(node[x : x + 1, :].astype(F32))
        rows += [work[k, x + 4][0:1, :] * scale for k in range(PITERS)]
        values = jnp.concatenate(rows, 0)
        who = owner[x : x + 1, :]
        here = jnp.where((lanes & 31) == slots[x : x + 1, :], 1.0, 0.0)
        place = jnp.where(lanes < 96, here, 0.0).astype(BF16)
        end = jnp.where(lanes >= 96, here, 0.0).astype(BF16)
        left_rows = jnp.concatenate([jnp.where(who == d, values, 0.0) for d in range(ranks)], 0)
        packed = packed + split_dot(left_rows, place, 3, True)
        weight_rows = jnp.concatenate(
            [
                jnp.where((who == d - 1 + field_row) & (field_row < 3), scale, 0.0)
                for d in range(ranks)
            ],
            0,
        )
        weights = weights + dot(weight_rows.astype(BF16), end, True)
    lane = lax.broadcasted_iota(jnp.int32, (8, 128), 1)
    zero = jnp.zeros((8, 128), F32)
    for d in range(ranks):
        mine = packed[d * 8 : d * 8 + 8]
        before = packed[d * 8 - 8 : d * 8] if d > 0 else zero
        after = packed[d * 8 + 8 : d * 8 + 16] if d < ranks - 1 else zero
        block = jnp.where(lane < 32, before, jnp.where(lane < 64, mine, after))
        block = jnp.where(lane < 96, block, 0.0) + weights[d * 8 : d * 8 + 8]
        payload[d] = block + tile


def row_of(matrix, k):
    return jnp.sum(jnp.where(at(matrix, 0) == k, matrix, 0.0), 0, keepdims=True)


def column_of(matrix, k):
    return jnp.sum(jnp.where(at(matrix, 1) == k, matrix, 0.0), 1, keepdims=True)


def as_column(row, matrix, shift):
    spread = jnp.broadcast_to(row, matrix.shape)
    return jnp.sum(jnp.where(at(matrix, 1) == at(matrix, 0) - shift, spread, 0.0), 1, keepdims=True)


def eliminate(matrix, first_row, first_lane, count):
    row_at = at(matrix, 0)
    start = matrix
    for k in range(count):
        row = row_of(matrix, first_row + k)
        column = column_of(matrix, first_lane + k)
        pivot = column_of(row, first_lane + k)
        scale = column_of(row_of(start, first_row + k), first_lane + k)
        good = pivot > TINY * scale
        inverse = jnp.where(good, 1.0 / jnp.where(good, pivot, 1.0), 0.0)
        row = row * inverse
        matrix = jnp.where(row_at == first_row + k, row, matrix - column * row)
    return matrix


def galerkin(gram, first_row, shifts, back, energy):
    count = len(shifts)
    lane, row = at(gram, 1), at(gram, 0)
    shift, prior = 0.0, 0.0
    for k in range(count):
        shift = jnp.where(lane == k, shifts[k], shift)
    for k in range(1, count):
        prior = jnp.where(lane == k, back[k - 1], prior)
    image = shift * gram + pltpu.roll(gram, 127, 1) + prior * pltpu.roll(gram, 1, 1)
    last = as_column(row_of(image, first_row + count - 1), gram, first_row)
    last = jnp.where(row == first_row + count - 1, energy, last)
    image = jnp.where(lane == count - 1, last, image)
    image = jnp.where(lane == count, column_of(gram, 0), image)
    inside = (row >= first_row) & (row < first_row + count) & (lane <= count)
    return jnp.where(inside, image, 0.0)


def shell_kernel(
    received, own, left, right, stiffness, stiffness_left, stiffness_right,
    displacement, residual_prev, solved_prev, residual_history, solved_history,
    payload, basis, factors, work, diagonal, off, table, *, ranks,
):
    lane8 = lax.broadcasted_iota(jnp.int32, (8, 128), 1)
    summed = received[0]
    for p in range(1, ranks):
        summed = summed + received[p]
    gram = pltpu.roll(jnp.where(lane8 >= 96, summed, 0.0), 32, 1)
    energy = jnp.sum(
        jnp.where((at(gram, 0) == 3 + PITERS - 1) & (lane8 == PITERS), gram, 0.0), keepdims=True
    )
    system = galerkin(gram, 3, P_SHIFT, P_BACK, energy)
    solved = column_of(eliminate(system, 3, 0, PITERS), PITERS)
    solved = jnp.where(lax.broadcasted_iota(jnp.int32, (8, 1), 0) >= 3, solved, 0.0)
    factors[...] = jnp.broadcast_to(solved, (8, 128))
    groups = [lane8 // 32 == q for q in range(4)]

    def gathered(j):
        chunks = []
        for k in range(ranks // 4):
            chunk = jnp.zeros((8, 128), F32)
            for q in range(4):
                chunk = jnp.where(
                    groups[q], pltpu.roll(received[4 * k + q], (32 * (q - j)) % 128, 1), chunk
                )
            chunks.append(chunk)
        return jnp.concatenate(chunks, 1)

    weights = gathered(3)
    entries = ranks * CAP
    target = lax.broadcasted_iota(jnp.int32, (64, entries), 0)
    low = lax.broadcasted_iota(jnp.int32, (128, entries), 0)
    node = None
    for j in range(3):
        values = gathered(j)
        numbers = values[2:3, :].astype(jnp.int32)
        if j == 1:
            node = numbers
        rows = (
            values[0:1, :],
            WALL * jnp.sum(values * solved, 0, keepdims=True),
            values[1:2, :],
        )
        code = ((numbers >> 7) & 7) * 8 + (numbers >> 10)
        spot = jnp.where(low == (numbers & 127), 1.0, 0.0).astype(BF16)
        match = target == code
        scattered = split_dot(
            jnp.concatenate([jnp.where(match, row, 0.0) for row in rows], 0), spot, 3, True
        )
        share = dot(jnp.where(match, weights[j : j + 1, :], 0.0).astype(BF16), spot, True)
        share = 1.0 / jnp.maximum(share, 1.0)
        ref = (left, own, right)[j]
        for c in range(3):
            force = scattered[c * 64 : c * 64 + 64] * share
            for k in range(8):
                place = SHELL_AT + (c * 8 + k) * 8
                work[0, c * 24 + j * 8 : c * 24 + j * 8 + 8, k * 128 : k * 128 + 128] = (
                    force[k * 8 : k * 8 + 8] + ref[place : place + 8, :]
                )
        stiff = (stiffness_left, stiffness, stiffness_right)[j][...]
        inside = stiff > 0.0
        main = jnp.where(inside, stiff + 4.0, 0.0)
        side = jnp.where(inside, 1.0, 0.0)
        for c in range(3):
            diagonal[c * 24 + j * 8 : c * 24 + j * 8 + 8, :] = main
            off[c * 24 + j * 8 : c * 24 + j * 8 + 8, :] = side
    for step in range(1, SITERS):
        now = work[step - 1]
        value = (diagonal[...] - S_SHIFT[step - 1]) * now - off[...] * shell_beside(now)
        if step > 1:
            value = value - S_BACK[step - 2] * work[step - 2]
        work[step] = value
    def basis_tile(k, c):
        return work[k, c * 24 + 8 : c * 24 + 16, :]

    vectors = [lambda c, k=k: basis_tile(k, c) for k in range(SITERS)]
    vectors.append(lambda c: residual_prev[c])
    vectors += [lambda c, k=k: residual_history[k, c] for k in range(residual_history.shape[0])]
    tile = jnp.zeros((16, 128), F32)
    for i in range(len(vectors)):
        for j in range(i, len(vectors)):
            total = sum(vectors[i](c) * vectors[j](c) for c in range(3))
            tile = place_pair(tile, i, (96 + j, j, 96 + i), whole(fold(total)))
    top = SITERS - 1
    total = 0.0
    for c in range(3):
        now = basis_tile(top, c)
        after = work[top, c * 24 + 9 : c * 24 + 17, :]
        image = (4.0 + stiffness[...]) * now - ahead(now, 1) - behind(now, 1) - 2.0 * after
        total = total + now * image
    tile = place_pair(tile, 13, (96 + 13, None, None), whole(fold(total)))
    for k in range(SITERS):
        for c in range(3):
            basis[k, c] = basis_tile(k, c)
    fields = vectors[:SITERS] + [lambda c: displacement[c]]
    fields += [lambda c, k=k: solved_history[k, c] for k in range(solved_history.shape[0])]
    fields.append(lambda c: solved_prev[c])
    for c in range(3):
        for f in range(16):
            value = fields[f](c) if f < len(fields) else jnp.zeros((8, 1024), F32)
            for k in range(8):
                table[k, pl.ds(c * 16 + f, 8, stride=48), :] = value[:, k * 128 : k * 128 + 128]
    column = lax.broadcasted_iota(jnp.int32, (1024, entries), 0)
    pick = jnp.where(column == (node & 1023), 1.0, 0.0).astype(BF16)
    found = split_dot(jnp.concatenate([table[k] for k in range(8)], 1), pick, 3)
    line = node >> 10
    answer = jnp.zeros((48, entries), F32)
    for r in range(8):
        answer = jnp.where(line == r, found[r * 48 : r * 48 + 48], answer)
    lane16 = lax.broadcasted_iota(jnp.int32, (16, 128), 1)
    for p in range(ranks):
        k = p // 4
        block = tile
        for c in range(3):
            piece = answer[c * 16 : c * 16 + 16, k * 128 : k * 128 + 128]
            block = jnp.where(
                lane16 // 32 == c, pltpu.roll(piece, (32 * (c - p % 4)) % 128, 1), block
            )
        payload[p] = block


def combine_kernel(basis, factors, pressure):
    for x in range(pressure.shape[0]):
        total = 0.0
        for k in range(PITERS):
            total = total + factors[3 + k : 4 + k, 0:1] * basis[k, x]
        pressure[x] = total


def update_kernel(
    received, basis, displacement, solved_prev, solved_history, owner, slots,
    new_displacement, wall, *, ranks,
):
    summed = received[0]
    for p in range(1, ranks):
        summed = summed + received[p]
    lane, row = at(summed, 1), at(summed, 0)
    gram = pltpu.roll(jnp.where(lane >= 96, summed, 0.0), 32, 1)
    energy = jnp.sum(jnp.where((row == 13) & (lane == 13), gram, 0.0), keepdims=True)
    system = galerkin(gram, 0, S_SHIFT, S_BACK, energy)
    steps = column_of(eliminate(system, 0, 0, SITERS), SITERS)
    down = lax.broadcasted_iota(jnp.int32, (16, 1), 0)
    steps = jnp.where(down < SITERS, steps, 0.0)
    base, count = SITERS, 1 + solved_history.shape[0]
    with_moved = jnp.sum(gram * steps, 0, keepdims=True)
    with_newest = with_moved - row_of(gram, base)
    steps_row = jnp.sum(jnp.where(row == lane, jnp.broadcast_to(steps, gram.shape), 0.0), 0, keepdims=True)
    newest_moved = jnp.sum(steps_row * with_newest, 1, keepdims=True)
    newest_newest = newest_moved - column_of(with_newest, base)
    block = jnp.where(row == base, with_newest, gram)
    block = jnp.where(lane == base, as_column(with_newest, gram, 0), block)
    block = jnp.where((row == base) & (lane == base), newest_newest, block)
    right = jnp.where(down == base, newest_moved, as_column(with_moved, gram, 0))
    block = jnp.where(lane == base + count, right, block)
    inside = (row >= base) & (row < base + count) & (lane >= base) & (lane <= base + count)
    block = jnp.where(inside, block, 0.0)
    coefficients = -column_of(eliminate(block, base, base, count), base + count)
    newest = row_of(coefficients, base)
    factors = jnp.where(
        down < base,
        (1.0 + newest) * steps,
        jnp.where(
            down == base,
            1.0 + newest,
            jnp.where(down < base + count, coefficients, jnp.where(down == base + count, -newest, 0.0)),
        ),
    )
    for c in range(3):
        total = row_of(factors, base) * displacement[c]
        for k in range(SITERS):
            total = total + row_of(factors, k) * basis[k, c]
        for k in range(count - 1):
            total = total + row_of(factors, base + 1 + k) * solved_history[k, c]
        total = total + row_of(factors, base + count) * solved_prev[c]
        new_displacement[c] = total
    answers = jnp.concatenate(
        [jnp.sum(received[p] * factors, 0, keepdims=True) for p in range(ranks)], 0
    )
    group = at(answers, 1) // 32
    stacked = jnp.concatenate([jnp.where(group == c, answers, 0.0) for c in range(3)], 0)
    slot_row = lax.broadcasted_iota(jnp.int32, (128, 256), 0) & 31
    rank = lax.broadcasted_iota(jnp.int32, (ranks, 256), 0)
    for x in range(owner.shape[0]):
        pick = jnp.where(slot_row == slots[x : x + 1, :], 1.0, 0.0).astype(BF16)
        spread = split_dot(stacked, pick, 3)
        mine = rank == owner[x : x + 1, :]
        for c in range(3):
            wall[c : c + 1, x * 256 : x * 256 + 256] = jnp.sum(
                jnp.where(mine, spread[c * ranks : (c + 1) * ranks], 0.0), 0, keepdims=True
            )


def on_device(
    velocity,
    pressure_shift,
    owner_rank,
    node_index,
    map_weight,
    shell_load,
    shell_stiffness,
    displacement,
    residual_prev,
    solved_prev,
    residual_history,
    solved_history,
):
    ranks = lax.axis_size("slab")
    layers = velocity.shape[1]
    kept = residual_history.shape[0]

    def leftward(values, by=1):
        return lax.ppermute(values, "slab", [(i, i - by) for i in range(by, ranks)])

    def rightward(values):
        return lax.ppermute(values, "slab", [(i, i + 1) for i in range(ranks - 1)])

    owner = owner_rank.reshape(layers, -1)
    node = node_index.reshape(layers, -1)
    weight = map_weight.reshape(layers, -1)

    to_left, to_right, source, wall = call(
        fluid_kernel,
        (shape(HALO_ROWS, 128), shape(HALO_ROWS, 128), shape(*velocity.shape[1:]), shape(8, 256)),
        (velocity, displacement),
    )
    from_right, from_left = leftward(to_left), rightward(to_right)
    shift_right, shift_left = leftward(pressure_shift), rightward(pressure_shift)
    stiffness_right, stiffness_left = leftward(shell_stiffness), rightward(shell_stiffness)
    (slots,) = call(
        lambda *refs: slots_kernel(*refs, ranks=ranks),
        (shape(layers, 256, dtype=jnp.int32),),
        (owner,),
    )
    fields, first, wall = call(
        source_kernel,
        (shape(FIELD_ROWS, 128), shape(128, 128), shape(8, 256)),
        (source, wall, to_left, to_right, from_left, from_right, displacement, shell_load, shell_stiffness),
    )
    fields_right, fields_left = leftward(fields), rightward(fields)
    beyond = leftward(first, 2)
    payload, pressure_basis = call(
        lambda *refs: pressure_kernel(*refs, ranks=ranks),
        (shape(ranks, 8, 128), shape(PITERS, *pressure_shift.shape)),
        (
            fields, fields_left, fields_right, beyond,
            pressure_shift, shift_left, shift_right,
            wall, owner, slots, node, weight,
        ),
        scratch=(
            pltpu.VMEM((PITERS, 13, 64, 256), F32),
            pltpu.VMEM((12, 64, 256), F32),
            pltpu.VMEM((12, 64, 256), F32),
        ),
    )
    received = lax.all_to_all(payload, "slab", split_axis=0, concat_axis=0, tiled=True)
    payload, shell_basis, factors = call(
        lambda *refs: shell_kernel(*refs, ranks=ranks),
        (shape(ranks, 16, 128), shape(SITERS, *displacement.shape), shape(8, 128)),
        (
            received, fields, fields_left, fields_right,
            shell_stiffness, stiffness_left, stiffness_right,
            displacement, residual_prev, solved_prev, residual_history, solved_history,
        ),
        scratch=(
            pltpu.VMEM((SITERS, 72, 1024), F32),
            pltpu.VMEM((72, 1024), F32),
            pltpu.VMEM((72, 1024), F32),
            pltpu.VMEM((8, 8 * 48, 128), F32),
        ),
    )
    answers = lax.all_to_all(payload, "slab", split_axis=0, concat_axis=0, tiled=True)
    (pressure,) = call(combine_kernel, (shape(*pressure_shift.shape),), (pressure_basis, factors))
    new_displacement, wall_displacement = call(
        lambda *refs: update_kernel(*refs, ranks=ranks),
        (shape(*displacement.shape), shape(3, owner_rank.shape[0])),
        (answers, shell_basis, displacement, solved_prev, solved_history, owner, slots),
    )
    return (pressure, new_displacement, wall_displacement)


def solution(mesh):
    in_specs = (
        P(None, ("groups", "slab"), None, None),
        P(("groups", "slab"), None, None),
        P(("groups", "slab"), None),
        P(("groups", "slab")),
        P(("groups", "slab")),
        P(None, ("groups", "slab"), None),
        P(("groups", "slab"), None),
        P(None, ("groups", "slab"), None),
        P(None, ("groups", "slab"), None),
        P(None, ("groups", "slab"), None),
        P(None, None, ("groups", "slab"), None),
        P(None, None, ("groups", "slab"), None),
    )
    out_specs = (
        P(("groups", "slab"), None, None),
        P(None, ("groups", "slab"), None),
        P(None, ("groups", "slab")),
    )
    return jax.shard_map(
        on_device, mesh=mesh, in_specs=in_specs, out_specs=out_specs, check_vma=False
    )
```

```python
import jax
import jax.numpy as jnp
from jax import lax
from jax.experimental import pallas as pl
from jax.experimental.pallas import tpu as pltpu
from jax.sharding import PartitionSpec as P

CAP = 32
PITERS = 5
SITERS = 8

NU = 0.15
MU = 0.5
WALL = 4.0

P_SHIFT, P_BACK = (4.93, 7.29, 5.13, 7.05, 5.38), (10.17, 6.01, 8.86, 8.24)
S_SHIFT = (5.7, 5.09, 4.26, 4.26, 4.08, 4.17, 4.1, 4.18)
S_BACK = (2.53, 3.17, 4.07, 3.95, 4.22, 4.01, 4.14)
TINY = 1e-7

VMEM = pl.BlockSpec(memory_space=pltpu.VMEM)
F32 = jnp.float32
BF16 = jnp.bfloat16

H2_AT, ROW_AT, DISP_AT, HALO_ROWS = 128, 256, 264, 288
FIELD_ROWS, STIFF_AT, SHELL_ROWS = 512, 192, 256


def even_device():
    return lax.rem(lax.axis_index("slab"), 2) == 0


class Late:
    def __init__(self, source, place, semaphore):
        self.place = place
        self.copy = pltpu.make_async_copy(source, place, semaphore)
        self.copy.start()
        self.pending = True

    def __call__(self):
        if self.pending:
            self.copy.wait()
            self.pending = False
        return self.place


class Sides:
    def __init__(self, to_mate, to_other, left, right, semaphores):
        even = even_device()
        self.copies = [
            pltpu.make_async_copy(to_mate, left, semaphores.at[0]),
            pltpu.make_async_copy(to_other, right, semaphores.at[1]),
        ]
        self.places = (left, right)

        @pl.when(even)
        def _():
            pltpu.make_async_copy(to_other, left, semaphores.at[0]).start()
            pltpu.make_async_copy(to_mate, right, semaphores.at[1]).start()

        @pl.when(jnp.logical_not(even))
        def _():
            for copy in self.copies:
                copy.start()

        self.pending = True

    def __call__(self):
        if self.pending:
            for copy in self.copies:
                copy.wait()
            self.pending = False
        return self.places


def call(
    kernel, outs, args, late=(), pairs=(), direct=(), stored=(), scratch=(),
    flops=1000000000, limit=48.0,
):
    count, made = len(args), len(outs)

    def body(*refs):
        operands = list(refs[:count])
        at_end = count + made + len(scratch)
        places = iter(refs[at_end:-1])
        wanted = []
        used = 0
        for i in late:
            operands[i] = Late(operands[i], next(places), refs[-1].at[used])
            wanted.append(operands[i])
            used += 1
        for i in pairs:
            operands[i] = Sides(
                operands[i], operands[i + 1], next(places), next(places), refs[-1].at[pl.ds(used, 2)]
            )
            wanted.append(operands[i])
            used += 2
        operands = [value for i, value in enumerate(operands) if i - 1 not in pairs]
        kernel(*operands, *refs[count:at_end])
        for value in wanted:
            value()

    outside = [i for i in late] + [i + k for i in pairs for k in (0, 1)]
    extra = [pltpu.VMEM(args[i].shape, args[i].dtype) for i in outside]
    extra.append(pltpu.SemaphoreType.DMA((max(1, len(outside)),)))
    args = [
        pltpu.with_memory_space_constraint(value, pltpu.HBM) if i in stored else value
        for i, value in enumerate(args)
    ]
    any_space = pl.BlockSpec(memory_space=pl.ANY)
    return pl.pallas_call(
        body,
        out_shape=outs,
        in_specs=[any_space if i in outside else VMEM for i in range(count)],
        out_specs=tuple(any_space if i in direct else VMEM for i in range(made)),
        scratch_shapes=list(scratch) + extra,
        compiler_params=pltpu.CompilerParams(vmem_limit_bytes=int(limit * 1024 * 1024)),
        cost_estimate=pl.CostEstimate(flops=flops, bytes_accessed=0, transcendentals=0),
    )(*args)


def shape(*dims, dtype=F32):
    return jax.ShapeDtypeStruct(dims, dtype)


def at(values, axis):
    return lax.broadcasted_iota(jnp.int32, values.shape, axis)


def ahead(values, axis):
    size = values.shape[axis]
    return jnp.where(at(values, axis) == size - 1, 0.0, pltpu.roll(values, size - 1, axis))


def behind(values, axis):
    return jnp.where(at(values, axis) == 0, 0.0, pltpu.roll(values, 1, axis))


def plane_sum(plane):
    return ahead(plane, 0) + behind(plane, 0) + ahead(plane, 1) + behind(plane, 1)


def difference(plane, axis):
    return ahead(plane, axis) - behind(plane, axis)


def halves(ref, start):
    return jnp.concatenate([ref[start : start + 64, :], ref[start + 64 : start + 128, :]], axis=1)


def put_halves(ref, start, plane):
    ref[start : start + 64, :] = plane[:, :128]
    ref[start + 64 : start + 128, :] = plane[:, 128:]


def parts(values, count):
    pieces = []
    for _ in range(count - 1):
        piece = values.astype(BF16)
        pieces.append(piece)
        values = values - piece.astype(F32)
    pieces.append(values.astype(BF16))
    return pieces


def dot(left, right, transposed=False):
    dims = (((1,), (1 if transposed else 0,)), ((), ()))
    return lax.dot_general(left, right, dims, preferred_element_type=F32)


def pieces_of(values, count):
    pieces = []
    for _ in range(count):
        pieces.append(values.astype(BF16).astype(F32))
        values = values - pieces[-1]
    return pieces


def added(product, count):
    rows = product.shape[0] // count
    return sum(product[i * rows : (i + 1) * rows] for i in range(count))


def split_dot(left, right, count, transposed=False):
    rows = left.shape[0]
    product = dot(jnp.concatenate(parts(left, count), 0), right, transposed)
    return sum(product[i * rows : (i + 1) * rows] for i in range(count))


def fluid_kernel(
    velocity, displacement, to_mate, to_other, own_left, own_right, source, wall
):
    velocity, displacement = velocity(), displacement()
    even = even_device()
    layers = velocity.shape[1]
    last = layers - 1
    field = [[velocity[c, x] for x in range(layers)] for c in range(3)]
    own = [[(1.0 - 6.0 * NU) * f + NU * plane_sum(f) for f in rows] for rows in field]
    spread = {
        x: NU * (difference(field[1][x], 0) + difference(field[2][x], 1)) for x in (0, last)
    }
    lefts = (own[0][0] + NU * field[0][1] + spread[0], NU * field[0][0])
    rights = (spread[last] - own[0][last] - NU * field[0][last - 1], NU * field[0][last])
    own_left[...] = lefts[1]
    own_right[...] = rights[1]
    edges = [
        (MU * NU) * (velocity[2, x, 1:2, :] - velocity[2, x, 0:1, :]) for x in (0, last)
    ]
    for ref, first, second in ((to_mate, rights, lefts), (to_other, lefts, rights)):
        put_halves(ref, 0, jnp.where(even, first[0], second[0]))
        put_halves(ref, H2_AT, jnp.where(even, first[1], second[1]))
        ref[ROW_AT : DISP_AT, :] = jnp.zeros((8, 128), F32)
        ref[ROW_AT + 2 : ROW_AT + 3, :] = jnp.ones((1, 128), F32)
        edge = jnp.where(even, edges[int(first is rights)], edges[int(second is rights)])
        ref[ROW_AT : ROW_AT + 1, :] = edge[:, :128]
        ref[ROW_AT + 1 : ROW_AT + 2, :] = edge[:, 128:]
        for c in range(3):
            rows = (displacement[c, 0:1, :], displacement[c, 7:8, :])
            row = jnp.where(even, rows[int(first is rights)], rows[int(second is rights)])
            for k in range(8):
                place = DISP_AT + c * 8 + k
                ref[place : place + 1, :] = row[:, k * 128 : k * 128 + 128]
    zero = jnp.zeros_like(field[0][0])
    predicted = [
        [
            own[c][x]
            + NU
            * (
                (field[c][x + 1] if x < last else zero)
                + (field[c][x - 1] if x > 0 else zero)
            )
            for x in range(layers)
        ]
        for c in range(3)
    ]
    for x in range(layers):
        after = predicted[0][x + 1] if x < last else zero
        before = predicted[0][x - 1] if x > 0 else zero
        source[x] = -0.5 * (
            after - before + difference(predicted[1][x], 0) + difference(predicted[2][x], 1)
        )
        wall[x : x + 1, :] = MU * (predicted[0][x][1:2, :] - predicted[0][x][0:1, :])
        wall[4 + x : 5 + x, :] = MU * (predicted[2][x][1:2, :] - predicted[2][x][0:1, :])


def shell_beside(field):
    return ahead(field, 0) + behind(field, 0) + ahead(field, 1) + behind(field, 1)


def source_kernel(
    source, wall, own_left, own_right, halo, displacement, load, stiffness,
    fields, first, shell, wall_out,
):
    from_left, from_right = halo()
    displacement, load, stiffness = displacement(), load(), stiffness()
    layers = source.shape[0]
    last = layers - 1
    left1, left2 = halves(from_left, 0), halves(from_left, H2_AT)
    right1, right2 = halves(from_right, 0), halves(from_right, H2_AT)
    has_left = from_left[ROW_AT + 2 : ROW_AT + 3, 0:1]
    has_right = from_right[ROW_AT + 2 : ROW_AT + 3, 0:1]
    left1 = left1 - has_left * own_left[...]
    right1 = right1 + has_right * own_right[...]
    for x in range(layers):
        plane = source[x]
        if x == 0:
            plane = plane - 0.5 * left1
        if x == 1:
            plane = plane + 0.5 * left2
        if x == last - 1:
            plane = plane - 0.5 * right2
        if x == last:
            plane = plane - 0.5 * right1
        put_halves(fields, x * 128, plane)
        if x == 0:
            put_halves(first, 0, plane)
    wall_out[...] = wall[...]
    for x, ref, plane in ((0, from_left, left2), (last, from_right, right2)):
        edge = jnp.concatenate([ref[ROW_AT : ROW_AT + 1, :], ref[ROW_AT + 1 : ROW_AT + 2, :]], 1)
        wall_out[x : x + 1, :] = wall[x : x + 1, :] + MU * (plane[1:2, :] - plane[0:1, :])
        wall_out[4 + x : 5 + x, :] = wall[4 + x : 5 + x, :] + edge
    for c in range(3):
        field = displacement[c]
        above = jnp.concatenate(
            [from_left[DISP_AT + c * 8 + k : DISP_AT + c * 8 + k + 1, :] for k in range(8)], 1
        )
        below = jnp.concatenate(
            [from_right[DISP_AT + c * 8 + k : DISP_AT + c * 8 + k + 1, :] for k in range(8)], 1
        )
        row = at(field, 0)
        beside = jnp.where(row == 0, above, pltpu.roll(field, 1, 0))
        beside = beside + jnp.where(row == 7, below, pltpu.roll(field, 7, 0))
        beside = beside + ahead(field, 1) + behind(field, 1)
        start = load[c] - ((4.0 + stiffness[...]) * field - beside)
        for k in range(8):
            place = (c * 8 + k) * 8
            shell[place : place + 8, :] = start[:, k * 128 : k * 128 + 128]
    for k in range(8):
        place = STIFF_AT + k * 8
        shell[place : place + 8, :] = stiffness[:, k * 128 : k * 128 + 128]


def slots_kernel(owner, slots, *, ranks):
    width = owner.shape[1]
    down = lax.broadcasted_iota(jnp.int32, (width, width), 0)
    across = lax.broadcasted_iota(jnp.int32, (width, width), 1)
    earlier = jnp.where(down < across, 1.0, 0.0).astype(BF16)
    rank = lax.broadcasted_iota(jnp.int32, (ranks, width), 0)
    seen = jnp.zeros((ranks, 1), F32)
    for x in range(owner.shape[0]):
        member = jnp.where(rank == owner[x : x + 1, :], 1.0, 0.0)
        before = dot(member.astype(BF16), earlier) + seen
        slots[x : x + 1, :] = jnp.sum(before * member, 0, keepdims=True).astype(jnp.int32)
        seen = seen + jnp.sum(member, 1, keepdims=True)


def fold(product):
    rows, columns = product.shape
    tall = product[0:8]
    for a in range(1, rows // 8):
        tall = tall + product[a * 8 : a * 8 + 8]
    total = tall[:, :128]
    for b in range(1, columns // 128):
        total = total + tall[:, b * 128 : b * 128 + 128]
    return total


def whole(tile):
    return jnp.sum(jnp.sum(tile, 0, keepdims=True), 1, keepdims=True)


def place_pair(tile, i, j, value):
    row, lane = at(tile, 0), at(tile, 1)
    here = (row == i) & (lane == j[0])
    if j[1] is not None:
        here = here | ((row == j[1]) & (lane == j[2]))
    return jnp.where(here, value, tile)


def pressure_kernel(
    own, halo, beyond, shift, shift_halo,
    wall, owner, slots, node, weight,
    payload, basis, work, diagonal, off, sent, *, ranks,
):
    left, right = halo()
    beyond, shift = beyond(), shift()
    shift_left, shift_right = shift_halo()
    layers = shift.shape[0]
    for x in range(layers):
        work[0, x] = halves(left, x * 128)
        work[0, x + 4] = halves(own, x * 128)
        work[0, x + 8] = halves(right, x * 128)
    work[0, 12] = halves(beyond, 0)
    for x in range(1, 12):
        values = (shift_left, shift, shift_right)[x // 4][x % 4]
        inside = values > 0.0
        diagonal[x] = jnp.where(inside, values + 6.0, 0.0)
        off[x] = jnp.where(inside, 1.0, 0.0)
    for step in range(1, PITERS):
        for x in range(step, 13 - step):
            now = work[step - 1, x]
            beside = work[step - 1, x - 1] + work[step - 1, x + 1] + plane_sum(now)
            if x < 4 or x >= 8:
                beside = off[x] * beside
            value = (diagonal[x] - P_SHIFT[step - 1]) * now - beside
            if step > 1:
                value = value - P_BACK[step - 2] * work[step - 2, x]
            work[step, x] = value
    copies = [
        pltpu.make_async_copy(work.at[k, pl.ds(4, layers)], basis.at[k], sent.at[k])
        for k in range(PITERS)
    ]
    for copy in copies:
        copy.start()
    tile = jnp.zeros((8, 128), F32)
    for i in range(PITERS):
        for j in range(i, PITERS):
            total = sum(work[i, x] * work[j, x] for x in range(4, 8))
            value = whole(fold(total))
            tile = place_pair(tile, 3 + i, (96 + j, 3 + j, 96 + i), value)
    top = PITERS - 1
    total = 0.0
    for x in range(4, 8):
        now = work[top, x]
        image = (6.0 + shift[x - 4]) * now - plane_sum(now) - 2.0 * work[top, x + 1]
        total = total + now * image
    tile = place_pair(tile, 3 + top, (96 + PITERS, None, None), whole(fold(total)))
    lanes = lax.broadcasted_iota(jnp.int32, (128, 256), 0)
    field_row = lax.broadcasted_iota(jnp.int32, (8, 256), 0)
    packed = jnp.zeros((ranks * 8, 128), F32)
    weights = jnp.zeros((ranks * 8, 128), F32)
    for x in range(layers):
        scale = weight[x : x + 1, :].astype(F32)
        rows = [wall[x : x + 1, :] * scale, wall[4 + x : 5 + x, :] * scale]
        rows.append(node[x : x + 1, :].astype(F32))
        rows += [work[k, x + 4][0:1, :] * scale for k in range(PITERS)]
        values = jnp.concatenate(rows, 0)
        who = owner[x : x + 1, :]
        here = jnp.where((lanes & 31) == slots[x : x + 1, :], 1.0, 0.0)
        place = jnp.where(lanes < 96, here, 0.0).astype(BF16)
        end = jnp.where(lanes >= 96, here, 0.0).astype(BF16)
        left_rows = jnp.concatenate(
            [jnp.where(who == d, piece, 0.0) for piece in pieces_of(values, 3) for d in range(ranks)], 0
        )
        packed = packed + added(dot(left_rows.astype(BF16), place, True), 3)
        weight_rows = jnp.concatenate(
            [
                jnp.where((who == d - 1 + field_row) & (field_row < 3), scale, 0.0)
                for d in range(ranks)
            ],
            0,
        )
        weights = weights + dot(weight_rows.astype(BF16), end, True)
    lane = lax.broadcasted_iota(jnp.int32, (8, 128), 1)
    zero = jnp.zeros((8, 128), F32)
    for d in range(ranks):
        mine = packed[d * 8 : d * 8 + 8]
        before = packed[d * 8 - 8 : d * 8] if d > 0 else zero
        after = packed[d * 8 + 8 : d * 8 + 16] if d < ranks - 1 else zero
        block = jnp.where(lane < 32, before, jnp.where(lane < 64, mine, after))
        block = jnp.where(lane < 96, block, 0.0) + weights[d * 8 : d * 8 + 8]
        payload[d] = block + tile
    for copy in copies:
        copy.wait()


def row_of(matrix, k):
    return jnp.sum(jnp.where(at(matrix, 0) == k, matrix, 0.0), 0, keepdims=True)


def column_of(matrix, k):
    return jnp.sum(jnp.where(at(matrix, 1) == k, matrix, 0.0), 1, keepdims=True)


def eliminate(columns, right, first):
    row = at(right, 0)
    lengths = [TINY * column[first + k : first + k + 1] for k, column in enumerate(columns)]
    for k in range(len(columns)):
        column = columns[k]
        here = first + k
        pivot = column[here : here + 1]
        good = pivot > lengths[k]
        inverse = jnp.where(good, 1.0 / jnp.where(good, pivot, 1.0), 0.0)
        factor = column * inverse

        def reduced(values):
            mine = values[here : here + 1]
            return jnp.where(row == here, mine * inverse, values - factor * mine)

        columns = columns[: k + 1] + [reduced(values) for values in columns[k + 1 :]]
        right = reduced(right)
    return right


def galerkin(gram, first, shifts, back, energy):
    count = len(shifts)
    images = []
    for k in range(count - 1):
        image = shifts[k] * gram[k] + gram[k + 1]
        if k > 0:
            image = image + back[k - 1] * gram[k - 1]
        images.append(image)
    last = jnp.broadcast_to(gram[count - 1], (gram[0].shape[0], 128))
    row = at(last, 0)
    shift, prior = 0.0, 0.0
    for k in range(count):
        shift = jnp.where(row == first + k, shifts[k], shift)
    for k in range(1, count):
        prior = jnp.where(row == first + k, back[k - 1], prior)
    size = last.shape[0]
    image = shift * last + pltpu.roll(last, size - 1, 0) + prior * pltpu.roll(last, 1, 0)
    image = jnp.where(row == first + count - 1, energy, image)
    images.append(image[:, 0:1])
    return images


def shell_kernel(
    received, own, halo,
    displacement, residual_prev, solved_prev, residual_history, solved_history,
    payload, basis, factors, work, diagonal, off, table, sent, *, ranks,
):
    received = received()
    lane8 = lax.broadcasted_iota(jnp.int32, (8, 128), 1)
    summed = received[0]
    for p in range(1, ranks):
        summed = summed + received[p]
    gram = [column_of(summed, 96 + k) for k in range(PITERS + 1)]
    system = galerkin(gram[:PITERS], 3, P_SHIFT, P_BACK, gram[PITERS][7:8])
    solved = eliminate(system, gram[0], 3)
    solved = jnp.where(lax.broadcasted_iota(jnp.int32, (8, 1), 0) >= 3, solved, 0.0)
    factors[...] = jnp.broadcast_to(solved, (8, 128))
    groups = [lane8 // 32 == q for q in range(4)]

    def gathered(j):
        chunks = []
        for k in range(ranks // 4):
            chunk = jnp.zeros((8, 128), F32)
            for q in range(4):
                chunk = jnp.where(
                    groups[q], pltpu.roll(received[4 * k + q], (32 * (q - j)) % 128, 1), chunk
                )
            chunks.append(chunk)
        return jnp.concatenate(chunks, 1)

    left, right = halo()
    weights = gathered(3)
    entries = ranks * CAP
    target = lax.broadcasted_iota(jnp.int32, (64, entries), 0)
    low = lax.broadcasted_iota(jnp.int32, (128, entries), 0)
    node = None
    for j in range(3):
        values = gathered(j)
        numbers = values[2:3, :].astype(jnp.int32)
        if j == 1:
            node = numbers
        rows = (
            values[0:1, :],
            WALL * jnp.sum(values * solved, 0, keepdims=True),
            values[1:2, :],
        )
        code = ((numbers >> 7) & 7) * 8 + (numbers >> 10)
        spot = jnp.where(low == (numbers & 127), 1.0, 0.0).astype(BF16)
        match = target == code
        pieces = pieces_of(jnp.concatenate(rows, 0), 3)
        left_rows = jnp.concatenate(
            [jnp.where(match, piece[c : c + 1], 0.0) for piece in pieces for c in range(3)], 0
        )
        scattered = added(dot(left_rows.astype(BF16), spot, True), 3)
        share = dot(jnp.where(match, weights[j : j + 1, :], 0.0).astype(BF16), spot, True)
        share = 1.0 / jnp.maximum(share, 1.0)
        ref = (left, own, right)[j]
        for c in range(3):
            force = scattered[c * 64 : c * 64 + 64] * share
            for k in range(8):
                place = (c * 8 + k) * 8
                work[0, c * 24 + j * 8 : c * 24 + j * 8 + 8, k * 128 : k * 128 + 128] = (
                    force[k * 8 : k * 8 + 8] + ref[place : place + 8, :]
                )
        stiff = jnp.concatenate(
            [ref[STIFF_AT + k * 8 : STIFF_AT + k * 8 + 8, :] for k in range(8)], 1
        )
        if j == 1:
            stiffness = stiff
        inside = stiff > 0.0
        main = jnp.where(inside, stiff + 4.0, 0.0)
        side = jnp.where(inside, 1.0, 0.0)
        for c in range(3):
            diagonal[c * 24 + j * 8 : c * 24 + j * 8 + 8, :] = main
            off[c * 24 + j * 8 : c * 24 + j * 8 + 8, :] = side
    for step in range(1, SITERS):
        now = work[step - 1]
        value = (diagonal[...] - S_SHIFT[step - 1]) * now - off[...] * shell_beside(now)
        if step > 1:
            value = value - S_BACK[step - 2] * work[step - 2]
        work[step] = value
    copies = [
        pltpu.make_async_copy(work.at[k, pl.ds(c * 24 + 8, 8)], basis.at[k, c], sent.at[k, c])
        for k in range(SITERS)
        for c in range(3)
    ]
    for copy in copies:
        copy.start()
    displacement, residual_prev, solved_prev = displacement(), residual_prev(), solved_prev()
    residual_history, solved_history = residual_history(), solved_history()
    def basis_tile(k, c):
        return work[k, c * 24 + 8 : c * 24 + 16, :]

    vectors = [lambda c, k=k: basis_tile(k, c) for k in range(SITERS)]
    vectors.append(lambda c: residual_prev[c])
    vectors += [lambda c, k=k: residual_history[k, c] for k in range(residual_history.shape[0])]
    tile = jnp.zeros((16, 128), F32)
    for i in range(len(vectors)):
        for j in range(i, len(vectors)):
            total = sum(vectors[i](c) * vectors[j](c) for c in range(3))
            tile = place_pair(tile, i, (96 + j, j, 96 + i), whole(fold(total)))
    top = SITERS - 1
    total = 0.0
    for c in range(3):
        now = basis_tile(top, c)
        after = work[top, c * 24 + 9 : c * 24 + 17, :]
        image = (4.0 + stiffness) * now - ahead(now, 1) - behind(now, 1) - 2.0 * after
        total = total + now * image
    tile = place_pair(tile, 13, (96 + 13, None, None), whole(fold(total)))
    fields = vectors[:SITERS] + [lambda c: displacement[c]]
    fields += [lambda c, k=k: solved_history[k, c] for k in range(solved_history.shape[0])]
    fields.append(lambda c: solved_prev[c])
    for c in range(3):
        for f in range(16):
            value = fields[f](c) if f < len(fields) else jnp.zeros((8, 1024), F32)
            for k in range(8):
                table[k, pl.ds(c * 16 + f, 8, stride=48), :] = value[:, k * 128 : k * 128 + 128]
    column = lax.broadcasted_iota(jnp.int32, (1024, entries), 0)
    pick = jnp.where(column == (node & 1023), 1.0, 0.0).astype(BF16)
    found = split_dot(jnp.concatenate([table[k] for k in range(8)], 1), pick, 2)
    line = node >> 10
    answer = jnp.zeros((48, entries), F32)
    for r in range(8):
        answer = jnp.where(line == r, found[r * 48 : r * 48 + 48], answer)
    lane16 = lax.broadcasted_iota(jnp.int32, (16, 128), 1)
    for p in range(ranks):
        k = p // 4
        block = tile
        for c in range(3):
            piece = answer[c * 16 : c * 16 + 16, k * 128 : k * 128 + 128]
            block = jnp.where(
                lane16 // 32 == c, pltpu.roll(piece, (32 * (c - p % 4)) % 128, 1), block
            )
        payload[p] = block
    for copy in copies:
        copy.wait()


def combine_kernel(basis, factors, pressure):
    basis = basis()
    for x in range(pressure.shape[0]):
        total = 0.0
        for k in range(PITERS):
            total = total + factors[3 + k : 4 + k, 0:1] * basis[k, x]
        pressure[x] = total


def update_kernel(
    received, basis, displacement, solved_prev, solved_history, owner, slots,
    new_displacement, wall, *, ranks,
):
    received = received()
    summed = received[0]
    for p in range(1, ranks):
        summed = summed + received[p]
    gram = [column_of(summed, 96 + k) for k in range(14)]
    system = galerkin(gram[:SITERS], 0, S_SHIFT, S_BACK, gram[13][13:14])
    steps = eliminate(system, gram[0], 0)
    down = lax.broadcasted_iota(jnp.int32, (16, 1), 0)
    steps = jnp.where(down < SITERS, steps, 0.0)
    base, count = SITERS, 1 + solved_history.place.shape[0]
    with_moved = sum(steps[k : k + 1] * gram[k] for k in range(SITERS))
    with_newest = with_moved - gram[base]
    newest_moved = jnp.sum(steps * with_newest, 0, keepdims=True)
    newest_newest = newest_moved - with_newest[base : base + 1]
    columns = [jnp.where(down == base, newest_newest, with_newest)]
    for k in range(1, count):
        columns.append(jnp.where(down == base, with_newest[base + k : base + k + 1], gram[base + k]))
    right = jnp.where(down == base, newest_moved, with_moved)
    coefficients = -eliminate(columns, right, base)
    newest = row_of(coefficients, base)
    factors = jnp.where(
        down < base,
        (1.0 + newest) * steps,
        jnp.where(
            down == base,
            1.0 + newest,
            jnp.where(down < base + count, coefficients, jnp.where(down == base + count, -newest, 0.0)),
        ),
    )
    basis = basis()
    displacement, solved_prev, solved_history = displacement(), solved_prev(), solved_history()
    for c in range(3):
        total = row_of(factors, base) * displacement[c]
        for k in range(SITERS):
            total = total + row_of(factors, k) * basis[k, c]
        for k in range(count - 1):
            total = total + row_of(factors, base + 1 + k) * solved_history[k, c]
        total = total + row_of(factors, base + count) * solved_prev[c]
        new_displacement[c] = total
    answers = jnp.concatenate(
        [jnp.sum(received[p] * factors, 0, keepdims=True) for p in range(ranks)], 0
    )
    group = at(answers, 1) // 32
    stacked = jnp.concatenate([jnp.where(group == c, answers, 0.0) for c in range(3)], 0)
    slot_row = lax.broadcasted_iota(jnp.int32, (128, 256), 0) & 31
    rank = lax.broadcasted_iota(jnp.int32, (ranks, 256), 0)
    for x in range(owner.shape[0]):
        pick = jnp.where(slot_row == slots[x : x + 1, :], 1.0, 0.0).astype(BF16)
        spread = split_dot(stacked, pick, 3)
        mine = rank == owner[x : x + 1, :]
        for c in range(3):
            wall[c : c + 1, x * 256 : x * 256 + 256] = jnp.sum(
                jnp.where(mine, spread[c * ranks : (c + 1) * ranks], 0.0), 0, keepdims=True
            )


def on_device(
    velocity,
    pressure_shift,
    owner_rank,
    node_index,
    map_weight,
    shell_load,
    shell_stiffness,
    displacement,
    residual_prev,
    solved_prev,
    residual_history,
    solved_history,
):
    ranks = lax.axis_size("slab")
    layers = velocity.shape[1]
    kept = residual_history.shape[0]

    def with_mate(values):
        return lax.ppermute(values, "slab", [(i, i ^ 1) for i in range(ranks)])

    def with_other(values):
        pairs = [(i, i + 1) for i in range(1, ranks - 1, 2)]
        return lax.ppermute(values, "slab", pairs + [(j, i) for i, j in pairs])

    owner = owner_rank.reshape(layers, -1)
    node = node_index.reshape(layers, -1)
    weight = map_weight.reshape(layers, -1)
    plane = shape(*velocity.shape[2:])

    to_mate, to_other, own_left, own_right, source, wall = call(
        fluid_kernel,
        (
            shape(HALO_ROWS, 128), shape(HALO_ROWS, 128), plane, plane,
            shape(*velocity.shape[1:]), shape(8, 256),
        ),
        (velocity, displacement),
        late=(0, 1),
        stored=(0, 1),
    )
    halo_other, halo_mate = with_other(to_other), with_mate(to_mate)
    shift_other, shift_mate = with_other(pressure_shift), with_mate(pressure_shift)
    (slots,) = call(
        lambda *refs: slots_kernel(*refs[:2], ranks=ranks),
        (shape(layers, 256, dtype=jnp.int32),),
        (owner,),
    )
    fields, first, shell, wall = call(
        lambda *refs: source_kernel(*refs),
        (shape(FIELD_ROWS, 128), shape(128, 128), shape(SHELL_ROWS, 128), shape(8, 256)),
        (
            source, wall, own_left, own_right, halo_mate, halo_other,
            displacement, shell_load, shell_stiffness,
        ),
        late=(6, 7, 8),
        stored=(6, 7, 8),
        pairs=(4,),
    )
    beyond = lax.ppermute(first, "slab", [(i, i - 2) for i in range(2, ranks)])
    fields_other, fields_mate = with_other(fields), with_mate(fields)
    shell_other, shell_mate = with_other(shell), with_mate(shell)
    payload, pressure_basis = call(
        lambda *refs: pressure_kernel(*refs, ranks=ranks),
        (shape(ranks, 8, 128), pltpu.HBM((PITERS, *pressure_shift.shape), F32)),
        (
            fields, fields_mate, fields_other, beyond, pressure_shift, shift_mate, shift_other,
            wall, owner, slots, node, weight,
        ),
        late=(3, 4),
        stored=(4,),
        pairs=(1, 5),
        direct=(1,),
        scratch=(
            pltpu.VMEM((PITERS, 13, 64, 256), F32),
            pltpu.VMEM((12, 64, 256), F32),
            pltpu.VMEM((12, 64, 256), F32),
            pltpu.SemaphoreType.DMA((PITERS,)),
        ),
    )
    received = lax.all_to_all(payload, "slab", split_axis=0, concat_axis=0, tiled=True)
    payload, shell_basis, factors = call(
        lambda *refs: shell_kernel(*refs, ranks=ranks),
        (shape(ranks, 16, 128), pltpu.HBM((SITERS, *displacement.shape), F32), shape(8, 128)),
        (
            received, shell, shell_mate, shell_other,
            displacement, residual_prev, solved_prev, residual_history, solved_history,
        ),
        late=(0, 4, 5, 6, 7, 8),
        stored=(4, 5, 6, 7, 8),
        pairs=(2,),
        direct=(1,),
        scratch=(
            pltpu.VMEM((SITERS, 72, 1024), F32),
            pltpu.VMEM((72, 1024), F32),
            pltpu.VMEM((72, 1024), F32),
            pltpu.VMEM((8, 8 * 48, 128), F32),
            pltpu.SemaphoreType.DMA((SITERS, 3)),
        ),
    )
    answers = lax.all_to_all(payload, "slab", split_axis=0, concat_axis=0, tiled=True)
    (pressure,) = call(
        combine_kernel,
        (shape(*pressure_shift.shape),),
        (pressure_basis, factors),
        late=(0,),
        stored=(0,),
    )
    new_displacement, wall_displacement = call(
        lambda *refs: update_kernel(*refs, ranks=ranks),
        (shape(*displacement.shape), shape(3, owner_rank.shape[0])),
        (answers, shell_basis, displacement, solved_prev, solved_history, owner, slots),
        late=(0, 1, 2, 3, 4),
        stored=(1, 2, 3, 4),
    )
    return (pressure, new_displacement, wall_displacement)


def solution(mesh):
    in_specs = (
        P(None, ("groups", "slab"), None, None),
        P(("groups", "slab"), None, None),
        P(("groups", "slab"), None),
        P(("groups", "slab")),
        P(("groups", "slab")),
        P(None, ("groups", "slab"), None),
        P(("groups", "slab"), None),
        P(None, ("groups", "slab"), None),
        P(None, ("groups", "slab"), None),
        P(None, ("groups", "slab"), None),
        P(None, None, ("groups", "slab"), None),
        P(None, None, ("groups", "slab"), None),
    )
    out_specs = (
        P(("groups", "slab"), None, None),
        P(None, ("groups", "slab"), None),
        P(None, ("groups", "slab")),
    )
    return jax.shard_map(
        on_device, mesh=mesh, in_specs=in_specs, out_specs=out_specs, check_vma=False
    )
```

```python
import jax
import jax.numpy as jnp
from jax import lax
from jax.experimental import pallas as pl
from jax.experimental.pallas import tpu as pltpu
from jax.sharding import PartitionSpec as P

CAP = 32
PITERS = 5
SITERS = 8

NU = 0.15
MU = 0.5
WALL = 4.0

P_SHIFT, P_BACK = (4.93, 7.29, 5.13, 7.05, 5.38), (10.17, 6.01, 8.86, 8.24)
S_SHIFT = (5.7, 5.09, 4.26, 4.26, 4.08, 4.17, 4.1, 4.18)
S_BACK = (2.53, 3.17, 4.07, 3.95, 4.22, 4.01, 4.14)
TINY = 1e-7

VMEM = pl.BlockSpec(memory_space=pltpu.VMEM)
F32 = jnp.float32
BF16 = jnp.bfloat16

H2_AT, ROW_AT, DISP_AT, HALO_ROWS = 128, 256, 264, 288
FIELD_ROWS, STIFF_AT, SHELL_ROWS = 512, 192, 256


def even_device():
    return lax.rem(lax.axis_index("slab"), 2) == 0


class Late:
    def __init__(self, source, place, semaphore):
        self.place = place
        self.copy = pltpu.make_async_copy(source, place, semaphore)
        self.copy.start()
        self.pending = True

    def __call__(self):
        if self.pending:
            self.copy.wait()
            self.pending = False
        return self.place


class Sides:
    def __init__(self, to_mate, to_other, left, right, semaphores):
        even = even_device()
        self.copies = [
            pltpu.make_async_copy(to_mate, left, semaphores.at[0]),
            pltpu.make_async_copy(to_other, right, semaphores.at[1]),
        ]
        self.places = (left, right)

        @pl.when(even)
        def _():
            pltpu.make_async_copy(to_other, left, semaphores.at[0]).start()
            pltpu.make_async_copy(to_mate, right, semaphores.at[1]).start()

        @pl.when(jnp.logical_not(even))
        def _():
            for copy in self.copies:
                copy.start()

        self.pending = True

    def __call__(self):
        if self.pending:
            for copy in self.copies:
                copy.wait()
            self.pending = False
        return self.places


class Either:
    def __init__(self, which, first, second):
        self.which, self.first, self.second = which, first, second

    def __getitem__(self, index):
        return jnp.where(self.which, self.first[index], self.second[index])


def sides(to_mate, to_other):
    even = even_device()
    return Either(even, to_other, to_mate), Either(even, to_mate, to_other)


def call(
    kernel, outs, args, late=(), outer=(), pairs=(), direct=(), stored=(), scratch=(),
    flops=1000000000, limit=48.0,
):
    count, made = len(args), len(outs)

    def body(*refs):
        operands = list(refs[:count])
        at_end = count + made + len(scratch)
        places = iter(refs[at_end:-1])
        wanted = []
        used = 0
        for i in late:
            operands[i] = Late(operands[i], next(places), refs[-1].at[used])
            wanted.append(operands[i])
            used += 1
        for i in pairs:
            operands[i] = Sides(
                operands[i], operands[i + 1], next(places), next(places), refs[-1].at[pl.ds(used, 2)]
            )
            wanted.append(operands[i])
            used += 2
        operands = [value for i, value in enumerate(operands) if i - 1 not in pairs]
        kernel(*operands, *refs[count:at_end])
        for value in wanted:
            value()

    outside = [i for i in late] + [i + k for i in pairs for k in (0, 1)]
    extra = [pltpu.VMEM(args[i].shape, args[i].dtype) for i in outside]
    extra.append(pltpu.SemaphoreType.DMA((max(1, len(outside)),)))
    args = [
        pltpu.with_memory_space_constraint(value, pltpu.HBM) if i in stored else value
        for i, value in enumerate(args)
    ]
    any_space = pl.BlockSpec(memory_space=pl.ANY)
    return pl.pallas_call(
        body,
        out_shape=outs,
        in_specs=[any_space if i in outside or i in outer else VMEM for i in range(count)],
        out_specs=tuple(any_space if i in direct else VMEM for i in range(made)),
        scratch_shapes=list(scratch) + extra,
        compiler_params=pltpu.CompilerParams(vmem_limit_bytes=int(limit * 1024 * 1024)),
        cost_estimate=pl.CostEstimate(flops=flops, bytes_accessed=0, transcendentals=0),
    )(*args)


def shape(*dims, dtype=F32):
    return jax.ShapeDtypeStruct(dims, dtype)


def at(values, axis):
    return lax.broadcasted_iota(jnp.int32, values.shape, axis)


def ahead(values, axis):
    size = values.shape[axis]
    return jnp.where(at(values, axis) == size - 1, 0.0, pltpu.roll(values, size - 1, axis))


def behind(values, axis):
    return jnp.where(at(values, axis) == 0, 0.0, pltpu.roll(values, 1, axis))


def plane_sum(plane):
    return ahead(plane, 0) + behind(plane, 0) + ahead(plane, 1) + behind(plane, 1)


def difference(plane, axis):
    return ahead(plane, axis) - behind(plane, axis)


def halves(ref, start):
    return jnp.concatenate([ref[start : start + 64, :], ref[start + 64 : start + 128, :]], axis=1)


def put_halves(ref, start, plane):
    ref[start : start + 64, :] = plane[:, :128]
    ref[start + 64 : start + 128, :] = plane[:, 128:]


def parts(values, count):
    pieces = []
    for _ in range(count - 1):
        piece = values.astype(BF16)
        pieces.append(piece)
        values = values - piece.astype(F32)
    pieces.append(values.astype(BF16))
    return pieces


def dot(left, right, transposed=False):
    dims = (((1,), (1 if transposed else 0,)), ((), ()))
    return lax.dot_general(left, right, dims, preferred_element_type=F32)


def pieces_of(values, count):
    pieces = []
    for _ in range(count):
        pieces.append(values.astype(BF16).astype(F32))
        values = values - pieces[-1]
    return pieces


def added(product, count):
    rows = product.shape[0] // count
    return sum(product[i * rows : (i + 1) * rows] for i in range(count))


def split_dot(left, right, count, transposed=False):
    rows = left.shape[0]
    product = dot(jnp.concatenate(parts(left, count), 0), right, transposed)
    return sum(product[i * rows : (i + 1) * rows] for i in range(count))


def fluid_kernel(
    velocity_in, displacement_in, to_mate, to_other, own_left, own_right, source, wall,
    velocity, displacement, arrived,
):
    copies = [pltpu.make_async_copy(velocity_in, velocity, arrived.at[0, 0])]
    copies.append(pltpu.make_async_copy(displacement_in, displacement, arrived.at[3, 0]))
    for copy in copies:
        copy.start()
    for copy in copies:
        copy.wait()
    even = even_device()
    layers = velocity.shape[1]
    last = layers - 1
    field = [[velocity[c, x] for x in range(layers)] for c in range(3)]
    own = [[(1.0 - 6.0 * NU) * f + NU * plane_sum(f) for f in rows] for rows in field]
    spread = {
        x: NU * (difference(field[1][x], 0) + difference(field[2][x], 1)) for x in (0, last)
    }
    lefts = (own[0][0] + NU * field[0][1] + spread[0], NU * field[0][0])
    rights = (spread[last] - own[0][last] - NU * field[0][last - 1], NU * field[0][last])
    own_left[...] = lefts[1]
    own_right[...] = rights[1]
    edges = [
        (MU * NU) * (velocity[2, x, 1:2, :] - velocity[2, x, 0:1, :]) for x in (0, last)
    ]
    for ref, first, second in ((to_mate, rights, lefts), (to_other, lefts, rights)):
        put_halves(ref, 0, jnp.where(even, first[0], second[0]))
        put_halves(ref, H2_AT, jnp.where(even, first[1], second[1]))
        ref[ROW_AT : DISP_AT, :] = jnp.zeros((8, 128), F32)
        ref[ROW_AT + 2 : ROW_AT + 3, :] = jnp.ones((1, 128), F32)
        edge = jnp.where(even, edges[int(first is rights)], edges[int(second is rights)])
        ref[ROW_AT : ROW_AT + 1, :] = edge[:, :128]
        ref[ROW_AT + 1 : ROW_AT + 2, :] = edge[:, 128:]
        for c in range(3):
            rows = (displacement[c, 0:1, :], displacement[c, 7:8, :])
            row = jnp.where(even, rows[int(first is rights)], rows[int(second is rights)])
            for k in range(8):
                place = DISP_AT + c * 8 + k
                ref[place : place + 1, :] = row[:, k * 128 : k * 128 + 128]
    zero = jnp.zeros_like(field[0][0])
    predicted = [
        [
            own[c][x]
            + NU
            * (
                (field[c][x + 1] if x < last else zero)
                + (field[c][x - 1] if x > 0 else zero)
            )
            for x in range(layers)
        ]
        for c in range(3)
    ]
    for x in range(layers):
        after = predicted[0][x + 1] if x < last else zero
        before = predicted[0][x - 1] if x > 0 else zero
        source[x] = -0.5 * (
            after - before + difference(predicted[1][x], 0) + difference(predicted[2][x], 1)
        )
        wall[x : x + 1, :] = MU * (predicted[0][x][1:2, :] - predicted[0][x][0:1, :])
        wall[4 + x : 5 + x, :] = MU * (predicted[2][x][1:2, :] - predicted[2][x][0:1, :])


def shell_beside(field):
    rows = field.shape[0]
    beside = pltpu.roll(field, rows - 1, 0) + pltpu.roll(field, 1, 0)
    return beside + ahead(field, 1) + behind(field, 1)


def source_kernel(
    source, wall, own_left, own_right, halo, displacement, load, stiffness,
    fields, first, shell, wall_out,
):
    from_left, from_right = halo()
    layers = source.shape[0]
    last = layers - 1
    left1, left2 = halves(from_left, 0), halves(from_left, H2_AT)
    right1, right2 = halves(from_right, 0), halves(from_right, H2_AT)
    has_left = from_left[ROW_AT + 2 : ROW_AT + 3, 0:1]
    has_right = from_right[ROW_AT + 2 : ROW_AT + 3, 0:1]
    left1 = left1 - has_left * own_left[...]
    right1 = right1 + has_right * own_right[...]
    for x in range(layers):
        plane = source[x]
        if x == 0:
            plane = plane - 0.5 * left1
        if x == 1:
            plane = plane + 0.5 * left2
        if x == last - 1:
            plane = plane - 0.5 * right2
        if x == last:
            plane = plane - 0.5 * right1
        put_halves(fields, x * 128, plane)
        if x == 0:
            put_halves(first, 0, plane)
    wall_out[...] = wall[...]
    for x, ref, plane in ((0, from_left, left2), (last, from_right, right2)):
        edge = jnp.concatenate([ref[ROW_AT : ROW_AT + 1, :], ref[ROW_AT + 1 : ROW_AT + 2, :]], 1)
        wall_out[x : x + 1, :] = wall[x : x + 1, :] + MU * (plane[1:2, :] - plane[0:1, :])
        wall_out[4 + x : 5 + x, :] = wall[4 + x : 5 + x, :] + edge
    for c in range(3):
        field = displacement[c]
        above = jnp.concatenate(
            [from_left[DISP_AT + c * 8 + k : DISP_AT + c * 8 + k + 1, :] for k in range(8)], 1
        )
        below = jnp.concatenate(
            [from_right[DISP_AT + c * 8 + k : DISP_AT + c * 8 + k + 1, :] for k in range(8)], 1
        )
        row = at(field, 0)
        beside = jnp.where(row == 0, above, pltpu.roll(field, 1, 0))
        beside = beside + jnp.where(row == 7, below, pltpu.roll(field, 7, 0))
        beside = beside + ahead(field, 1) + behind(field, 1)
        start = load[c] - ((4.0 + stiffness[...]) * field - beside)
        for k in range(8):
            place = (c * 8 + k) * 8
            shell[place : place + 8, :] = start[:, k * 128 : k * 128 + 128]
    for k in range(8):
        place = STIFF_AT + k * 8
        shell[place : place + 8, :] = stiffness[:, k * 128 : k * 128 + 128]


def slots_kernel(owner, slots, *, ranks):
    width = owner.shape[1]
    down = lax.broadcasted_iota(jnp.int32, (width, width), 0)
    across = lax.broadcasted_iota(jnp.int32, (width, width), 1)
    earlier = jnp.where(down < across, 1.0, 0.0).astype(BF16)
    rank = lax.broadcasted_iota(jnp.int32, (ranks, width), 0)
    seen = jnp.zeros((ranks, 1), F32)
    for x in range(owner.shape[0]):
        member = jnp.where(rank == owner[x : x + 1, :], 1.0, 0.0)
        before = dot(member.astype(BF16), earlier) + seen
        slots[x : x + 1, :] = jnp.sum(before * member, 0, keepdims=True).astype(jnp.int32)
        seen = seen + jnp.sum(member, 1, keepdims=True)


def fold(product):
    rows, columns = product.shape
    tall = product[0:8]
    for a in range(1, rows // 8):
        tall = tall + product[a * 8 : a * 8 + 8]
    total = tall[:, :128]
    for b in range(1, columns // 128):
        total = total + tall[:, b * 128 : b * 128 + 128]
    return total


def whole(tile):
    return jnp.sum(jnp.sum(tile, 0, keepdims=True), 1, keepdims=True)


def place_pair(tile, i, j, value):
    row, lane = at(tile, 0), at(tile, 1)
    here = (row == i) & (lane == j[0])
    if j[1] is not None:
        here = here | ((row == j[1]) & (lane == j[2]))
    return jnp.where(here, value, tile)


def pressure_kernel(
    own, mate, other, beyond, shift, shift_mate, shift_other,
    wall, owner, slots, node, weight,
    payload, basis, work, diagonal, off, sent, *, ranks,
):
    left, right = sides(mate, other)
    shift_left, shift_right = sides(shift_mate, shift_other)
    layers = shift.shape[0]
    for x in range(layers):
        work[0, x] = halves(left, x * 128)
        work[0, x + 4] = halves(own, x * 128)
        work[0, x + 8] = halves(right, x * 128)
    work[0, 12] = halves(beyond, 0)
    for x in range(1, 12):
        values = (shift_left, shift, shift_right)[x // 4][x % 4]
        inside = values > 0.0
        diagonal[x] = jnp.where(inside, values + 6.0, 0.0)
        off[x] = jnp.where(inside, 1.0, 0.0)
    copies = [
        pltpu.make_async_copy(work.at[k, pl.ds(4, layers)], basis.at[k], sent.at[k])
        for k in range(PITERS)
    ]
    copies[0].start()
    for step in range(1, PITERS):
        for x in range(step, 13 - step):
            now = work[step - 1, x]
            beside = work[step - 1, x - 1] + work[step - 1, x + 1] + plane_sum(now)
            if x < 4 or x >= 8:
                beside = off[x] * beside
            value = (diagonal[x] - P_SHIFT[step - 1]) * now - beside
            if step > 1:
                value = value - P_BACK[step - 2] * work[step - 2, x]
            work[step, x] = value
        copies[step].start()
    tile = jnp.zeros((8, 128), F32)
    for i in range(PITERS):
        for j in range(i, PITERS):
            total = sum(work[i, x] * work[j, x] for x in range(4, 8))
            value = whole(fold(total))
            tile = place_pair(tile, 3 + i, (96 + j, 3 + j, 96 + i), value)
    top = PITERS - 1
    total = 0.0
    for x in range(4, 8):
        now = work[top, x]
        image = (6.0 + shift[x - 4]) * now - plane_sum(now) - 2.0 * work[top, x + 1]
        total = total + now * image
    tile = place_pair(tile, 3 + top, (96 + PITERS, None, None), whole(fold(total)))
    lanes = lax.broadcasted_iota(jnp.int32, (128, 256), 0)
    field_row = lax.broadcasted_iota(jnp.int32, (8, 256), 0)
    packed = jnp.zeros((ranks * 8, 128), F32)
    weights = jnp.zeros((ranks * 8, 128), F32)
    for x in range(layers):
        scale = weight[x : x + 1, :].astype(F32)
        rows = [wall[x : x + 1, :] * scale, wall[4 + x : 5 + x, :] * scale]
        rows.append(node[x : x + 1, :].astype(F32))
        rows += [work[k, x + 4][0:1, :] * scale for k in range(PITERS)]
        values = jnp.concatenate(rows, 0)
        who = owner[x : x + 1, :]
        here = jnp.where((lanes & 31) == slots[x : x + 1, :], 1.0, 0.0)
        place = jnp.where(lanes < 96, here, 0.0).astype(BF16)
        end = jnp.where(lanes >= 96, here, 0.0).astype(BF16)
        left_rows = jnp.concatenate(
            [jnp.where(who == d, piece, 0.0) for piece in pieces_of(values, 3) for d in range(ranks)], 0
        )
        packed = packed + added(dot(left_rows.astype(BF16), place, True), 3)
        weight_rows = jnp.concatenate(
            [
                jnp.where((who == d - 1 + field_row) & (field_row < 3), scale, 0.0)
                for d in range(ranks)
            ],
            0,
        )
        weights = weights + dot(weight_rows.astype(BF16), end, True)
    lane = lax.broadcasted_iota(jnp.int32, (8, 128), 1)
    zero = jnp.zeros((8, 128), F32)
    for d in range(ranks):
        mine = packed[d * 8 : d * 8 + 8]
        before = packed[d * 8 - 8 : d * 8] if d > 0 else zero
        after = packed[d * 8 + 8 : d * 8 + 16] if d < ranks - 1 else zero
        block = jnp.where(lane < 32, before, jnp.where(lane < 64, mine, after))
        block = jnp.where(lane < 96, block, 0.0) + weights[d * 8 : d * 8 + 8]
        payload[d] = block + tile
    for copy in copies:
        copy.wait()


def row_of(matrix, k):
    return jnp.sum(jnp.where(at(matrix, 0) == k, matrix, 0.0), 0, keepdims=True)


def column_of(matrix, k):
    return jnp.sum(jnp.where(at(matrix, 1) == k, matrix, 0.0), 1, keepdims=True)


def eliminate(columns, right, first):
    row = at(right, 0)
    lengths = [TINY * column[first + k : first + k + 1] for k, column in enumerate(columns)]
    for k in range(len(columns)):
        column = columns[k]
        here = first + k
        pivot = column[here : here + 1]
        good = pivot > lengths[k]
        inverse = jnp.where(good, 1.0 / jnp.where(good, pivot, 1.0), 0.0)
        factor = column * inverse

        def reduced(values):
            mine = values[here : here + 1]
            return jnp.where(row == here, mine * inverse, values - factor * mine)

        columns = columns[: k + 1] + [reduced(values) for values in columns[k + 1 :]]
        right = reduced(right)
    return right


def galerkin(gram, first, shifts, back, energy):
    count = len(shifts)
    images = []
    for k in range(count - 1):
        image = shifts[k] * gram[k] + gram[k + 1]
        if k > 0:
            image = image + back[k - 1] * gram[k - 1]
        images.append(image)
    last = jnp.broadcast_to(gram[count - 1], (gram[0].shape[0], 128))
    row = at(last, 0)
    shift, prior = 0.0, 0.0
    for k in range(count):
        shift = jnp.where(row == first + k, shifts[k], shift)
    for k in range(1, count):
        prior = jnp.where(row == first + k, back[k - 1], prior)
    size = last.shape[0]
    image = shift * last + pltpu.roll(last, size - 1, 0) + prior * pltpu.roll(last, 1, 0)
    image = jnp.where(row == first + count - 1, energy, image)
    images.append(image[:, 0:1])
    return images


def shell_kernel(
    received, own, mate, other,
    displacement, residual_prev, solved_prev, residual_history, solved_history,
    payload, basis, factors, work, diagonal, off, table, sent, *, ranks,
):
    received = received()
    lane8 = lax.broadcasted_iota(jnp.int32, (8, 128), 1)
    summed = received[0]
    for p in range(1, ranks):
        summed = summed + received[p]
    gram = [column_of(summed, 96 + k) for k in range(PITERS + 1)]
    system = galerkin(gram[:PITERS], 3, P_SHIFT, P_BACK, gram[PITERS][7:8])
    solved = eliminate(system, gram[0], 3)
    solved = jnp.where(lax.broadcasted_iota(jnp.int32, (8, 1), 0) >= 3, solved, 0.0)
    factors[...] = jnp.broadcast_to(solved, (8, 128))
    groups = [lane8 // 32 == q for q in range(4)]

    def gathered(j):
        chunks = []
        for k in range(ranks // 4):
            chunk = jnp.zeros((8, 128), F32)
            for q in range(4):
                chunk = jnp.where(
                    groups[q], pltpu.roll(received[4 * k + q], (32 * (q - j)) % 128, 1), chunk
                )
            chunks.append(chunk)
        return jnp.concatenate(chunks, 1)

    left, right = sides(mate, other)
    weights = gathered(3)
    entries = ranks * CAP
    target = lax.broadcasted_iota(jnp.int32, (64, entries), 0)
    low = lax.broadcasted_iota(jnp.int32, (128, entries), 0)
    node = None
    for j in range(3):
        values = gathered(j)
        numbers = values[2:3, :].astype(jnp.int32)
        if j == 1:
            node = numbers
        rows = (
            values[0:1, :],
            WALL * jnp.sum(values * solved, 0, keepdims=True),
            values[1:2, :],
        )
        code = ((numbers >> 7) & 7) * 8 + (numbers >> 10)
        spot = jnp.where(low == (numbers & 127), 1.0, 0.0).astype(BF16)
        match = target == code
        pieces = pieces_of(jnp.concatenate(rows, 0), 2)
        left_rows = jnp.concatenate(
            [jnp.where(match, piece[c : c + 1], 0.0) for piece in pieces for c in range(3)], 0
        )
        scattered = added(dot(left_rows.astype(BF16), spot, True), 2)
        share = dot(jnp.where(match, weights[j : j + 1, :], 0.0).astype(BF16), spot, True)
        share = 1.0 / jnp.maximum(share, 1.0)
        ref = (left, own, right)[j]
        for c in range(3):
            force = scattered[c * 64 : c * 64 + 64] * share
            for k in range(8):
                place = (c * 8 + k) * 8
                work[0, c * 24 + j * 8 : c * 24 + j * 8 + 8, k * 128 : k * 128 + 128] = (
                    force[k * 8 : k * 8 + 8] + ref[place : place + 8, :]
                )
        stiff = jnp.concatenate(
            [ref[STIFF_AT + k * 8 : STIFF_AT + k * 8 + 8, :] for k in range(8)], 1
        )
        if j == 1:
            stiffness = stiff
        inside = stiff > 0.0
        main = jnp.where(inside, stiff + 4.0, 0.0)
        side = jnp.where(inside, 1.0, 0.0)
        for c in range(3):
            diagonal[c * 24 + j * 8 : c * 24 + j * 8 + 8, :] = main
            off[c * 24 + j * 8 : c * 24 + j * 8 + 8, :] = side
    copies = [
        pltpu.make_async_copy(work.at[k, pl.ds(c * 24 + 8, 8)], basis.at[k, c], sent.at[k, c])
        for k in range(SITERS)
        for c in range(3)
    ]
    for step in range(1, SITERS):
        now = work[step - 1]
        value = (diagonal[...] - S_SHIFT[step - 1]) * now - off[...] * shell_beside(now)
        if step > 1:
            value = value - S_BACK[step - 2] * work[step - 2]
        work[step] = value
        for copy in copies[step * 3 - 3 : step * 3]:
            copy.start()
    for copy in copies[-3:]:
        copy.start()
    def basis_tile(k, c, columns=slice(None)):
        return work[k, c * 24 + 8 : c * 24 + 16, columns]

    def tile_of(ref):
        return lambda c, columns=slice(None): ref[c, :, columns]

    vectors = [lambda c, columns=slice(None), k=k: basis_tile(k, c, columns) for k in range(SITERS)]
    vectors.append(tile_of(residual_prev))
    vectors += [tile_of(residual_history.at[k]) for k in range(residual_history.shape[0])]
    tile = jnp.zeros((16, 128), F32)
    pairs = [(i, j) for i in range(len(vectors)) for j in range(i, len(vectors))]
    for some in (pairs[:46], pairs[46:]):
        totals = [0.0] * len(some)
        used = sorted({v for pair in some for v in pair})
        for c in range(3):
            for k in range(8):
                tiles = {v: vectors[v](c, slice(k * 128, k * 128 + 128)) for v in used}
                totals = [total + tiles[i] * tiles[j] for total, (i, j) in zip(totals, some)]
        for total, (i, j) in zip(totals, some):
            tile = place_pair(tile, i, (96 + j, j, 96 + i), whole(total))
    top = SITERS - 1
    total = 0.0
    for c in range(3):
        now = basis_tile(top, c)
        after = work[top, c * 24 + 9 : c * 24 + 17, :]
        image = (4.0 + stiffness) * now - ahead(now, 1) - behind(now, 1) - 2.0 * after
        total = total + now * image
    tile = place_pair(tile, 13, (96 + 13, None, None), whole(fold(total)))
    fields = vectors[:SITERS] + [lambda c: displacement[c]]
    fields += [lambda c, k=k: solved_history[k, c] for k in range(solved_history.shape[0])]
    fields.append(lambda c: solved_prev[c])
    for c in range(3):
        for f in range(16):
            value = fields[f](c) if f < len(fields) else jnp.zeros((8, 1024), F32)
            for k in range(8):
                table[k, pl.ds(c * 16 + f, 8, stride=48), :] = value[:, k * 128 : k * 128 + 128]
    column = lax.broadcasted_iota(jnp.int32, (1024, entries), 0)
    pick = jnp.where(column == (node & 1023), 1.0, 0.0).astype(BF16)
    found = split_dot(jnp.concatenate([table[k] for k in range(8)], 1), pick, 2)
    line = node >> 10
    answer = jnp.zeros((48, entries), F32)
    for r in range(8):
        answer = jnp.where(line == r, found[r * 48 : r * 48 + 48], answer)
    lane16 = lax.broadcasted_iota(jnp.int32, (16, 128), 1)
    for p in range(ranks):
        k = p // 4
        block = tile
        for c in range(3):
            piece = answer[c * 16 : c * 16 + 16, k * 128 : k * 128 + 128]
            block = jnp.where(
                lane16 // 32 == c, pltpu.roll(piece, (32 * (c - p % 4)) % 128, 1), block
            )
        payload[p] = block
    for copy in copies:
        copy.wait()


def combine_kernel(basis, factors, pressure):
    basis = basis()
    for x in range(pressure.shape[0]):
        total = 0.0
        for k in range(PITERS):
            total = total + factors[3 + k : 4 + k, 0:1] * basis[k, x]
        pressure[x] = total


def update_kernel(
    received, basis, displacement, solved_prev, solved_history, owner, slots,
    new_displacement, wall, *, ranks,
):
    received = received()
    summed = received[0]
    for p in range(1, ranks):
        summed = summed + received[p]
    gram = [column_of(summed, 96 + k) for k in range(14)]
    system = galerkin(gram[:SITERS], 0, S_SHIFT, S_BACK, gram[13][13:14])
    steps = eliminate(system, gram[0], 0)
    down = lax.broadcasted_iota(jnp.int32, (16, 1), 0)
    steps = jnp.where(down < SITERS, steps, 0.0)
    base, count = SITERS, 1 + solved_history.shape[0]
    with_moved = sum(steps[k : k + 1] * gram[k] for k in range(SITERS))
    with_newest = with_moved - gram[base]
    newest_moved = jnp.sum(steps * with_newest, 0, keepdims=True)
    newest_newest = newest_moved - with_newest[base : base + 1]
    columns = [jnp.where(down == base, newest_newest, with_newest)]
    for k in range(1, count):
        columns.append(jnp.where(down == base, with_newest[base + k : base + k + 1], gram[base + k]))
    right = jnp.where(down == base, newest_moved, with_moved)
    coefficients = -eliminate(columns, right, base)
    newest = row_of(coefficients, base)
    factors = jnp.where(
        down < base,
        (1.0 + newest) * steps,
        jnp.where(
            down == base,
            1.0 + newest,
            jnp.where(down < base + count, coefficients, jnp.where(down == base + count, -newest, 0.0)),
        ),
    )
    for c in range(3):
        total = row_of(factors, base) * displacement[c]
        for k in range(SITERS):
            total = total + row_of(factors, k) * basis[k, c]
        for k in range(count - 1):
            total = total + row_of(factors, base + 1 + k) * solved_history[k, c]
        total = total + row_of(factors, base + count) * solved_prev[c]
        new_displacement[c] = total
    answers = jnp.concatenate(
        [jnp.sum(received[p] * factors, 0, keepdims=True) for p in range(ranks)], 0
    )
    group = at(answers, 1) // 32
    stacked = jnp.concatenate([jnp.where(group == c, answers, 0.0) for c in range(3)], 0)
    slot_row = lax.broadcasted_iota(jnp.int32, (128, 256), 0) & 31
    rank = lax.broadcasted_iota(jnp.int32, (ranks, 256), 0)
    for x in range(owner.shape[0]):
        pick = jnp.where(slot_row == slots[x : x + 1, :], 1.0, 0.0).astype(BF16)
        spread = split_dot(stacked, pick, 3)
        mine = rank == owner[x : x + 1, :]
        for c in range(3):
            wall[c : c + 1, x * 256 : x * 256 + 256] = jnp.sum(
                jnp.where(mine, spread[c * ranks : (c + 1) * ranks], 0.0), 0, keepdims=True
            )


def on_device(
    velocity,
    pressure_shift,
    owner_rank,
    node_index,
    map_weight,
    shell_load,
    shell_stiffness,
    displacement,
    residual_prev,
    solved_prev,
    residual_history,
    solved_history,
):
    ranks = lax.axis_size("slab")
    layers = velocity.shape[1]
    kept = residual_history.shape[0]

    def with_mate(values):
        return lax.ppermute(values, "slab", [(i, i ^ 1) for i in range(ranks)])

    def with_other(values):
        pairs = [(i, i + 1) for i in range(1, ranks - 1, 2)]
        return lax.ppermute(values, "slab", pairs + [(j, i) for i, j in pairs])

    owner = owner_rank.reshape(layers, -1)
    node = node_index.reshape(layers, -1)
    weight = map_weight.reshape(layers, -1)
    plane = shape(*velocity.shape[2:])

    to_mate, to_other, own_left, own_right, source, wall = call(
        fluid_kernel,
        (
            shape(HALO_ROWS, 128), shape(HALO_ROWS, 128), plane, plane,
            shape(*velocity.shape[1:]), shape(8, 256),
        ),
        (velocity, displacement),
        outer=(0, 1),
        stored=(0, 1),
        scratch=(
            pltpu.VMEM(velocity.shape, F32),
            pltpu.VMEM(displacement.shape, F32),
            pltpu.SemaphoreType.DMA((4, max(layers, 1))),
        ),
    )
    halo_other, halo_mate = with_other(to_other), with_mate(to_mate)
    shift_other, shift_mate = with_other(pressure_shift), with_mate(pressure_shift)
    (slots,) = call(
        lambda *refs: slots_kernel(*refs[:2], ranks=ranks),
        (shape(layers, 256, dtype=jnp.int32),),
        (owner,),
    )
    fields, first, shell, wall = call(
        lambda *refs: source_kernel(*refs),
        (shape(FIELD_ROWS, 128), shape(128, 128), shape(SHELL_ROWS, 128), shape(8, 256)),
        (
            source, wall, own_left, own_right, halo_mate, halo_other,
            displacement, shell_load, shell_stiffness,
        ),
        pairs=(4,),
    )
    beyond = lax.ppermute(first, "slab", [(i, i - 2) for i in range(2, ranks)])
    fields_other, fields_mate = with_other(fields), with_mate(fields)
    shell_other, shell_mate = with_other(shell), with_mate(shell)
    payload, pressure_basis = call(
        lambda *refs: pressure_kernel(*refs, ranks=ranks),
        (shape(ranks, 8, 128), pltpu.HBM((PITERS, *pressure_shift.shape), F32)),
        (
            fields, fields_mate, fields_other, beyond, pressure_shift, shift_mate, shift_other,
            wall, owner, slots, node, weight,
        ),
        direct=(1,),
        scratch=(
            pltpu.VMEM((PITERS, 13, 64, 256), F32),
            pltpu.VMEM((12, 64, 256), F32),
            pltpu.VMEM((12, 64, 256), F32),
            pltpu.SemaphoreType.DMA((PITERS,)),
        ),
    )
    received = lax.all_to_all(payload, "slab", split_axis=0, concat_axis=0, tiled=True)
    payload, shell_basis, factors = call(
        lambda *refs: shell_kernel(*refs, ranks=ranks),
        (shape(ranks, 16, 128), pltpu.HBM((SITERS, *displacement.shape), F32), shape(8, 128)),
        (
            received, shell, shell_mate, shell_other,
            displacement, residual_prev, solved_prev, residual_history, solved_history,
        ),
        late=(0,),
        direct=(1,),
        scratch=(
            pltpu.VMEM((SITERS, 72, 1024), F32),
            pltpu.VMEM((72, 1024), F32),
            pltpu.VMEM((72, 1024), F32),
            pltpu.VMEM((8, 8 * 48, 128), F32),
            pltpu.SemaphoreType.DMA((SITERS, 3)),
        ),
    )
    answers = lax.all_to_all(payload, "slab", split_axis=0, concat_axis=0, tiled=True)
    (pressure,) = call(
        combine_kernel,
        (shape(*pressure_shift.shape),),
        (pressure_basis, factors),
        late=(0,),
        stored=(0,),
    )
    new_displacement, wall_displacement = call(
        lambda *refs: update_kernel(*refs, ranks=ranks),
        (shape(*displacement.shape), shape(3, owner_rank.shape[0])),
        (answers, shell_basis, displacement, solved_prev, solved_history, owner, slots),
        late=(0,),
    )
    return (pressure, new_displacement, wall_displacement)


def solution(mesh):
    in_specs = (
        P(None, ("groups", "slab"), None, None),
        P(("groups", "slab"), None, None),
        P(("groups", "slab"), None),
        P(("groups", "slab")),
        P(("groups", "slab")),
        P(None, ("groups", "slab"), None),
        P(("groups", "slab"), None),
        P(None, ("groups", "slab"), None),
        P(None, ("groups", "slab"), None),
        P(None, ("groups", "slab"), None),
        P(None, None, ("groups", "slab"), None),
        P(None, None, ("groups", "slab"), None),
    )
    out_specs = (
        P(("groups", "slab"), None, None),
        P(None, ("groups", "slab"), None),
        P(None, ("groups", "slab")),
    )
    return jax.shard_map(
        on_device, mesh=mesh, in_specs=in_specs, out_specs=out_specs, check_vma=False
    )
```

```python
import jax
import jax.numpy as jnp
from jax import lax
from jax.experimental import pallas as pl
from jax.experimental.pallas import tpu as pltpu
from jax.sharding import PartitionSpec as P

CAP = 32
PITERS = 5
SITERS = 8

NU = 0.15
MU = 0.5
WALL = 4.0

P_SHIFT, P_BACK = (4.93, 7.29, 5.13, 7.05, 5.38), (10.17, 6.01, 8.86, 8.24)
S_SHIFT = (5.7, 5.09, 4.26, 4.26, 4.08, 4.17, 4.1, 4.18)
S_BACK = (2.53, 3.17, 4.07, 3.95, 4.22, 4.01, 4.14)
TINY = 1e-7

VMEM = pl.BlockSpec(memory_space=pltpu.VMEM)
F32 = jnp.float32
BF16 = jnp.bfloat16

H2_AT, ROW_AT, DISP_AT, HALO_ROWS = 128, 256, 264, 288
FIELD_ROWS, STIFF_AT, SHELL_ROWS = 512, 192, 256


def even_device():
    return lax.rem(lax.axis_index("slab"), 2) == 0


class Late:
    def __init__(self, source, place, semaphore):
        self.place = place
        self.copy = pltpu.make_async_copy(source, place, semaphore)
        self.copy.start()
        self.pending = True

    def __call__(self):
        if self.pending:
            self.copy.wait()
            self.pending = False
        return self.place


class Sides:
    def __init__(self, to_mate, to_other, left, right, semaphores):
        even = even_device()
        self.copies = [
            pltpu.make_async_copy(to_mate, left, semaphores.at[0]),
            pltpu.make_async_copy(to_other, right, semaphores.at[1]),
        ]
        self.places = (left, right)

        @pl.when(even)
        def _():
            pltpu.make_async_copy(to_other, left, semaphores.at[0]).start()
            pltpu.make_async_copy(to_mate, right, semaphores.at[1]).start()

        @pl.when(jnp.logical_not(even))
        def _():
            for copy in self.copies:
                copy.start()

        self.pending = True

    def __call__(self):
        if self.pending:
            for copy in self.copies:
                copy.wait()
            self.pending = False
        return self.places


class Either:
    def __init__(self, which, first, second):
        self.which, self.first, self.second = which, first, second

    def __getitem__(self, index):
        return jnp.where(self.which, self.first[index], self.second[index])


def sides(to_mate, to_other):
    even = even_device()
    return Either(even, to_other, to_mate), Either(even, to_mate, to_other)


def call(
    kernel, outs, args, late=(), outer=(), pairs=(), direct=(), stored=(), scratch=(),
    flops=1000000000, limit=48.0,
):
    count, made = len(args), len(outs)

    def body(*refs):
        operands = list(refs[:count])
        at_end = count + made + len(scratch)
        places = iter(refs[at_end:-1])
        wanted = []
        used = 0
        for i in late:
            operands[i] = Late(operands[i], next(places), refs[-1].at[used])
            wanted.append(operands[i])
            used += 1
        for i in pairs:
            operands[i] = Sides(
                operands[i], operands[i + 1], next(places), next(places), refs[-1].at[pl.ds(used, 2)]
            )
            wanted.append(operands[i])
            used += 2
        operands = [value for i, value in enumerate(operands) if i - 1 not in pairs]
        kernel(*operands, *refs[count:at_end])
        for value in wanted:
            value()

    outside = [i for i in late] + [i + k for i in pairs for k in (0, 1)]
    extra = [pltpu.VMEM(args[i].shape, args[i].dtype) for i in outside]
    extra.append(pltpu.SemaphoreType.DMA((max(1, len(outside)),)))
    args = [
        pltpu.with_memory_space_constraint(value, pltpu.HBM) if i in stored else value
        for i, value in enumerate(args)
    ]
    any_space = pl.BlockSpec(memory_space=pl.ANY)
    return pl.pallas_call(
        body,
        out_shape=outs,
        in_specs=[any_space if i in outside or i in outer else VMEM for i in range(count)],
        out_specs=tuple(any_space if i in direct else VMEM for i in range(made)),
        scratch_shapes=list(scratch) + extra,
        compiler_params=pltpu.CompilerParams(vmem_limit_bytes=int(limit * 1024 * 1024)),
        cost_estimate=pl.CostEstimate(flops=flops, bytes_accessed=0, transcendentals=0),
    )(*args)


def shape(*dims, dtype=F32):
    return jax.ShapeDtypeStruct(dims, dtype)


def at(values, axis):
    return lax.broadcasted_iota(jnp.int32, values.shape, axis)


def without_edge(values, axis, index):
    width = (8, 128)[axis]
    size = values.shape[axis]
    edge = 0 if index == 0 else size - width
    tile = lax.slice_in_dim(values, edge, edge + width, axis=axis)
    tile = jnp.where(at(tile, axis) == index - edge, 0.0, tile)
    if index == 0:
        rest = lax.slice_in_dim(values, width, size, axis=axis)
        return jnp.concatenate([tile, rest], axis)
    return jnp.concatenate([lax.slice_in_dim(values, 0, edge, axis=axis), tile], axis)


def ahead(values, axis):
    size = values.shape[axis]
    return without_edge(pltpu.roll(values, size - 1, axis), axis, size - 1)


def behind(values, axis):
    return without_edge(pltpu.roll(values, 1, axis), axis, 0)


def plane_sum(plane):
    return ahead(plane, 0) + behind(plane, 0) + ahead(plane, 1) + behind(plane, 1)


def difference(plane, axis):
    return ahead(plane, axis) - behind(plane, axis)


def halves(ref, start):
    return jnp.concatenate([ref[start : start + 64, :], ref[start + 64 : start + 128, :]], axis=1)


def put_halves(ref, start, plane):
    ref[start : start + 64, :] = plane[:, :128]
    ref[start + 64 : start + 128, :] = plane[:, 128:]


def parts(values, count):
    pieces = []
    for _ in range(count - 1):
        piece = values.astype(BF16)
        pieces.append(piece)
        values = values - piece.astype(F32)
    pieces.append(values.astype(BF16))
    return pieces


def dot(left, right, transposed=False):
    dims = (((1,), (1 if transposed else 0,)), ((), ()))
    return lax.dot_general(left, right, dims, preferred_element_type=F32)


def pieces_of(values, count):
    pieces = []
    for _ in range(count):
        pieces.append(values.astype(BF16).astype(F32))
        values = values - pieces[-1]
    return pieces


def added(product, count):
    rows = product.shape[0] // count
    return sum(product[i * rows : (i + 1) * rows] for i in range(count))


def split_dot(left, right, count, transposed=False):
    rows = left.shape[0]
    product = dot(jnp.concatenate(parts(left, count), 0), right, transposed)
    return sum(product[i * rows : (i + 1) * rows] for i in range(count))


def fluid_kernel(
    velocity_in, displacement_in, to_mate, to_other, own_left, own_right, source, wall,
    velocity, displacement, arrived,
):
    copies = [pltpu.make_async_copy(velocity_in, velocity, arrived.at[0, 0])]
    copies.append(pltpu.make_async_copy(displacement_in, displacement, arrived.at[3, 0]))
    for copy in copies:
        copy.start()
    for copy in copies:
        copy.wait()
    even = even_device()
    layers = velocity.shape[1]
    last = layers - 1
    field = [[velocity[c, x] for x in range(layers)] for c in range(3)]
    own = [[(1.0 - 6.0 * NU) * f + NU * plane_sum(f) for f in rows] for rows in field]
    spread = {
        x: NU * (difference(field[1][x], 0) + difference(field[2][x], 1)) for x in (0, last)
    }
    lefts = (own[0][0] + NU * field[0][1] + spread[0], NU * field[0][0])
    rights = (spread[last] - own[0][last] - NU * field[0][last - 1], NU * field[0][last])
    own_left[...] = lefts[1]
    own_right[...] = rights[1]
    edges = [
        (MU * NU) * (velocity[2, x, 1:2, :] - velocity[2, x, 0:1, :]) for x in (0, last)
    ]
    for ref, first, second in ((to_mate, rights, lefts), (to_other, lefts, rights)):
        put_halves(ref, 0, jnp.where(even, first[0], second[0]))
        put_halves(ref, H2_AT, jnp.where(even, first[1], second[1]))
        ref[ROW_AT : DISP_AT, :] = jnp.zeros((8, 128), F32)
        ref[ROW_AT + 2 : ROW_AT + 3, :] = jnp.ones((1, 128), F32)
        edge = jnp.where(even, edges[int(first is rights)], edges[int(second is rights)])
        ref[ROW_AT : ROW_AT + 1, :] = edge[:, :128]
        ref[ROW_AT + 1 : ROW_AT + 2, :] = edge[:, 128:]
        for c in range(3):
            rows = (displacement[c, 0:1, :], displacement[c, 7:8, :])
            row = jnp.where(even, rows[int(first is rights)], rows[int(second is rights)])
            for k in range(8):
                place = DISP_AT + c * 8 + k
                ref[place : place + 1, :] = row[:, k * 128 : k * 128 + 128]
    zero = jnp.zeros_like(field[0][0])
    predicted = [
        [
            own[c][x]
            + NU
            * (
                (field[c][x + 1] if x < last else zero)
                + (field[c][x - 1] if x > 0 else zero)
            )
            for x in range(layers)
        ]
        for c in range(3)
    ]
    for x in range(layers):
        after = predicted[0][x + 1] if x < last else zero
        before = predicted[0][x - 1] if x > 0 else zero
        source[x] = -0.5 * (
            after - before + difference(predicted[1][x], 0) + difference(predicted[2][x], 1)
        )
        wall[x : x + 1, :] = MU * (predicted[0][x][1:2, :] - predicted[0][x][0:1, :])
        wall[4 + x : 5 + x, :] = MU * (predicted[2][x][1:2, :] - predicted[2][x][0:1, :])


def shell_beside(field):
    rows = field.shape[0]
    beside = pltpu.roll(field, rows - 1, 0) + pltpu.roll(field, 1, 0)
    return beside + ahead(field, 1) + behind(field, 1)


def source_kernel(
    source, wall, own_left, own_right, halo, displacement, load, stiffness,
    fields, first, shell, wall_out,
):
    from_left, from_right = halo()
    layers = source.shape[0]
    last = layers - 1
    left1, left2 = halves(from_left, 0), halves(from_left, H2_AT)
    right1, right2 = halves(from_right, 0), halves(from_right, H2_AT)
    has_left = from_left[ROW_AT + 2 : ROW_AT + 3, 0:1]
    has_right = from_right[ROW_AT + 2 : ROW_AT + 3, 0:1]
    left1 = left1 - has_left * own_left[...]
    right1 = right1 + has_right * own_right[...]
    for x in range(layers):
        plane = source[x]
        if x == 0:
            plane = plane - 0.5 * left1
        if x == 1:
            plane = plane + 0.5 * left2
        if x == last - 1:
            plane = plane - 0.5 * right2
        if x == last:
            plane = plane - 0.5 * right1
        put_halves(fields, x * 128, plane)
        if x == 0:
            put_halves(first, 0, plane)
    wall_out[...] = wall[...]
    for x, ref, plane in ((0, from_left, left2), (last, from_right, right2)):
        edge = jnp.concatenate([ref[ROW_AT : ROW_AT + 1, :], ref[ROW_AT + 1 : ROW_AT + 2, :]], 1)
        wall_out[x : x + 1, :] = wall[x : x + 1, :] + MU * (plane[1:2, :] - plane[0:1, :])
        wall_out[4 + x : 5 + x, :] = wall[4 + x : 5 + x, :] + edge
    for c in range(3):
        field = displacement[c]
        above = jnp.concatenate(
            [from_left[DISP_AT + c * 8 + k : DISP_AT + c * 8 + k + 1, :] for k in range(8)], 1
        )
        below = jnp.concatenate(
            [from_right[DISP_AT + c * 8 + k : DISP_AT + c * 8 + k + 1, :] for k in range(8)], 1
        )
        row = at(field, 0)
        beside = jnp.where(row == 0, above, pltpu.roll(field, 1, 0))
        beside = beside + jnp.where(row == 7, below, pltpu.roll(field, 7, 0))
        beside = beside + ahead(field, 1) + behind(field, 1)
        start = load[c] - ((4.0 + stiffness[...]) * field - beside)
        for k in range(8):
            place = (c * 8 + k) * 8
            shell[place : place + 8, :] = start[:, k * 128 : k * 128 + 128]
    for k in range(8):
        place = STIFF_AT + k * 8
        shell[place : place + 8, :] = stiffness[:, k * 128 : k * 128 + 128]


def slots_kernel(owner, slots, *, ranks):
    width = owner.shape[1]
    down = lax.broadcasted_iota(jnp.int32, (width, width), 0)
    across = lax.broadcasted_iota(jnp.int32, (width, width), 1)
    earlier = jnp.where(down < across, 1.0, 0.0).astype(BF16)
    rank = lax.broadcasted_iota(jnp.int32, (ranks, width), 0)
    seen = jnp.zeros((ranks, 1), F32)
    for x in range(owner.shape[0]):
        member = jnp.where(rank == owner[x : x + 1, :], 1.0, 0.0)
        before = dot(member.astype(BF16), earlier) + seen
        slots[x : x + 1, :] = jnp.sum(before * member, 0, keepdims=True).astype(jnp.int32)
        seen = seen + jnp.sum(member, 1, keepdims=True)


def fold(product):
    rows, columns = product.shape
    tall = product[0:8]
    for a in range(1, rows // 8):
        tall = tall + product[a * 8 : a * 8 + 8]
    total = tall[:, :128]
    for b in range(1, columns // 128):
        total = total + tall[:, b * 128 : b * 128 + 128]
    return total


def whole(tile):
    return jnp.sum(jnp.sum(tile, 0, keepdims=True), 1, keepdims=True)


def place_pair(tile, i, j, value):
    row, lane = at(tile, 0), at(tile, 1)
    here = (row == i) & (lane == j[0])
    if j[1] is not None:
        here = here | ((row == j[1]) & (lane == j[2]))
    return jnp.where(here, value, tile)


def pressure_kernel(
    own, mate, other, beyond, shift, shift_mate, shift_other,
    wall, owner, slots, node, weight,
    payload, basis, work, sent, *, ranks,
):
    left, right = sides(mate, other)
    shift_left, shift_right = sides(shift_mate, shift_other)
    layers = shift.shape[0]
    for x in range(layers):
        work[0, x] = halves(left, x * 128)
        work[0, x + 4] = halves(own, x * 128)
        work[0, x + 8] = halves(right, x * 128)
    work[0, 12] = halves(beyond, 0)
    inside = [jnp.where(side[3 * end][0:1, 0:1] > 0.0, 1.0, 0.0) for side, end in ((shift_left, 1), (shift_right, 0))]
    copies = [
        pltpu.make_async_copy(work.at[k, pl.ds(4, layers)], basis.at[k], sent.at[k])
        for k in range(PITERS)
    ]
    copies[0].start()
    for step in range(1, PITERS):
        for x in range(step, 13 - step):
            now = work[step - 1, x]
            beside = work[step - 1, x - 1] + work[step - 1, x + 1] + plane_sum(now)
            if x < 4 or x >= 8:
                beside = inside[x // 8] * beside
            diagonal = (shift_left, shift, shift_right)[x // 4][x % 4] + (6.0 - P_SHIFT[step - 1])
            value = diagonal * now - beside
            if step > 1:
                value = value - P_BACK[step - 2] * work[step - 2, x]
            work[step, x] = value
        copies[step].start()
    tile = jnp.zeros((8, 128), F32)
    for i in range(PITERS):
        for j in range(i, PITERS):
            total = sum(work[i, x] * work[j, x] for x in range(4, 8))
            value = whole(fold(total))
            tile = place_pair(tile, 3 + i, (96 + j, 3 + j, 96 + i), value)
    top = PITERS - 1
    total = 0.0
    for x in range(4, 8):
        now = work[top, x]
        image = (6.0 + shift[x - 4]) * now - plane_sum(now) - 2.0 * work[top, x + 1]
        total = total + now * image
    tile = place_pair(tile, 3 + top, (96 + PITERS, None, None), whole(fold(total)))
    lanes = lax.broadcasted_iota(jnp.int32, (128, 256), 0)
    field_row = lax.broadcasted_iota(jnp.int32, (8, 256), 0)
    packed = jnp.zeros((ranks * 8, 128), F32)
    weights = jnp.zeros((ranks * 8, 128), F32)
    for x in range(layers):
        scale = weight[x : x + 1, :].astype(F32)
        rows = [wall[x : x + 1, :] * scale, wall[4 + x : 5 + x, :] * scale]
        rows.append(node[x : x + 1, :].astype(F32))
        rows += [work[k, x + 4][0:1, :] * scale for k in range(PITERS)]
        values = jnp.concatenate(rows, 0)
        who = owner[x : x + 1, :]
        here = jnp.where((lanes & 31) == slots[x : x + 1, :], 1.0, 0.0)
        place = jnp.where(lanes < 96, here, 0.0).astype(BF16)
        end = jnp.where(lanes >= 96, here, 0.0).astype(BF16)
        left_rows = jnp.concatenate(
            [jnp.where(who == d, piece, 0.0) for piece in pieces_of(values, 3) for d in range(ranks)], 0
        )
        packed = packed + added(dot(left_rows.astype(BF16), place, True), 3)
        weight_rows = jnp.concatenate(
            [
                jnp.where((who == d - 1 + field_row) & (field_row < 3), scale, 0.0)
                for d in range(ranks)
            ],
            0,
        )
        weights = weights + dot(weight_rows.astype(BF16), end, True)
    lane = lax.broadcasted_iota(jnp.int32, (8, 128), 1)
    zero = jnp.zeros((8, 128), F32)
    for d in range(ranks):
        mine = packed[d * 8 : d * 8 + 8]
        before = packed[d * 8 - 8 : d * 8] if d > 0 else zero
        after = packed[d * 8 + 8 : d * 8 + 16] if d < ranks - 1 else zero
        block = jnp.where(lane < 32, before, jnp.where(lane < 64, mine, after))
        block = jnp.where(lane < 96, block, 0.0) + weights[d * 8 : d * 8 + 8]
        payload[d] = block + tile
    for copy in copies:
        copy.wait()


def second_spot(i, j):
    if i < SITERS:
        return 6 + i % 4, 96 + 16 * (i // 4) + j
    return 10 + (i - SITERS) // 4, 96 + 8 * ((i - SITERS) % 4) + j - SITERS


ENERGY_AT = (11, 112)


def place_second(tile, i, j, value):
    row, lane = second_spot(i, j)
    if i < SITERS <= j:
        return place_pair(tile, row, (lane, None, None), value)
    return place_pair(tile, row, (lane, *second_spot(j, i)), value)


def second_gram(summed):
    row, lane = at(summed, 0), at(summed, 1)
    first = pltpu.roll(pltpu.roll(summed, 32, 1), 10, 0)
    second = pltpu.roll(pltpu.roll(summed, 16, 1), 14, 0)
    gram = jnp.where(row < 4, first, second)
    gram = jnp.where((row < SITERS) & (lane < 16), gram, 0.0)
    for k in range(5):
        source, start = second_spot(SITERS + k, SITERS)
        moved = pltpu.roll(summed, (SITERS - start) % 128, 1)[source : source + 1]
        here = (row == SITERS + k) & (lane >= SITERS) & (lane < SITERS + 5)
        gram = jnp.where(here, jnp.broadcast_to(moved, gram.shape), gram)
    return gram


def row_of(matrix, k):
    return jnp.sum(jnp.where(at(matrix, 0) == k, matrix, 0.0), 0, keepdims=True)


def column_of(matrix, k):
    return jnp.sum(jnp.where(at(matrix, 1) == k, matrix, 0.0), 1, keepdims=True)


def eliminate(columns, right, first):
    row = at(right, 0)
    lengths = [TINY * column[first + k : first + k + 1] for k, column in enumerate(columns)]
    for k in range(len(columns)):
        column = columns[k]
        here = first + k
        pivot = column[here : here + 1]
        good = pivot > lengths[k]
        inverse = jnp.where(good, 1.0 / jnp.where(good, pivot, 1.0), 0.0)
        factor = column * inverse

        def reduced(values):
            mine = values[here : here + 1]
            return jnp.where(row == here, mine * inverse, values - factor * mine)

        columns = columns[: k + 1] + [reduced(values) for values in columns[k + 1 :]]
        right = reduced(right)
    return right


def galerkin(gram, first, shifts, back, energy):
    count = len(shifts)
    images = []
    for k in range(count - 1):
        image = shifts[k] * gram[k] + gram[k + 1]
        if k > 0:
            image = image + back[k - 1] * gram[k - 1]
        images.append(image)
    last = jnp.broadcast_to(gram[count - 1], (gram[0].shape[0], 128))
    row = at(last, 0)
    shift, prior = 0.0, 0.0
    for k in range(count):
        shift = jnp.where(row == first + k, shifts[k], shift)
    for k in range(1, count):
        prior = jnp.where(row == first + k, back[k - 1], prior)
    size = last.shape[0]
    image = shift * last + pltpu.roll(last, size - 1, 0) + prior * pltpu.roll(last, 1, 0)
    image = jnp.where(row == first + count - 1, energy, image)
    images.append(image[:, 0:1])
    return images


def shell_kernel(
    received, own, mate, other,
    displacement, residual_prev, solved_prev, residual_history, solved_history,
    payload, basis, factors, work, diagonal, table, sent, *, ranks,
):
    lane8 = lax.broadcasted_iota(jnp.int32, (8, 128), 1)
    summed = received[0]
    for p in range(1, ranks):
        summed = summed + received[p]
    gram = [column_of(summed, 96 + k) for k in range(PITERS + 1)]
    system = galerkin(gram[:PITERS], 3, P_SHIFT, P_BACK, gram[PITERS][7:8])
    solved = eliminate(system, gram[0], 3)
    solved = jnp.where(lax.broadcasted_iota(jnp.int32, (8, 1), 0) >= 3, solved, 0.0)
    factors[...] = jnp.broadcast_to(solved, (8, 128))
    groups = [lane8 // 32 == q for q in range(4)]

    def gathered(j):
        chunks = []
        for k in range(ranks // 4):
            chunk = jnp.zeros((8, 128), F32)
            for q in range(4):
                chunk = jnp.where(
                    groups[q], pltpu.roll(received[4 * k + q], (32 * (q - j)) % 128, 1), chunk
                )
            chunks.append(chunk)
        return jnp.concatenate(chunks, 1)

    left, right = sides(mate, other)
    weights = gathered(3)
    entries = ranks * CAP
    target = lax.broadcasted_iota(jnp.int32, (64, entries), 0)
    low = lax.broadcasted_iota(jnp.int32, (128, entries), 0)
    node = None
    inside = []
    for j in range(3):
        values = gathered(j)
        numbers = values[2:3, :].astype(jnp.int32)
        if j == 1:
            node = numbers
        rows = (
            values[0:1, :],
            WALL * jnp.sum(values * solved, 0, keepdims=True),
            values[1:2, :],
        )
        code = ((numbers >> 7) & 7) * 8 + (numbers >> 10)
        spot = jnp.where(low == (numbers & 127), 1.0, 0.0).astype(BF16)
        match = target == code
        pieces = pieces_of(jnp.concatenate(rows, 0), 2)
        left_rows = jnp.concatenate(
            [jnp.where(match, piece[c : c + 1], 0.0) for piece in pieces for c in range(3)], 0
        )
        scattered = added(dot(left_rows.astype(BF16), spot, True), 2)
        share = dot(jnp.where(match, weights[j : j + 1, :], 0.0).astype(BF16), spot, True)
        share = 1.0 / jnp.maximum(share, 1.0)
        ref = (left, own, right)[j]
        for c in range(3):
            force = scattered[c * 64 : c * 64 + 64] * share
            for k in range(8):
                place = (c * 8 + k) * 8
                work[0, c, j * 8 : j * 8 + 8, k * 128 : k * 128 + 128] = (
                    force[k * 8 : k * 8 + 8] + ref[place : place + 8, :]
                )
        stiff = jnp.concatenate(
            [ref[STIFF_AT + k * 8 : STIFF_AT + k * 8 + 8, :] for k in range(8)], 1
        )
        if j == 1:
            stiffness = stiff
        for c in range(3):
            diagonal[c * 24 + j * 8 : c * 24 + j * 8 + 8, :] = stiff
        inside.append(jnp.where(stiff[:, 0:1] > 0.0, 1.0, 0.0))
    inside = jnp.concatenate(inside * 3, 0)
    copies = [
        pltpu.make_async_copy(work.at[k, :, pl.ds(8, 8)], basis.at[k], sent.at[k])
        for k in range(SITERS)
    ]
    for step in range(1, SITERS):
        now = work[step - 1].reshape(72, 1024)
        value = (diagonal[...] + (4.0 - S_SHIFT[step - 1])) * now - inside * shell_beside(now)
        if step > 1:
            value = value - S_BACK[step - 2] * work[step - 2].reshape(72, 1024)
        work[step] = value.reshape(3, 24, 1024)
        copies[step - 1].start()
    copies[-1].start()
    def basis_tile(k, c, columns=slice(None)):
        return work[k, c, 8:16, columns]

    def tile_of(ref):
        return lambda c, columns=slice(None): ref[c, :, columns]

    vectors = [lambda c, columns=slice(None), k=k: basis_tile(k, c, columns) for k in range(SITERS)]
    vectors.append(tile_of(residual_prev))
    vectors += [tile_of(residual_history.at[k]) for k in range(residual_history.shape[0])]
    tile = jnp.zeros((16, 128), F32)
    pairs = [(i, j) for i in range(len(vectors)) for j in range(i, len(vectors))]
    for some in (pairs[:46], pairs[46:]):
        totals = [0.0] * len(some)
        used = sorted({v for pair in some for v in pair})
        for c in range(3):
            for k in range(8):
                tiles = {v: vectors[v](c, slice(k * 128, k * 128 + 128)) for v in used}
                totals = [total + tiles[i] * tiles[j] for total, (i, j) in zip(totals, some)]
        for total, (i, j) in zip(totals, some):
            tile = place_second(tile, i, j, whole(total))
    top = SITERS - 1
    total = 0.0
    for c in range(3):
        now = basis_tile(top, c)
        after = work[top, c, 9:17, :]
        image = (4.0 + stiffness) * now - ahead(now, 1) - behind(now, 1) - 2.0 * after
        total = total + now * image
    tile = place_pair(tile, ENERGY_AT[0], (ENERGY_AT[1], None, None), whole(fold(total)))
    fields = vectors[:SITERS] + [lambda c: displacement[c]]
    fields += [lambda c, k=k: solved_history[k, c] for k in range(solved_history.shape[0])]
    fields.append(lambda c: solved_prev[c])
    for c in range(3):
        for f in range(16):
            value = fields[f](c) if f < len(fields) else jnp.zeros((8, 1024), F32)
            for k in range(8):
                table[k, pl.ds(c * 16 + f, 8, stride=48), :] = value[:, k * 128 : k * 128 + 128]
    column = lax.broadcasted_iota(jnp.int32, (1024, entries), 0)
    pick = jnp.where(column == (node & 1023), 1.0, 0.0).astype(BF16)
    found = split_dot(jnp.concatenate([table[k] for k in range(8)], 1), pick, 2)
    line = node >> 10
    answer = jnp.zeros((48, entries), F32)
    for r in range(8):
        answer = jnp.where(line == r, found[r * 48 : r * 48 + 48], answer)
    lane16 = lax.broadcasted_iota(jnp.int32, (16, 128), 1)
    row16 = lax.broadcasted_iota(jnp.int32, (16, 128), 0)
    extra = jnp.concatenate(
        [answer[c * 16 + 12 : c * 16 + 14] for c in range(3)] + [jnp.zeros((10, entries), F32)], 0
    )
    for p in range(ranks):
        columns = slice(p // 4 * 128, p // 4 * 128 + 128)
        block = jnp.where(row16 < 6, pltpu.roll(extra[:, columns], (32 * (3 - p % 4)) % 128, 1), tile)
        for c in range(3):
            piece = answer[c * 16 : c * 16 + 16, columns]
            block = jnp.where(
                lane16 // 32 == c, pltpu.roll(piece, (32 * (c - p % 4)) % 128, 1), block
            )
        for t in range(3):
            payload[p, t] = block[t * 4 : t * 4 + 4]
    for copy in copies:
        copy.wait()


def combine_kernel(basis, factors, pressure):
    basis = basis()
    for x in range(pressure.shape[0]):
        total = 0.0
        for k in range(PITERS):
            total = total + factors[3 + k : 4 + k, 0:1] * basis[k, x]
        pressure[x] = total


def update_kernel(
    received, basis, displacement, solved_prev, solved_history, owner, slots,
    new_displacement, wall, *, ranks,
):
    blocks = [
        jnp.concatenate([received[p, t] for t in range(3)] + [jnp.zeros((4, 128), F32)], 0)
        for p in range(ranks)
    ]
    summed = sum(blocks)
    matrix = second_gram(summed)
    gram = [column_of(matrix, k) for k in range(SITERS + 5)]
    energy = summed[ENERGY_AT[0] : ENERGY_AT[0] + 1, ENERGY_AT[1] : ENERGY_AT[1] + 1]
    system = galerkin(gram[:SITERS], 0, S_SHIFT, S_BACK, energy)
    steps = eliminate(system, gram[0], 0)
    down = lax.broadcasted_iota(jnp.int32, (16, 1), 0)
    steps = jnp.where(down < SITERS, steps, 0.0)
    base, count = SITERS, 1 + solved_history.shape[0]
    with_moved = jnp.sum(matrix * steps, 0, keepdims=True)
    diagonal = at(matrix, 0) == at(matrix, 1)
    with_moved = jnp.sum(
        jnp.where(diagonal, jnp.broadcast_to(with_moved, matrix.shape), 0.0), 1, keepdims=True
    )
    with_newest = with_moved - gram[base]
    newest_moved = jnp.sum(steps * with_newest, 0, keepdims=True)
    newest_newest = newest_moved - with_newest[base : base + 1]
    columns = [jnp.where(down == base, newest_newest, with_newest)]
    for k in range(1, count):
        columns.append(jnp.where(down == base, with_newest[base + k : base + k + 1], gram[base + k]))
    right = jnp.where(down == base, newest_moved, with_moved)
    coefficients = -eliminate(columns, right, base)
    newest = row_of(coefficients, base)
    factors = jnp.where(
        down < base,
        (1.0 + newest) * steps,
        jnp.where(
            down == base,
            1.0 + newest,
            jnp.where(down < base + count, coefficients, jnp.where(down == base + count, -newest, 0.0)),
        ),
    )
    for c in range(3):
        total = row_of(factors, base) * displacement[c]
        for k in range(SITERS):
            total = total + row_of(factors, k) * basis[k, c]
        for k in range(count - 1):
            total = total + row_of(factors, base + 1 + k) * solved_history[k, c]
        total = total + row_of(factors, base + count) * solved_prev[c]
        new_displacement[c] = total
    row, group = at(summed, 0), at(summed, 1) // 32
    spare = jnp.where(row % 2 == 0, factors[12:13], factors[13:14])
    stacked = []
    for c in range(3):
        scales = jnp.where(group == c, factors, jnp.where((group == 3) & (row // 2 == c), spare, 0.0))
        stacked += [jnp.sum(block * scales, 0, keepdims=True) for block in blocks]
    stacked = jnp.concatenate(stacked, 0)
    slot_row = lax.broadcasted_iota(jnp.int32, (128, 256), 0) & 31
    rank = lax.broadcasted_iota(jnp.int32, (ranks, 256), 0)
    for x in range(owner.shape[0]):
        pick = jnp.where(slot_row == slots[x : x + 1, :], 1.0, 0.0).astype(BF16)
        spread = split_dot(stacked, pick, 3)
        mine = rank == owner[x : x + 1, :]
        for c in range(3):
            wall[c : c + 1, x * 256 : x * 256 + 256] = jnp.sum(
                jnp.where(mine, spread[c * ranks : (c + 1) * ranks], 0.0), 0, keepdims=True
            )


def on_device(
    velocity,
    pressure_shift,
    owner_rank,
    node_index,
    map_weight,
    shell_load,
    shell_stiffness,
    displacement,
    residual_prev,
    solved_prev,
    residual_history,
    solved_history,
):
    ranks = lax.axis_size("slab")
    layers = velocity.shape[1]
    kept = residual_history.shape[0]

    def with_mate(values):
        return lax.ppermute(values, "slab", [(i, i ^ 1) for i in range(ranks)])

    def with_other(values):
        pairs = [(i, i + 1) for i in range(1, ranks - 1, 2)]
        return lax.ppermute(values, "slab", pairs + [(j, i) for i, j in pairs])

    owner = owner_rank.reshape(layers, -1)
    node = node_index.reshape(layers, -1)
    weight = map_weight.reshape(layers, -1)
    plane = shape(*velocity.shape[2:])

    to_mate, to_other, own_left, own_right, source, wall = call(
        fluid_kernel,
        (
            shape(HALO_ROWS, 128), shape(HALO_ROWS, 128), plane, plane,
            shape(*velocity.shape[1:]), shape(8, 256),
        ),
        (velocity, displacement),
        outer=(0, 1),
        stored=(0, 1),
        scratch=(
            pltpu.VMEM(velocity.shape, F32),
            pltpu.VMEM(displacement.shape, F32),
            pltpu.SemaphoreType.DMA((4, max(layers, 1))),
        ),
    )
    halo_other, halo_mate = with_other(to_other), with_mate(to_mate)
    shift_other, shift_mate = with_other(pressure_shift), with_mate(pressure_shift)
    (slots,) = call(
        lambda *refs: slots_kernel(*refs[:2], ranks=ranks),
        (shape(layers, 256, dtype=jnp.int32),),
        (owner,),
    )
    fields, first, shell, wall = call(
        lambda *refs: source_kernel(*refs),
        (shape(FIELD_ROWS, 128), shape(128, 128), shape(SHELL_ROWS, 128), shape(8, 256)),
        (
            source, wall, own_left, own_right, halo_mate, halo_other,
            displacement, shell_load, shell_stiffness,
        ),
        pairs=(4,),
    )
    beyond = lax.ppermute(first, "slab", [(i, i - 2) for i in range(2, ranks)])
    fields_other, fields_mate = with_other(fields), with_mate(fields)
    shell_other, shell_mate = with_other(shell), with_mate(shell)
    payload, pressure_basis = call(
        lambda *refs: pressure_kernel(*refs, ranks=ranks),
        (shape(ranks, 8, 128), pltpu.HBM((PITERS, *pressure_shift.shape), F32)),
        (
            fields, fields_mate, fields_other, beyond, pressure_shift, shift_mate, shift_other,
            wall, owner, slots, node, weight,
        ),
        direct=(1,),
        scratch=(
            pltpu.VMEM((PITERS, 13, 64, 256), F32),
            pltpu.SemaphoreType.DMA((PITERS,)),
        ),
    )
    received = lax.all_to_all(payload, "slab", split_axis=0, concat_axis=0, tiled=True)
    payload, shell_basis, factors = call(
        lambda *refs: shell_kernel(*refs, ranks=ranks),
        (shape(ranks, 3, 4, 128), pltpu.HBM((SITERS, *displacement.shape), F32), shape(8, 128)),
        (
            received, shell, shell_mate, shell_other,
            displacement, residual_prev, solved_prev, residual_history, solved_history,
        ),
        direct=(1,),
        scratch=(
            pltpu.VMEM((SITERS, 3, 24, 1024), F32),
            pltpu.VMEM((72, 1024), F32),
            pltpu.VMEM((8, 8 * 48, 128), F32),
            pltpu.SemaphoreType.DMA((SITERS,)),
        ),
    )
    answers = lax.all_to_all(payload, "slab", split_axis=0, concat_axis=0, tiled=True)
    (pressure,) = call(
        combine_kernel,
        (shape(*pressure_shift.shape),),
        (pressure_basis, factors),
        late=(0,),
        stored=(0,),
    )
    new_displacement, wall_displacement = call(
        lambda *refs: update_kernel(*refs, ranks=ranks),
        (shape(*displacement.shape), shape(3, owner_rank.shape[0])),
        (answers, shell_basis, displacement, solved_prev, solved_history, owner, slots),
    )
    return (pressure, new_displacement, wall_displacement)


def solution(mesh):
    in_specs = (
        P(None, ("groups", "slab"), None, None),
        P(("groups", "slab"), None, None),
        P(("groups", "slab"), None),
        P(("groups", "slab")),
        P(("groups", "slab")),
        P(None, ("groups", "slab"), None),
        P(("groups", "slab"), None),
        P(None, ("groups", "slab"), None),
        P(None, ("groups", "slab"), None),
        P(None, ("groups", "slab"), None),
        P(None, None, ("groups", "slab"), None),
        P(None, None, ("groups", "slab"), None),
    )
    out_specs = (
        P(("groups", "slab"), None, None),
        P(None, ("groups", "slab"), None),
        P(None, ("groups", "slab")),
    )
    return jax.shard_map(
        on_device, mesh=mesh, in_specs=in_specs, out_specs=out_specs, check_vma=False
    )
```

```python
import jax
import jax.numpy as jnp
from jax import lax
from jax.experimental import pallas as pl
from jax.experimental.pallas import tpu as pltpu
from jax.sharding import PartitionSpec as P

CAP = 32
PITERS = 5
SITERS = 8

NU = 0.15
MU = 0.5
WALL = 4.0

P_SHIFT, P_BACK = (4.93, 7.29, 5.13, 7.05, 5.38), (10.17, 6.01, 8.86, 8.24)
S_SHIFT = (5.7, 5.09, 4.26, 4.26, 4.08, 4.17, 4.1, 4.18)
S_BACK = (2.53, 3.17, 4.07, 3.95, 4.22, 4.01, 4.14)
TINY = 1e-7

VMEM = pl.BlockSpec(memory_space=pltpu.VMEM)
F32 = jnp.float32
BF16 = jnp.bfloat16

H2_AT, ROW_AT, DISP_AT, HALO_ROWS = 128, 256, 264, 288
FIELD_ROWS, STIFF_AT, SHELL_ROWS = 512, 192, 256


def even_device():
    return lax.rem(lax.axis_index("slab"), 2) == 0


class Late:
    def __init__(self, source, place, semaphore):
        self.place = place
        self.copy = pltpu.make_async_copy(source, place, semaphore)
        self.copy.start()
        self.pending = True

    def __call__(self):
        if self.pending:
            self.copy.wait()
            self.pending = False
        return self.place


class Sides:
    def __init__(self, to_mate, to_other, left, right, semaphores):
        even = even_device()
        self.copies = [
            pltpu.make_async_copy(to_mate, left, semaphores.at[0]),
            pltpu.make_async_copy(to_other, right, semaphores.at[1]),
        ]
        self.places = (left, right)

        @pl.when(even)
        def _():
            pltpu.make_async_copy(to_other, left, semaphores.at[0]).start()
            pltpu.make_async_copy(to_mate, right, semaphores.at[1]).start()

        @pl.when(jnp.logical_not(even))
        def _():
            for copy in self.copies:
                copy.start()

        self.pending = True

    def __call__(self):
        if self.pending:
            for copy in self.copies:
                copy.wait()
            self.pending = False
        return self.places


class Either:
    def __init__(self, which, first, second):
        self.which, self.first, self.second = which, first, second

    def __getitem__(self, index):
        return jnp.where(self.which, self.first[index], self.second[index])


def sides(to_mate, to_other):
    even = even_device()
    return Either(even, to_other, to_mate), Either(even, to_mate, to_other)


def call(
    kernel, outs, args, late=(), outer=(), pairs=(), direct=(), stored=(), scratch=(),
    flops=1000000000, limit=48.0,
):
    count, made = len(args), len(outs)

    def body(*refs):
        operands = list(refs[:count])
        at_end = count + made + len(scratch)
        places = iter(refs[at_end:-1])
        wanted = []
        used = 0
        for i in late:
            operands[i] = Late(operands[i], next(places), refs[-1].at[used])
            wanted.append(operands[i])
            used += 1
        for i in pairs:
            operands[i] = Sides(
                operands[i], operands[i + 1], next(places), next(places), refs[-1].at[pl.ds(used, 2)]
            )
            wanted.append(operands[i])
            used += 2
        operands = [value for i, value in enumerate(operands) if i - 1 not in pairs]
        kernel(*operands, *refs[count:at_end])
        for value in wanted:
            value()

    outside = [i for i in late] + [i + k for i in pairs for k in (0, 1)]
    extra = [pltpu.VMEM(args[i].shape, args[i].dtype) for i in outside]
    extra.append(pltpu.SemaphoreType.DMA((max(1, len(outside)),)))
    args = [
        pltpu.with_memory_space_constraint(value, pltpu.HBM) if i in stored else value
        for i, value in enumerate(args)
    ]
    any_space = pl.BlockSpec(memory_space=pl.ANY)
    return pl.pallas_call(
        body,
        out_shape=outs,
        in_specs=[any_space if i in outside or i in outer else VMEM for i in range(count)],
        out_specs=tuple(any_space if i in direct else VMEM for i in range(made)),
        scratch_shapes=list(scratch) + extra,
        compiler_params=pltpu.CompilerParams(vmem_limit_bytes=int(limit * 1024 * 1024)),
        cost_estimate=pl.CostEstimate(flops=flops, bytes_accessed=0, transcendentals=0),
    )(*args)


def shape(*dims, dtype=F32):
    return jax.ShapeDtypeStruct(dims, dtype)


def at(values, axis):
    return lax.broadcasted_iota(jnp.int32, values.shape, axis)


def without_edge(values, axis, index):
    width = (8, 128)[axis]
    size = values.shape[axis]
    edge = 0 if index == 0 else size - width
    tile = lax.slice_in_dim(values, edge, edge + width, axis=axis)
    tile = jnp.where(at(tile, axis) == index - edge, 0.0, tile)
    if index == 0:
        rest = lax.slice_in_dim(values, width, size, axis=axis)
        return jnp.concatenate([tile, rest], axis)
    return jnp.concatenate([lax.slice_in_dim(values, 0, edge, axis=axis), tile], axis)


def ahead(values, axis):
    size = values.shape[axis]
    return without_edge(pltpu.roll(values, size - 1, axis), axis, size - 1)


def behind(values, axis):
    return without_edge(pltpu.roll(values, 1, axis), axis, 0)


def plane_sum(plane):
    return ahead(plane, 0) + behind(plane, 0) + ahead(plane, 1) + behind(plane, 1)


def difference(plane, axis):
    return ahead(plane, axis) - behind(plane, axis)


def halves(ref, start):
    return jnp.concatenate([ref[start : start + 64, :], ref[start + 64 : start + 128, :]], axis=1)


def put_halves(ref, start, plane):
    ref[start : start + 64, :] = plane[:, :128]
    ref[start + 64 : start + 128, :] = plane[:, 128:]


def parts(values, count):
    pieces = []
    for _ in range(count - 1):
        piece = values.astype(BF16)
        pieces.append(piece)
        values = values - piece.astype(F32)
    pieces.append(values.astype(BF16))
    return pieces


def dot(left, right, transposed=False):
    dims = (((1,), (1 if transposed else 0,)), ((), ()))
    return lax.dot_general(left, right, dims, preferred_element_type=F32)


def pieces_of(values, count):
    pieces = []
    for _ in range(count):
        pieces.append(values.astype(BF16).astype(F32))
        values = values - pieces[-1]
    return pieces


def added(product, count):
    rows = product.shape[0] // count
    return sum(product[i * rows : (i + 1) * rows] for i in range(count))


def split_dot(left, right, count, transposed=False):
    rows = left.shape[0]
    product = dot(jnp.concatenate(parts(left, count), 0), right, transposed)
    return sum(product[i * rows : (i + 1) * rows] for i in range(count))


def fluid_kernel(
    velocity_in, displacement_in, to_mate, to_other, own_left, own_right, source, wall,
    velocity, displacement, arrived,
):
    copies = [pltpu.make_async_copy(velocity_in, velocity, arrived.at[0, 0])]
    copies.append(pltpu.make_async_copy(displacement_in, displacement, arrived.at[3, 0]))
    for copy in copies:
        copy.start()
    for copy in copies:
        copy.wait()
    even = even_device()
    layers = velocity.shape[1]
    last = layers - 1
    field = [[velocity[c, x] for x in range(layers)] for c in range(3)]
    own = [[(1.0 - 6.0 * NU) * f + NU * plane_sum(f) for f in rows] for rows in field]
    spread = {
        x: NU * (difference(field[1][x], 0) + difference(field[2][x], 1)) for x in (0, last)
    }
    lefts = (own[0][0] + NU * field[0][1] + spread[0], NU * field[0][0])
    rights = (spread[last] - own[0][last] - NU * field[0][last - 1], NU * field[0][last])
    own_left[...] = lefts[1]
    own_right[...] = rights[1]
    edges = [
        (MU * NU) * (velocity[2, x, 1:2, :] - velocity[2, x, 0:1, :]) for x in (0, last)
    ]
    for ref, first, second in ((to_mate, rights, lefts), (to_other, lefts, rights)):
        put_halves(ref, 0, jnp.where(even, first[0], second[0]))
        put_halves(ref, H2_AT, jnp.where(even, first[1], second[1]))
        ref[ROW_AT : DISP_AT, :] = jnp.zeros((8, 128), F32)
        ref[ROW_AT + 2 : ROW_AT + 3, :] = jnp.ones((1, 128), F32)
        edge = jnp.where(even, edges[int(first is rights)], edges[int(second is rights)])
        ref[ROW_AT : ROW_AT + 1, :] = edge[:, :128]
        ref[ROW_AT + 1 : ROW_AT + 2, :] = edge[:, 128:]
        for c in range(3):
            rows = (displacement[c, 0:1, :], displacement[c, 7:8, :])
            row = jnp.where(even, rows[int(first is rights)], rows[int(second is rights)])
            for k in range(8):
                place = DISP_AT + c * 8 + k
                ref[place : place + 1, :] = row[:, k * 128 : k * 128 + 128]
    zero = jnp.zeros_like(field[0][0])
    predicted = [
        [
            own[c][x]
            + NU
            * (
                (field[c][x + 1] if x < last else zero)
                + (field[c][x - 1] if x > 0 else zero)
            )
            for x in range(layers)
        ]
        for c in range(3)
    ]
    for x in range(layers):
        after = predicted[0][x + 1] if x < last else zero
        before = predicted[0][x - 1] if x > 0 else zero
        source[x] = -0.5 * (
            after - before + difference(predicted[1][x], 0) + difference(predicted[2][x], 1)
        )
        wall[x : x + 1, :] = MU * (predicted[0][x][1:2, :] - predicted[0][x][0:1, :])
        wall[4 + x : 5 + x, :] = MU * (predicted[2][x][1:2, :] - predicted[2][x][0:1, :])


def shell_beside(field):
    rows = field.shape[0]
    beside = pltpu.roll(field, rows - 1, 0) + pltpu.roll(field, 1, 0)
    return beside + ahead(field, 1) + behind(field, 1)


def source_kernel(
    source, wall, own_left, own_right, halo, displacement, load, stiffness,
    fields, first, shell, wall_out,
):
    from_left, from_right = halo()
    layers = source.shape[0]
    last = layers - 1
    left1, left2 = halves(from_left, 0), halves(from_left, H2_AT)
    right1, right2 = halves(from_right, 0), halves(from_right, H2_AT)
    has_left = from_left[ROW_AT + 2 : ROW_AT + 3, 0:1]
    has_right = from_right[ROW_AT + 2 : ROW_AT + 3, 0:1]
    left1 = left1 - has_left * own_left[...]
    right1 = right1 + has_right * own_right[...]
    for x in range(layers):
        plane = source[x]
        if x == 0:
            plane = plane - 0.5 * left1
        if x == 1:
            plane = plane + 0.5 * left2
        if x == last - 1:
            plane = plane - 0.5 * right2
        if x == last:
            plane = plane - 0.5 * right1
        put_halves(fields, x * 128, plane)
        if x == 0:
            put_halves(first, 0, plane)
    wall_out[...] = wall[...]
    for x, ref, plane in ((0, from_left, left2), (last, from_right, right2)):
        edge = jnp.concatenate([ref[ROW_AT : ROW_AT + 1, :], ref[ROW_AT + 1 : ROW_AT + 2, :]], 1)
        wall_out[x : x + 1, :] = wall[x : x + 1, :] + MU * (plane[1:2, :] - plane[0:1, :])
        wall_out[4 + x : 5 + x, :] = wall[4 + x : 5 + x, :] + edge
    for c in range(3):
        field = displacement[c]
        above = jnp.concatenate(
            [from_left[DISP_AT + c * 8 + k : DISP_AT + c * 8 + k + 1, :] for k in range(8)], 1
        )
        below = jnp.concatenate(
            [from_right[DISP_AT + c * 8 + k : DISP_AT + c * 8 + k + 1, :] for k in range(8)], 1
        )
        row = at(field, 0)
        beside = jnp.where(row == 0, above, pltpu.roll(field, 1, 0))
        beside = beside + jnp.where(row == 7, below, pltpu.roll(field, 7, 0))
        beside = beside + ahead(field, 1) + behind(field, 1)
        start = load[c] - ((4.0 + stiffness[...]) * field - beside)
        for k in range(8):
            place = (c * 8 + k) * 8
            shell[place : place + 8, :] = start[:, k * 128 : k * 128 + 128]
    for k in range(8):
        place = STIFF_AT + k * 8
        shell[place : place + 8, :] = stiffness[:, k * 128 : k * 128 + 128]


def slots_kernel(owner, slots, *, ranks):
    width = owner.shape[1]
    down = lax.broadcasted_iota(jnp.int32, (width, width), 0)
    across = lax.broadcasted_iota(jnp.int32, (width, width), 1)
    earlier = jnp.where(down < across, 1.0, 0.0).astype(BF16)
    rank = lax.broadcasted_iota(jnp.int32, (ranks, width), 0)
    seen = jnp.zeros((ranks, 1), F32)
    for x in range(owner.shape[0]):
        member = jnp.where(rank == owner[x : x + 1, :], 1.0, 0.0)
        before = dot(member.astype(BF16), earlier) + seen
        slots[x : x + 1, :] = jnp.sum(before * member, 0, keepdims=True).astype(jnp.int32)
        seen = seen + jnp.sum(member, 1, keepdims=True)


def fold(product):
    rows, columns = product.shape
    tall = product[0:8]
    for a in range(1, rows // 8):
        tall = tall + product[a * 8 : a * 8 + 8]
    total = tall[:, :128]
    for b in range(1, columns // 128):
        total = total + tall[:, b * 128 : b * 128 + 128]
    return total


def whole(tile):
    return jnp.sum(jnp.sum(tile, 0, keepdims=True), 1, keepdims=True)


def place_pair(tile, i, j, value):
    row, lane = at(tile, 0), at(tile, 1)
    here = (row == i) & (lane == j[0])
    if j[1] is not None:
        here = here | ((row == j[1]) & (lane == j[2]))
    return jnp.where(here, value, tile)


def pressure_kernel(
    own, mate, other, beyond, shift, shift_mate, shift_other,
    wall, owner, slots, node, weight,
    payload, basis, work, sent, *, ranks,
):
    left, right = sides(mate, other)
    shift_left, shift_right = sides(shift_mate, shift_other)
    layers = shift.shape[0]
    for x in range(layers):
        work[0, x] = halves(left, x * 128)
        work[0, x + 4] = halves(own, x * 128)
        work[0, x + 8] = halves(right, x * 128)
    work[0, 12] = halves(beyond, 0)
    inside = [jnp.where(side[3 * end][0:1, 0:1] > 0.0, 1.0, 0.0) for side, end in ((shift_left, 1), (shift_right, 0))]
    copies = [
        pltpu.make_async_copy(work.at[k, pl.ds(4, layers)], basis.at[k], sent.at[k])
        for k in range(PITERS)
    ]
    copies[0].start()
    for step in range(1, PITERS):
        for x in range(step, 13 - step):
            now = work[step - 1, x]
            beside = work[step - 1, x - 1] + work[step - 1, x + 1] + plane_sum(now)
            if x < 4 or x >= 8:
                beside = inside[x // 8] * beside
            diagonal = (shift_left, shift, shift_right)[x // 4][x % 4] + (6.0 - P_SHIFT[step - 1])
            value = diagonal * now - beside
            if step > 1:
                value = value - P_BACK[step - 2] * work[step - 2, x]
            work[step, x] = value
        copies[step].start()
    tile = jnp.zeros((8, 128), F32)
    pairs = [(i, j) for i in range(PITERS) for j in range(i, PITERS)]
    totals = [0.0] * len(pairs)
    for x in range(4, 8):
        for y in range(0, 64, 8):
            for z in (0, 128):
                tiles = [work[k, x, y : y + 8, z : z + 128] for k in range(PITERS)]
                totals = [total + tiles[i] * tiles[j] for total, (i, j) in zip(totals, pairs)]
    for total, (i, j) in zip(totals, pairs):
        tile = place_pair(tile, 3 + i, (96 + j, 3 + j, 96 + i), whole(total))
    top = PITERS - 1
    total = 0.0
    for x in range(4, 8):
        now = work[top, x]
        image = (6.0 + shift[x - 4]) * now - plane_sum(now) - 2.0 * work[top, x + 1]
        total = total + now * image
    tile = place_pair(tile, 3 + top, (96 + PITERS, None, None), whole(fold(total)))
    lanes = lax.broadcasted_iota(jnp.int32, (128, 256), 0)
    field_row = lax.broadcasted_iota(jnp.int32, (8, 256), 0)
    packed = jnp.zeros((ranks * 8, 128), F32)
    weights = jnp.zeros((ranks * 8, 128), F32)
    for x in range(layers):
        scale = weight[x : x + 1, :].astype(F32)
        rows = [wall[x : x + 1, :] * scale, wall[4 + x : 5 + x, :] * scale]
        rows.append(node[x : x + 1, :].astype(F32))
        rows += [work[k, x + 4][0:1, :] * scale for k in range(PITERS)]
        values = jnp.concatenate(rows, 0)
        who = owner[x : x + 1, :]
        here = jnp.where((lanes & 31) == slots[x : x + 1, :], 1.0, 0.0)
        place = jnp.where(lanes < 96, here, 0.0).astype(BF16)
        end = jnp.where(lanes >= 96, here, 0.0).astype(BF16)
        left_rows = jnp.concatenate(
            [jnp.where(who == d, piece, 0.0) for piece in pieces_of(values, 3) for d in range(ranks)], 0
        )
        packed = packed + added(dot(left_rows.astype(BF16), place, True), 3)
        weight_rows = jnp.concatenate(
            [
                jnp.where((who == d - 1 + field_row) & (field_row < 3), scale, 0.0)
                for d in range(ranks)
            ],
            0,
        )
        weights = weights + dot(weight_rows.astype(BF16), end, True)
    lane = lax.broadcasted_iota(jnp.int32, (8, 128), 1)
    zero = jnp.zeros((8, 128), F32)
    for d in range(ranks):
        mine = packed[d * 8 : d * 8 + 8]
        before = packed[d * 8 - 8 : d * 8] if d > 0 else zero
        after = packed[d * 8 + 8 : d * 8 + 16] if d < ranks - 1 else zero
        block = jnp.where(lane < 32, before, jnp.where(lane < 64, mine, after))
        block = jnp.where(lane < 96, block, 0.0) + weights[d * 8 : d * 8 + 8]
        payload[d] = block + tile
    for copy in copies:
        copy.wait()


def second_spot(i, j):
    if i < SITERS:
        return 6 + i % 4, 96 + 16 * (i // 4) + j
    return 10 + (i - SITERS) // 4, 96 + 8 * ((i - SITERS) % 4) + j - SITERS


ENERGY_AT = (11, 112)


def place_second(tile, i, j, value):
    row, lane = second_spot(i, j)
    if i < SITERS <= j:
        return place_pair(tile, row, (lane, None, None), value)
    return place_pair(tile, row, (lane, *second_spot(j, i)), value)


def second_gram(summed):
    row, lane = at(summed, 0), at(summed, 1)
    first = pltpu.roll(pltpu.roll(summed, 32, 1), 10, 0)
    second = pltpu.roll(pltpu.roll(summed, 16, 1), 14, 0)
    gram = jnp.where(row < 4, first, second)
    gram = jnp.where((row < SITERS) & (lane < 16), gram, 0.0)
    for k in range(5):
        source, start = second_spot(SITERS + k, SITERS)
        moved = pltpu.roll(summed, (SITERS - start) % 128, 1)[source : source + 1]
        here = (row == SITERS + k) & (lane >= SITERS) & (lane < SITERS + 5)
        gram = jnp.where(here, jnp.broadcast_to(moved, gram.shape), gram)
    return gram


def row_of(matrix, k):
    return jnp.sum(jnp.where(at(matrix, 0) == k, matrix, 0.0), 0, keepdims=True)


def column_of(matrix, k):
    return jnp.sum(jnp.where(at(matrix, 1) == k, matrix, 0.0), 1, keepdims=True)


def eliminate(columns, right, first):
    row = at(right, 0)
    lengths = [TINY * column[first + k : first + k + 1] for k, column in enumerate(columns)]
    for k in range(len(columns)):
        column = columns[k]
        here = first + k
        pivot = column[here : here + 1]
        good = pivot > lengths[k]
        inverse = jnp.where(good, 1.0 / jnp.where(good, pivot, 1.0), 0.0)
        factor = column * inverse

        def reduced(values):
            mine = values[here : here + 1]
            return jnp.where(row == here, mine * inverse, values - factor * mine)

        columns = columns[: k + 1] + [reduced(values) for values in columns[k + 1 :]]
        right = reduced(right)
    return right


def galerkin(gram, first, shifts, back, energy):
    count = len(shifts)
    images = []
    for k in range(count - 1):
        image = shifts[k] * gram[k] + gram[k + 1]
        if k > 0:
            image = image + back[k - 1] * gram[k - 1]
        images.append(image)
    last = jnp.broadcast_to(gram[count - 1], (gram[0].shape[0], 128))
    row = at(last, 0)
    shift, prior = 0.0, 0.0
    for k in range(count):
        shift = jnp.where(row == first + k, shifts[k], shift)
    for k in range(1, count):
        prior = jnp.where(row == first + k, back[k - 1], prior)
    size = last.shape[0]
    image = shift * last + pltpu.roll(last, size - 1, 0) + prior * pltpu.roll(last, 1, 0)
    image = jnp.where(row == first + count - 1, energy, image)
    images.append(image[:, 0:1])
    return images


def picked_nodes(node):
    column = lax.broadcasted_iota(jnp.int32, (1024, node.shape[1]), 0)
    return jnp.where(column == (node & 1023), 1.0, 0.0).astype(BF16)


def nodes_values(fields, table, pick, line):
    for c in range(3):
        for f in range(8):
            value = fields[f](c) if f < len(fields) else jnp.zeros((8, 1024), F32)
            for k in range(8):
                table[k, pl.ds(c * 8 + f, 8, stride=24), :] = value[:, k * 128 : k * 128 + 128]
    found = split_dot(jnp.concatenate([table[k] for k in range(8)], 1), pick, 2)
    values = found[0:24]
    for r in range(1, 8):
        values = jnp.where(line == r, found[r * 24 : r * 24 + 24], values)
    return values


def force_kernel(
    received, displacement, solved_prev, solved_history,
    forces, requests, fixed, factors, table, *, ranks,
):
    lane8 = lax.broadcasted_iota(jnp.int32, (8, 128), 1)
    summed = received[0]
    for p in range(1, ranks):
        summed = summed + received[p]
    gram = [column_of(summed, 96 + k) for k in range(PITERS + 1)]
    system = galerkin(gram[:PITERS], 3, P_SHIFT, P_BACK, gram[PITERS][7:8])
    solved = eliminate(system, gram[0], 3)
    solved = jnp.where(lax.broadcasted_iota(jnp.int32, (8, 1), 0) >= 3, solved, 0.0)
    factors[...] = jnp.broadcast_to(solved, (8, 128))
    groups = [lane8 // 32 == q for q in range(4)]

    def gathered(j):
        chunks = []
        for k in range(ranks // 4):
            chunk = jnp.zeros((8, 128), F32)
            for q in range(4):
                chunk = jnp.where(
                    groups[q], pltpu.roll(received[4 * k + q], (32 * (q - j)) % 128, 1), chunk
                )
            chunks.append(chunk)
        return jnp.concatenate(chunks, 1)

    weights = gathered(3)
    entries = ranks * CAP
    target = lax.broadcasted_iota(jnp.int32, (64, entries), 0)
    low = lax.broadcasted_iota(jnp.int32, (128, entries), 0)
    node = None
    for j in range(3):
        values = gathered(j)
        numbers = values[2:3, :].astype(jnp.int32)
        if j == 1:
            node = numbers
        rows = (
            values[0:1, :],
            WALL * jnp.sum(values * solved, 0, keepdims=True),
            values[1:2, :],
        )
        code = ((numbers >> 7) & 7) * 8 + (numbers >> 10)
        spot = jnp.where(low == (numbers & 127), 1.0, 0.0).astype(BF16)
        match = target == code
        pieces = pieces_of(jnp.concatenate(rows, 0), 2)
        left_rows = jnp.concatenate(
            [jnp.where(match, piece[c : c + 1], 0.0) for piece in pieces for c in range(3)], 0
        )
        scattered = added(dot(left_rows.astype(BF16), spot, True), 2)
        share = dot(jnp.where(match, weights[j : j + 1, :], 0.0).astype(BF16), spot, True)
        share = 1.0 / jnp.maximum(share, 1.0)
        for c in range(3):
            force = scattered[c * 64 : c * 64 + 64] * share
            for k in range(8):
                forces[c, j * 8 : j * 8 + 8, k * 128 : k * 128 + 128] = force[k * 8 : k * 8 + 8]
    requests[...] = jnp.broadcast_to(node, (8, entries))
    pick = picked_nodes(node)
    fields = [lambda c: displacement[c]]
    fields += [lambda c, k=k: solved_history[k, c] for k in range(solved_history.shape[0])]
    fields.append(lambda c: solved_prev[c])
    fixed[...] = nodes_values(fields, table, pick, node >> 10)


def shell_kernel(
    forces, requests, fixed, own, mate, other, residual_prev, residual_history,
    payload, basis, work, diagonal, table, sent, *, ranks,
):
    left, right = sides(mate, other)
    inside = []
    for j, ref in enumerate((left, own, right)):
        stiff = []
        for k in range(8):
            columns = slice(k * 128, k * 128 + 128)
            stiff.append(ref[STIFF_AT + k * 8 : STIFF_AT + k * 8 + 8, :])
            for c in range(3):
                place = (c * 8 + k) * 8
                here = slice(j * 8, j * 8 + 8)
                work[0, c, here, columns] = forces[c, here, columns] + ref[place : place + 8, :]
        stiff = jnp.concatenate(stiff, 1)
        if j == 1:
            stiffness = stiff
        for c in range(3):
            diagonal[c * 24 + j * 8 : c * 24 + j * 8 + 8, :] = stiff
        inside.append(jnp.where(stiff[:, 0:1] > 0.0, 1.0, 0.0))
    inside = jnp.concatenate(inside * 3, 0)
    copies = [
        pltpu.make_async_copy(work.at[k, :, pl.ds(8, 8)], basis.at[k], sent.at[k])
        for k in range(SITERS)
    ]
    for step in range(1, SITERS):
        now = work[step - 1].reshape(72, 1024)
        value = (diagonal[...] + (4.0 - S_SHIFT[step - 1])) * now - inside * shell_beside(now)
        if step > 1:
            value = value - S_BACK[step - 2] * work[step - 2].reshape(72, 1024)
        work[step] = value.reshape(3, 24, 1024)
        copies[step - 1].start()
    copies[-1].start()
    def basis_tile(k, c, columns=slice(None)):
        return work[k, c, 8:16, columns]

    def tile_of(ref):
        return lambda c, columns=slice(None): ref[c, :, columns]

    vectors = [lambda c, columns=slice(None), k=k: basis_tile(k, c, columns) for k in range(SITERS)]
    vectors.append(tile_of(residual_prev))
    vectors += [tile_of(residual_history.at[k]) for k in range(residual_history.shape[0])]
    tile = jnp.zeros((16, 128), F32)
    pairs = [(i, j) for i in range(len(vectors)) for j in range(i, len(vectors))]
    for some in (pairs[:46], pairs[46:]):
        totals = [0.0] * len(some)
        used = sorted({v for pair in some for v in pair})
        for c in range(3):
            for k in range(8):
                tiles = {v: vectors[v](c, slice(k * 128, k * 128 + 128)) for v in used}
                totals = [total + tiles[i] * tiles[j] for total, (i, j) in zip(totals, some)]
        for total, (i, j) in zip(totals, some):
            tile = place_second(tile, i, j, whole(total))
    top = SITERS - 1
    total = 0.0
    for c in range(3):
        now = basis_tile(top, c)
        after = work[top, c, 9:17, :]
        image = (4.0 + stiffness) * now - ahead(now, 1) - behind(now, 1) - 2.0 * after
        total = total + now * image
    tile = place_pair(tile, ENERGY_AT[0], (ENERGY_AT[1], None, None), whole(fold(total)))
    node = requests[0:1, :]
    entries = node.shape[1]
    found = nodes_values(
        [lambda c, k=k: basis_tile(k, c) for k in range(SITERS)], table, picked_nodes(node), node >> 10
    )
    answer = [values[c * 8 : c * 8 + 8] for c in range(3) for values in (found, fixed)]
    answer = jnp.concatenate(answer, 0)
    lane16 = lax.broadcasted_iota(jnp.int32, (16, 128), 1)
    row16 = lax.broadcasted_iota(jnp.int32, (16, 128), 0)
    extra = jnp.concatenate(
        [answer[c * 16 + 12 : c * 16 + 14] for c in range(3)] + [jnp.zeros((10, entries), F32)], 0
    )
    for p in range(ranks):
        columns = slice(p // 4 * 128, p // 4 * 128 + 128)
        block = jnp.where(row16 < 6, pltpu.roll(extra[:, columns], (32 * (3 - p % 4)) % 128, 1), tile)
        for c in range(3):
            piece = answer[c * 16 : c * 16 + 16, columns]
            block = jnp.where(
                lane16 // 32 == c, pltpu.roll(piece, (32 * (c - p % 4)) % 128, 1), block
            )
        for t in range(3):
            payload[p, t] = block[t * 4 : t * 4 + 4]
    for copy in copies:
        copy.wait()


def combine_kernel(basis, factors, pressure):
    basis = basis()
    for x in range(pressure.shape[0]):
        total = 0.0
        for k in range(PITERS):
            total = total + factors[3 + k : 4 + k, 0:1] * basis[k, x]
        pressure[x] = total


def update_kernel(
    received, basis, displacement, solved_prev, solved_history, owner, slots,
    new_displacement, wall, *, ranks,
):
    blocks = [
        jnp.concatenate([received[p, t] for t in range(3)] + [jnp.zeros((4, 128), F32)], 0)
        for p in range(ranks)
    ]
    summed = sum(blocks)
    matrix = second_gram(summed)
    gram = [column_of(matrix, k) for k in range(SITERS + 5)]
    energy = summed[ENERGY_AT[0] : ENERGY_AT[0] + 1, ENERGY_AT[1] : ENERGY_AT[1] + 1]
    system = galerkin(gram[:SITERS], 0, S_SHIFT, S_BACK, energy)
    steps = eliminate(system, gram[0], 0)
    down = lax.broadcasted_iota(jnp.int32, (16, 1), 0)
    steps = jnp.where(down < SITERS, steps, 0.0)
    base, count = SITERS, 1 + solved_history.shape[0]
    with_moved = jnp.sum(matrix * steps, 0, keepdims=True)
    diagonal = at(matrix, 0) == at(matrix, 1)
    with_moved = jnp.sum(
        jnp.where(diagonal, jnp.broadcast_to(with_moved, matrix.shape), 0.0), 1, keepdims=True
    )
    with_newest = with_moved - gram[base]
    newest_moved = jnp.sum(steps * with_newest, 0, keepdims=True)
    newest_newest = newest_moved - with_newest[base : base + 1]
    columns = [jnp.where(down == base, newest_newest, with_newest)]
    for k in range(1, count):
        columns.append(jnp.where(down == base, with_newest[base + k : base + k + 1], gram[base + k]))
    right = jnp.where(down == base, newest_moved, with_moved)
    coefficients = -eliminate(columns, right, base)
    newest = row_of(coefficients, base)
    factors = jnp.where(
        down < base,
        (1.0 + newest) * steps,
        jnp.where(
            down == base,
            1.0 + newest,
            jnp.where(down < base + count, coefficients, jnp.where(down == base + count, -newest, 0.0)),
        ),
    )
    for c in range(3):
        total = row_of(factors, base) * displacement[c]
        for k in range(SITERS):
            total = total + row_of(factors, k) * basis[k, c]
        for k in range(count - 1):
            total = total + row_of(factors, base + 1 + k) * solved_history[k, c]
        total = total + row_of(factors, base + count) * solved_prev[c]
        new_displacement[c] = total
    row, group = at(summed, 0), at(summed, 1) // 32
    spare = jnp.where(row % 2 == 0, factors[12:13], factors[13:14])
    stacked = []
    for c in range(3):
        scales = jnp.where(group == c, factors, jnp.where((group == 3) & (row // 2 == c), spare, 0.0))
        stacked += [jnp.sum(block * scales, 0, keepdims=True) for block in blocks]
    stacked = jnp.concatenate(stacked, 0)
    slot_row = lax.broadcasted_iota(jnp.int32, (128, 256), 0) & 31
    rank = lax.broadcasted_iota(jnp.int32, (ranks, 256), 0)
    for x in range(owner.shape[0]):
        pick = jnp.where(slot_row == slots[x : x + 1, :], 1.0, 0.0).astype(BF16)
        spread = split_dot(stacked, pick, 3)
        mine = rank == owner[x : x + 1, :]
        for c in range(3):
            wall[c : c + 1, x * 256 : x * 256 + 256] = jnp.sum(
                jnp.where(mine, spread[c * ranks : (c + 1) * ranks], 0.0), 0, keepdims=True
            )


def on_device(
    velocity,
    pressure_shift,
    owner_rank,
    node_index,
    map_weight,
    shell_load,
    shell_stiffness,
    displacement,
    residual_prev,
    solved_prev,
    residual_history,
    solved_history,
):
    ranks = lax.axis_size("slab")
    layers = velocity.shape[1]
    kept = residual_history.shape[0]

    def with_mate(values):
        return lax.ppermute(values, "slab", [(i, i ^ 1) for i in range(ranks)])

    def with_other(values):
        pairs = [(i, i + 1) for i in range(1, ranks - 1, 2)]
        return lax.ppermute(values, "slab", pairs + [(j, i) for i, j in pairs])

    owner = owner_rank.reshape(layers, -1)
    node = node_index.reshape(layers, -1)
    weight = map_weight.reshape(layers, -1)
    plane = shape(*velocity.shape[2:])

    to_mate, to_other, own_left, own_right, source, wall = call(
        fluid_kernel,
        (
            shape(HALO_ROWS, 128), shape(HALO_ROWS, 128), plane, plane,
            shape(*velocity.shape[1:]), shape(8, 256),
        ),
        (velocity, displacement),
        outer=(0, 1),
        stored=(0, 1),
        scratch=(
            pltpu.VMEM(velocity.shape, F32),
            pltpu.VMEM(displacement.shape, F32),
            pltpu.SemaphoreType.DMA((4, max(layers, 1))),
        ),
    )
    halo_other, halo_mate = with_other(to_other), with_mate(to_mate)
    shift_other, shift_mate = with_other(pressure_shift), with_mate(pressure_shift)
    (slots,) = call(
        lambda *refs: slots_kernel(*refs[:2], ranks=ranks),
        (shape(layers, 256, dtype=jnp.int32),),
        (owner,),
    )
    fields, first, shell, wall = call(
        lambda *refs: source_kernel(*refs),
        (shape(FIELD_ROWS, 128), shape(128, 128), shape(SHELL_ROWS, 128), shape(8, 256)),
        (
            source, wall, own_left, own_right, halo_mate, halo_other,
            displacement, shell_load, shell_stiffness,
        ),
        pairs=(4,),
    )
    beyond = lax.ppermute(first, "slab", [(i, i - 2) for i in range(2, ranks)])
    fields_other, fields_mate = with_other(fields), with_mate(fields)
    shell_other, shell_mate = with_other(shell), with_mate(shell)
    payload, pressure_basis = call(
        lambda *refs: pressure_kernel(*refs, ranks=ranks),
        (shape(ranks, 8, 128), pltpu.HBM((PITERS, *pressure_shift.shape), F32)),
        (
            fields, fields_mate, fields_other, beyond, pressure_shift, shift_mate, shift_other,
            wall, owner, slots, node, weight,
        ),
        direct=(1,),
        scratch=(
            pltpu.VMEM((PITERS, 13, 64, 256), F32),
            pltpu.SemaphoreType.DMA((PITERS,)),
        ),
    )
    received = lax.all_to_all(payload, "slab", split_axis=0, concat_axis=0, tiled=True)
    entries = ranks * CAP
    forces, requests, fixed, factors = call(
        lambda *refs: force_kernel(*refs, ranks=ranks),
        (
            shape(3, 3 * displacement.shape[1], displacement.shape[2]),
            shape(8, entries, dtype=jnp.int32), shape(24, entries), shape(8, 128),
        ),
        (received, displacement, solved_prev, solved_history),
        scratch=(pltpu.VMEM((8, 8 * 24, 128), F32),),
    )
    payload, shell_basis = call(
        lambda *refs: shell_kernel(*refs, ranks=ranks),
        (shape(ranks, 3, 4, 128), pltpu.HBM((SITERS, *displacement.shape), F32)),
        (
            forces, requests, fixed, shell, shell_mate, shell_other, residual_prev, residual_history,
        ),
        direct=(1,),
        scratch=(
            pltpu.VMEM((SITERS, 3, 24, 1024), F32),
            pltpu.VMEM((72, 1024), F32),
            pltpu.VMEM((8, 8 * 24, 128), F32),
            pltpu.SemaphoreType.DMA((SITERS,)),
        ),
    )
    answers = lax.all_to_all(payload, "slab", split_axis=0, concat_axis=0, tiled=True)
    (pressure,) = call(
        combine_kernel,
        (shape(*pressure_shift.shape),),
        (pressure_basis, factors),
        late=(0,),
        stored=(0,),
    )
    new_displacement, wall_displacement = call(
        lambda *refs: update_kernel(*refs, ranks=ranks),
        (shape(*displacement.shape), shape(3, owner_rank.shape[0])),
        (answers, shell_basis, displacement, solved_prev, solved_history, owner, slots),
    )
    return (pressure, new_displacement, wall_displacement)


def solution(mesh):
    in_specs = (
        P(None, ("groups", "slab"), None, None),
        P(("groups", "slab"), None, None),
        P(("groups", "slab"), None),
        P(("groups", "slab")),
        P(("groups", "slab")),
        P(None, ("groups", "slab"), None),
        P(("groups", "slab"), None),
        P(None, ("groups", "slab"), None),
        P(None, ("groups", "slab"), None),
        P(None, ("groups", "slab"), None),
        P(None, None, ("groups", "slab"), None),
        P(None, None, ("groups", "slab"), None),
    )
    out_specs = (
        P(("groups", "slab"), None, None),
        P(None, ("groups", "slab"), None),
        P(None, ("groups", "slab")),
    )
    return jax.shard_map(
        on_device, mesh=mesh, in_specs=in_specs, out_specs=out_specs, check_vma=False
    )
```

```python
import jax
import jax.numpy as jnp
from jax import lax
from jax.experimental import pallas as pl
from jax.experimental.pallas import tpu as pltpu
from jax.sharding import PartitionSpec as P

CAP = 32
PITERS = 5
SITERS = 8

NU = 0.15
MU = 0.5
WALL = 4.0

P_SHIFT, P_BACK = (4.93, 7.29, 5.13, 7.05, 5.38), (10.17, 6.01, 8.86, 8.24)
S_SHIFT = (5.7, 5.09, 4.26, 4.26, 4.08, 4.17, 4.1, 4.18)
S_BACK = (2.53, 3.17, 4.07, 3.95, 4.22, 4.01, 4.14)
TINY = 1e-7

VMEM = pl.BlockSpec(memory_space=pltpu.VMEM)
F32 = jnp.float32
BF16 = jnp.bfloat16

H2_AT, ROW_AT, DISP_AT, HALO_ROWS = 128, 256, 264, 288
FIELD_ROWS, STIFF_AT, SHELL_ROWS = 512, 192, 256


def even_device():
    return lax.rem(lax.axis_index("slab"), 2) == 0


class Late:
    def __init__(self, source, place, semaphore):
        self.place = place
        self.copy = pltpu.make_async_copy(source, place, semaphore)
        self.copy.start()
        self.pending = True

    def __call__(self):
        if self.pending:
            self.copy.wait()
            self.pending = False
        return self.place


class Sides:
    def __init__(self, to_mate, to_other, left, right, semaphores):
        even = even_device()
        self.copies = [
            pltpu.make_async_copy(to_mate, left, semaphores.at[0]),
            pltpu.make_async_copy(to_other, right, semaphores.at[1]),
        ]
        self.places = (left, right)

        @pl.when(even)
        def _():
            pltpu.make_async_copy(to_other, left, semaphores.at[0]).start()
            pltpu.make_async_copy(to_mate, right, semaphores.at[1]).start()

        @pl.when(jnp.logical_not(even))
        def _():
            for copy in self.copies:
                copy.start()

        self.pending = True

    def __call__(self):
        if self.pending:
            for copy in self.copies:
                copy.wait()
            self.pending = False
        return self.places


class Either:
    def __init__(self, which, first, second):
        self.which, self.first, self.second = which, first, second

    def __getitem__(self, index):
        return jnp.where(self.which, self.first[index], self.second[index])


def sides(to_mate, to_other):
    even = even_device()
    return Either(even, to_other, to_mate), Either(even, to_mate, to_other)


def call(
    kernel, outs, args, late=(), outer=(), pairs=(), direct=(), stored=(), scratch=(),
    flops=1000000000, limit=48.0,
):
    count, made = len(args), len(outs)

    def body(*refs):
        operands = list(refs[:count])
        at_end = count + made + len(scratch)
        places = iter(refs[at_end:-1])
        wanted = []
        used = 0
        for i in late:
            operands[i] = Late(operands[i], next(places), refs[-1].at[used])
            wanted.append(operands[i])
            used += 1
        for i in pairs:
            operands[i] = Sides(
                operands[i], operands[i + 1], next(places), next(places), refs[-1].at[pl.ds(used, 2)]
            )
            wanted.append(operands[i])
            used += 2
        operands = [value for i, value in enumerate(operands) if i - 1 not in pairs]
        kernel(*operands, *refs[count:at_end])
        for value in wanted:
            value()

    outside = [i for i in late] + [i + k for i in pairs for k in (0, 1)]
    extra = [pltpu.VMEM(args[i].shape, args[i].dtype) for i in outside]
    extra.append(pltpu.SemaphoreType.DMA((max(1, len(outside)),)))
    args = [
        pltpu.with_memory_space_constraint(value, pltpu.HBM) if i in stored else value
        for i, value in enumerate(args)
    ]
    any_space = pl.BlockSpec(memory_space=pl.ANY)
    return pl.pallas_call(
        body,
        out_shape=outs,
        in_specs=[any_space if i in outside or i in outer else VMEM for i in range(count)],
        out_specs=tuple(any_space if i in direct else VMEM for i in range(made)),
        scratch_shapes=list(scratch) + extra,
        compiler_params=pltpu.CompilerParams(vmem_limit_bytes=int(limit * 1024 * 1024)),
        cost_estimate=pl.CostEstimate(flops=flops, bytes_accessed=0, transcendentals=0),
    )(*args)


def shape(*dims, dtype=F32):
    return jax.ShapeDtypeStruct(dims, dtype)


def at(values, axis):
    return lax.broadcasted_iota(jnp.int32, values.shape, axis)


def without_edge(values, axis, index):
    width = (8, 128)[axis]
    size = values.shape[axis]
    edge = 0 if index == 0 else size - width
    tile = lax.slice_in_dim(values, edge, edge + width, axis=axis)
    tile = jnp.where(at(tile, axis) == index - edge, 0.0, tile)
    if index == 0:
        rest = lax.slice_in_dim(values, width, size, axis=axis)
        return jnp.concatenate([tile, rest], axis)
    return jnp.concatenate([lax.slice_in_dim(values, 0, edge, axis=axis), tile], axis)


def ahead(values, axis):
    size = values.shape[axis]
    return without_edge(pltpu.roll(values, size - 1, axis), axis, size - 1)


def behind(values, axis):
    return without_edge(pltpu.roll(values, 1, axis), axis, 0)


def plane_sum(plane):
    return ahead(plane, 0) + behind(plane, 0) + ahead(plane, 1) + behind(plane, 1)


def difference(plane, axis):
    return ahead(plane, axis) - behind(plane, axis)


def halves(ref, start):
    return jnp.concatenate([ref[start : start + 64, :], ref[start + 64 : start + 128, :]], axis=1)


def put_halves(ref, start, plane):
    ref[start : start + 64, :] = plane[:, :128]
    ref[start + 64 : start + 128, :] = plane[:, 128:]


def parts(values, count):
    pieces = []
    for _ in range(count - 1):
        piece = values.astype(BF16)
        pieces.append(piece)
        values = values - piece.astype(F32)
    pieces.append(values.astype(BF16))
    return pieces


def dot(left, right, transposed=False):
    dims = (((1,), (1 if transposed else 0,)), ((), ()))
    return lax.dot_general(left, right, dims, preferred_element_type=F32)


def pieces_of(values, count):
    pieces = []
    for _ in range(count):
        pieces.append(values.astype(BF16).astype(F32))
        values = values - pieces[-1]
    return pieces


def added(product, count):
    rows = product.shape[0] // count
    return sum(product[i * rows : (i + 1) * rows] for i in range(count))


def split_dot(left, right, count, transposed=False):
    rows = left.shape[0]
    product = dot(jnp.concatenate(parts(left, count), 0), right, transposed)
    return sum(product[i * rows : (i + 1) * rows] for i in range(count))


def plane_part(plane):
    return (1.0 - 6.0 * NU) * plane + NU * plane_sum(plane)


def edge_kernel(
    velocity_in, displacement_in, to_mate, to_other, own_left, own_right,
    velocity, displacement, arrived,
):
    layers = velocity.shape[1]
    last = layers - 1
    copies = [pltpu.make_async_copy(velocity_in.at[0], velocity.at[0], arrived.at[0, 0])]
    for c in (1, 2):
        for x in (0, last):
            copies.append(
                pltpu.make_async_copy(velocity_in.at[c, x], velocity.at[c, x], arrived.at[c, x])
            )
    copies.append(pltpu.make_async_copy(displacement_in, displacement, arrived.at[3, 0]))
    for copy in copies:
        copy.start()
    for copy in copies:
        copy.wait()
    even = even_device()
    spread = {
        x: NU * (difference(velocity[1, x], 0) + difference(velocity[2, x], 1)) for x in (0, last)
    }
    lefts = (plane_part(velocity[0, 0]) + NU * velocity[0, 1] + spread[0], NU * velocity[0, 0])
    rights = (
        spread[last] - plane_part(velocity[0, last]) - NU * velocity[0, last - 1],
        NU * velocity[0, last],
    )
    own_left[...] = lefts[1]
    own_right[...] = rights[1]
    edges = [
        (MU * NU) * (velocity[2, x, 1:2, :] - velocity[2, x, 0:1, :]) for x in (0, last)
    ]
    for ref, first, second in ((to_mate, rights, lefts), (to_other, lefts, rights)):
        put_halves(ref, 0, jnp.where(even, first[0], second[0]))
        put_halves(ref, H2_AT, jnp.where(even, first[1], second[1]))
        ref[ROW_AT : DISP_AT, :] = jnp.zeros((8, 128), F32)
        ref[ROW_AT + 2 : ROW_AT + 3, :] = jnp.ones((1, 128), F32)
        edge = jnp.where(even, edges[int(first is rights)], edges[int(second is rights)])
        ref[ROW_AT : ROW_AT + 1, :] = edge[:, :128]
        ref[ROW_AT + 1 : ROW_AT + 2, :] = edge[:, 128:]
        for c in range(3):
            rows = (displacement[c, 0:1, :], displacement[c, 7:8, :])
            row = jnp.where(even, rows[int(first is rights)], rows[int(second is rights)])
            for k in range(8):
                place = DISP_AT + c * 8 + k
                ref[place : place + 1, :] = row[:, k * 128 : k * 128 + 128]


def fluid_kernel(velocity, source, wall):
    layers = velocity.shape[1]
    last = layers - 1
    field = [[velocity[c, x] for x in range(layers)] for c in range(3)]
    own = [[plane_part(f) for f in rows] for rows in field]
    zero = jnp.zeros_like(field[0][0])
    predicted = [
        [
            own[c][x]
            + NU
            * (
                (field[c][x + 1] if x < last else zero)
                + (field[c][x - 1] if x > 0 else zero)
            )
            for x in range(layers)
        ]
        for c in range(3)
    ]
    for x in range(layers):
        after = predicted[0][x + 1] if x < last else zero
        before = predicted[0][x - 1] if x > 0 else zero
        source[x] = -0.5 * (
            after - before + difference(predicted[1][x], 0) + difference(predicted[2][x], 1)
        )
        wall[x : x + 1, :] = MU * (predicted[0][x][1:2, :] - predicted[0][x][0:1, :])
        wall[4 + x : 5 + x, :] = MU * (predicted[2][x][1:2, :] - predicted[2][x][0:1, :])


def shell_beside(field):
    rows = field.shape[0]
    beside = pltpu.roll(field, rows - 1, 0) + pltpu.roll(field, 1, 0)
    return beside + ahead(field, 1) + behind(field, 1)


def source_kernel(
    source, wall, own_left, own_right, halo, displacement, load, stiffness,
    fields, first, shell, wall_out,
):
    from_left, from_right = halo()
    layers = source.shape[0]
    last = layers - 1
    left1, left2 = halves(from_left, 0), halves(from_left, H2_AT)
    right1, right2 = halves(from_right, 0), halves(from_right, H2_AT)
    has_left = from_left[ROW_AT + 2 : ROW_AT + 3, 0:1]
    has_right = from_right[ROW_AT + 2 : ROW_AT + 3, 0:1]
    left1 = left1 - has_left * own_left[...]
    right1 = right1 + has_right * own_right[...]
    for x in range(layers):
        plane = source[x]
        if x == 0:
            plane = plane - 0.5 * left1
        if x == 1:
            plane = plane + 0.5 * left2
        if x == last - 1:
            plane = plane - 0.5 * right2
        if x == last:
            plane = plane - 0.5 * right1
        put_halves(fields, x * 128, plane)
        if x == 0:
            put_halves(first, 0, plane)
    wall_out[...] = wall[...]
    for x, ref, plane in ((0, from_left, left2), (last, from_right, right2)):
        edge = jnp.concatenate([ref[ROW_AT : ROW_AT + 1, :], ref[ROW_AT + 1 : ROW_AT + 2, :]], 1)
        wall_out[x : x + 1, :] = wall[x : x + 1, :] + MU * (plane[1:2, :] - plane[0:1, :])
        wall_out[4 + x : 5 + x, :] = wall[4 + x : 5 + x, :] + edge
    for c in range(3):
        field = displacement[c]
        above = jnp.concatenate(
            [from_left[DISP_AT + c * 8 + k : DISP_AT + c * 8 + k + 1, :] for k in range(8)], 1
        )
        below = jnp.concatenate(
            [from_right[DISP_AT + c * 8 + k : DISP_AT + c * 8 + k + 1, :] for k in range(8)], 1
        )
        row = at(field, 0)
        beside = jnp.where(row == 0, above, pltpu.roll(field, 1, 0))
        beside = beside + jnp.where(row == 7, below, pltpu.roll(field, 7, 0))
        beside = beside + ahead(field, 1) + behind(field, 1)
        start = load[c] - ((4.0 + stiffness[...]) * field - beside)
        for k in range(8):
            place = (c * 8 + k) * 8
            shell[place : place + 8, :] = start[:, k * 128 : k * 128 + 128]
    for k in range(8):
        place = STIFF_AT + k * 8
        shell[place : place + 8, :] = stiffness[:, k * 128 : k * 128 + 128]


def slots_kernel(owners, slots, owner, *, ranks):
    width = owner.shape[1]
    for x in range(owner.shape[0]):
        owner[x : x + 1, :] = owners[:, x * width : x * width + width]
    down = lax.broadcasted_iota(jnp.int32, (width, width), 0)
    across = lax.broadcasted_iota(jnp.int32, (width, width), 1)
    earlier = jnp.where(down < across, 1.0, 0.0).astype(BF16)
    rank = lax.broadcasted_iota(jnp.int32, (ranks, width), 0)
    seen = jnp.zeros((ranks, 1), F32)
    for x in range(owner.shape[0]):
        member = jnp.where(rank == owner[x : x + 1, :], 1.0, 0.0)
        before = dot(member.astype(BF16), earlier) + seen
        slots[x : x + 1, :] = jnp.sum(before * member, 0, keepdims=True).astype(jnp.int32)
        seen = seen + jnp.sum(member, 1, keepdims=True)


def fold(product):
    rows, columns = product.shape
    tall = product[0:8]
    for a in range(1, rows // 8):
        tall = tall + product[a * 8 : a * 8 + 8]
    total = tall[:, :128]
    for b in range(1, columns // 128):
        total = total + tall[:, b * 128 : b * 128 + 128]
    return total


def whole(tile):
    return jnp.sum(jnp.sum(tile, 0, keepdims=True), 1, keepdims=True)


def place_pair(tile, i, j, value):
    row, lane = at(tile, 0), at(tile, 1)
    here = (row == i) & (lane == j[0])
    if j[1] is not None:
        here = here | ((row == j[1]) & (lane == j[2]))
    return jnp.where(here, value, tile)


def pressure_kernel(
    own, mate, other, beyond, shift, shift_mate, shift_other,
    wall, owner, slots, node, weight,
    payload, basis, work, sent, *, ranks,
):
    left, right = sides(mate, other)
    shift_left, shift_right = sides(shift_mate, shift_other)
    layers = shift.shape[0]
    for x in range(layers):
        work[0, x] = halves(left, x * 128)
        work[0, x + 4] = halves(own, x * 128)
        work[0, x + 8] = halves(right, x * 128)
    work[0, 12] = halves(beyond, 0)
    inside = [jnp.where(side[3 * end][0:1, 0:1] > 0.0, 1.0, 0.0) for side, end in ((shift_left, 1), (shift_right, 0))]
    copies = [
        pltpu.make_async_copy(work.at[k, pl.ds(4, layers)], basis.at[k], sent.at[k])
        for k in range(PITERS)
    ]
    copies[0].start()
    for step in range(1, PITERS):
        for x in range(step, 13 - step):
            now = work[step - 1, x]
            beside = work[step - 1, x - 1] + work[step - 1, x + 1] + plane_sum(now)
            if x < 4 or x >= 8:
                beside = inside[x // 8] * beside
            diagonal = (shift_left, shift, shift_right)[x // 4][x % 4] + (6.0 - P_SHIFT[step - 1])
            value = diagonal * now - beside
            if step > 1:
                value = value - P_BACK[step - 2] * work[step - 2, x]
            work[step, x] = value
        copies[step].start()
    tile = jnp.zeros((8, 128), F32)
    pairs = [(i, j) for i in range(PITERS) for j in range(i, PITERS)]
    totals = [0.0] * len(pairs)
    for x in range(4, 8):
        for y in range(0, 64, 8):
            for z in (0, 128):
                tiles = [work[k, x, y : y + 8, z : z + 128] for k in range(PITERS)]
                totals = [total + tiles[i] * tiles[j] for total, (i, j) in zip(totals, pairs)]
    for total, (i, j) in zip(totals, pairs):
        tile = place_pair(tile, 3 + i, (96 + j, 3 + j, 96 + i), whole(total))
    top = PITERS - 1
    total = 0.0
    for x in range(4, 8):
        now = work[top, x]
        image = (6.0 + shift[x - 4]) * now - plane_sum(now) - 2.0 * work[top, x + 1]
        total = total + now * image
    tile = place_pair(tile, 3 + top, (96 + PITERS, None, None), whole(fold(total)))
    lanes = lax.broadcasted_iota(jnp.int32, (128, 256), 0)
    field_row = lax.broadcasted_iota(jnp.int32, (8, 256), 0)
    packed = jnp.zeros((ranks * 8, 128), F32)
    weights = jnp.zeros((ranks * 8, 128), F32)
    for x in range(layers):
        scale = weight[x : x + 1, :].astype(F32)
        rows = [wall[x : x + 1, :] * scale, wall[4 + x : 5 + x, :] * scale]
        rows.append(node[x : x + 1, :].astype(F32))
        rows += [work[k, x + 4][0:1, :] * scale for k in range(PITERS)]
        values = jnp.concatenate(rows, 0)
        who = owner[x : x + 1, :]
        here = jnp.where((lanes & 31) == slots[x : x + 1, :], 1.0, 0.0)
        place = jnp.where(lanes < 96, here, 0.0).astype(BF16)
        end = jnp.where(lanes >= 96, here, 0.0).astype(BF16)
        left_rows = jnp.concatenate(
            [jnp.where(who == d, piece, 0.0) for piece in pieces_of(values, 3) for d in range(ranks)], 0
        )
        packed = packed + added(dot(left_rows.astype(BF16), place, True), 3)
        weight_rows = jnp.concatenate(
            [
                jnp.where((who == d - 1 + field_row) & (field_row < 3), scale, 0.0)
                for d in range(ranks)
            ],
            0,
        )
        weights = weights + dot(weight_rows.astype(BF16), end, True)
    lane = lax.broadcasted_iota(jnp.int32, (8, 128), 1)
    zero = jnp.zeros((8, 128), F32)
    for d in range(ranks):
        mine = packed[d * 8 : d * 8 + 8]
        before = packed[d * 8 - 8 : d * 8] if d > 0 else zero
        after = packed[d * 8 + 8 : d * 8 + 16] if d < ranks - 1 else zero
        block = jnp.where(lane < 32, before, jnp.where(lane < 64, mine, after))
        block = jnp.where(lane < 96, block, 0.0) + weights[d * 8 : d * 8 + 8]
        payload[d] = block + tile
    for copy in copies:
        copy.wait()


def second_spot(i, j):
    if i < SITERS:
        return 6 + i % 4, 96 + 16 * (i // 4) + j
    return 10 + (i - SITERS) // 4, 96 + 8 * ((i - SITERS) % 4) + j - SITERS


ENERGY_AT = (11, 112)


def place_second(tile, i, j, value):
    row, lane = second_spot(i, j)
    if i < SITERS <= j:
        return place_pair(tile, row, (lane, None, None), value)
    return place_pair(tile, row, (lane, *second_spot(j, i)), value)


def second_gram(summed):
    row, lane = at(summed, 0), at(summed, 1)
    first = pltpu.roll(pltpu.roll(summed, 32, 1), 10, 0)
    second = pltpu.roll(pltpu.roll(summed, 16, 1), 14, 0)
    gram = jnp.where(row < 4, first, second)
    gram = jnp.where((row < SITERS) & (lane < 16), gram, 0.0)
    for k in range(5):
        source, start = second_spot(SITERS + k, SITERS)
        moved = pltpu.roll(summed, (SITERS - start) % 128, 1)[source : source + 1]
        here = (row == SITERS + k) & (lane >= SITERS) & (lane < SITERS + 5)
        gram = jnp.where(here, jnp.broadcast_to(moved, gram.shape), gram)
    return gram


def row_of(matrix, k):
    return jnp.sum(jnp.where(at(matrix, 0) == k, matrix, 0.0), 0, keepdims=True)


def column_of(matrix, k):
    return jnp.sum(jnp.where(at(matrix, 1) == k, matrix, 0.0), 1, keepdims=True)


def eliminate(columns, right, first):
    row = at(right, 0)
    lengths = [TINY * column[first + k : first + k + 1] for k, column in enumerate(columns)]
    for k in range(len(columns)):
        column = columns[k]
        here = first + k
        pivot = column[here : here + 1]
        good = pivot > lengths[k]
        inverse = jnp.where(good, 1.0 / jnp.where(good, pivot, 1.0), 0.0)
        factor = column * inverse

        def reduced(values):
            mine = values[here : here + 1]
            return jnp.where(row == here, mine * inverse, values - factor * mine)

        columns = columns[: k + 1] + [reduced(values) for values in columns[k + 1 :]]
        right = reduced(right)
    return right


def galerkin(gram, first, shifts, back, energy):
    count = len(shifts)
    images = []
    for k in range(count - 1):
        image = shifts[k] * gram[k] + gram[k + 1]
        if k > 0:
            image = image + back[k - 1] * gram[k - 1]
        images.append(image)
    last = jnp.broadcast_to(gram[count - 1], (gram[0].shape[0], 128))
    row = at(last, 0)
    shift, prior = 0.0, 0.0
    for k in range(count):
        shift = jnp.where(row == first + k, shifts[k], shift)
    for k in range(1, count):
        prior = jnp.where(row == first + k, back[k - 1], prior)
    size = last.shape[0]
    image = shift * last + pltpu.roll(last, size - 1, 0) + prior * pltpu.roll(last, 1, 0)
    image = jnp.where(row == first + count - 1, energy, image)
    images.append(image[:, 0:1])
    return images


def picked_nodes(node):
    column = lax.broadcasted_iota(jnp.int32, (1024, node.shape[1]), 0)
    return jnp.where(column == (node & 1023), 1.0, 0.0).astype(BF16)


def nodes_values(fields, table, pick, line):
    for c in range(3):
        for f in range(8):
            value = fields[f](c) if f < len(fields) else jnp.zeros((8, 1024), F32)
            for k in range(8):
                table[k, pl.ds(c * 8 + f, 8, stride=24), :] = value[:, k * 128 : k * 128 + 128]
    found = split_dot(jnp.concatenate([table[k] for k in range(8)], 1), pick, 2)
    values = found[0:24]
    for r in range(1, 8):
        values = jnp.where(line == r, found[r * 24 : r * 24 + 24], values)
    return values


def force_kernel(
    received, displacement, solved_prev, solved_history,
    forces, requests, fixed, factors, table, *, ranks,
):
    lane8 = lax.broadcasted_iota(jnp.int32, (8, 128), 1)
    summed = received[0]
    for p in range(1, ranks):
        summed = summed + received[p]
    gram = [column_of(summed, 96 + k) for k in range(PITERS + 1)]
    system = galerkin(gram[:PITERS], 3, P_SHIFT, P_BACK, gram[PITERS][7:8])
    solved = eliminate(system, gram[0], 3)
    solved = jnp.where(lax.broadcasted_iota(jnp.int32, (8, 1), 0) >= 3, solved, 0.0)
    factors[...] = jnp.broadcast_to(solved, (8, 128))
    groups = [lane8 // 32 == q for q in range(4)]

    def gathered(j):
        chunks = []
        for k in range(ranks // 4):
            chunk = jnp.zeros((8, 128), F32)
            for q in range(4):
                chunk = jnp.where(
                    groups[q], pltpu.roll(received[4 * k + q], (32 * (q - j)) % 128, 1), chunk
                )
            chunks.append(chunk)
        return jnp.concatenate(chunks, 1)

    weights = gathered(3)
    entries = ranks * CAP
    target = lax.broadcasted_iota(jnp.int32, (64, entries), 0)
    low = lax.broadcasted_iota(jnp.int32, (128, entries), 0)
    node = None
    for j in range(3):
        values = gathered(j)
        numbers = values[2:3, :].astype(jnp.int32)
        if j == 1:
            node = numbers
        rows = (
            values[0:1, :],
            WALL * jnp.sum(values * solved, 0, keepdims=True),
            values[1:2, :],
        )
        code = ((numbers >> 7) & 7) * 8 + (numbers >> 10)
        spot = jnp.where(low == (numbers & 127), 1.0, 0.0).astype(BF16)
        match = target == code
        pieces = pieces_of(jnp.concatenate(rows, 0), 2)
        left_rows = jnp.concatenate(
            [jnp.where(match, piece[c : c + 1], 0.0) for piece in pieces for c in range(3)], 0
        )
        scattered = added(dot(left_rows.astype(BF16), spot, True), 2)
        share = dot(jnp.where(match, weights[j : j + 1, :], 0.0).astype(BF16), spot, True)
        share = 1.0 / jnp.maximum(share, 1.0)
        for c in range(3):
            force = scattered[c * 64 : c * 64 + 64] * share
            for k in range(8):
                forces[c, j * 8 : j * 8 + 8, k * 128 : k * 128 + 128] = force[k * 8 : k * 8 + 8]
    requests[...] = jnp.broadcast_to(node, (8, entries))
    pick = picked_nodes(node)
    fields = [lambda c: displacement[c]]
    fields += [lambda c, k=k: solved_history[k, c] for k in range(solved_history.shape[0])]
    fields.append(lambda c: solved_prev[c])
    fixed[...] = nodes_values(fields, table, pick, node >> 10)


def shell_kernel(
    forces, requests, fixed, own, mate, other, residual_prev, residual_history,
    payload, basis, work, diagonal, table, sent, *, ranks,
):
    left, right = sides(mate, other)
    inside = []
    for j, ref in enumerate((left, own, right)):
        stiff = []
        for k in range(8):
            columns = slice(k * 128, k * 128 + 128)
            stiff.append(ref[STIFF_AT + k * 8 : STIFF_AT + k * 8 + 8, :])
            for c in range(3):
                place = (c * 8 + k) * 8
                here = slice(j * 8, j * 8 + 8)
                work[0, c, here, columns] = forces[c, here, columns] + ref[place : place + 8, :]
        stiff = jnp.concatenate(stiff, 1)
        if j == 1:
            stiffness = stiff
        for c in range(3):
            diagonal[c * 24 + j * 8 : c * 24 + j * 8 + 8, :] = stiff
        inside.append(jnp.where(stiff[:, 0:1] > 0.0, 1.0, 0.0))
    inside = jnp.concatenate(inside * 3, 0)
    copies = [
        pltpu.make_async_copy(work.at[k, :, pl.ds(8, 8)], basis.at[k], sent.at[k])
        for k in range(SITERS)
    ]
    for step in range(1, SITERS):
        now = work[step - 1].reshape(72, 1024)
        value = (diagonal[...] + (4.0 - S_SHIFT[step - 1])) * now - inside * shell_beside(now)
        if step > 1:
            value = value - S_BACK[step - 2] * work[step - 2].reshape(72, 1024)
        work[step] = value.reshape(3, 24, 1024)
        copies[step - 1].start()
    copies[-1].start()
    def basis_tile(k, c, columns=slice(None)):
        return work[k, c, 8:16, columns]

    def tile_of(ref):
        return lambda c, columns=slice(None): ref[c, :, columns]

    vectors = [lambda c, columns=slice(None), k=k: basis_tile(k, c, columns) for k in range(SITERS)]
    vectors.append(tile_of(residual_prev))
    vectors += [tile_of(residual_history.at[k]) for k in range(residual_history.shape[0])]
    tile = jnp.zeros((16, 128), F32)
    pairs = [(i, j) for i in range(len(vectors)) for j in range(i, len(vectors))]
    for some in (pairs[:46], pairs[46:]):
        totals = [0.0] * len(some)
        used = sorted({v for pair in some for v in pair})
        for c in range(3):
            for k in range(8):
                tiles = {v: vectors[v](c, slice(k * 128, k * 128 + 128)) for v in used}
                totals = [total + tiles[i] * tiles[j] for total, (i, j) in zip(totals, some)]
        for total, (i, j) in zip(totals, some):
            tile = place_second(tile, i, j, whole(total))
    top = SITERS - 1
    total = 0.0
    for c in range(3):
        now = basis_tile(top, c)
        after = work[top, c, 9:17, :]
        image = (4.0 + stiffness) * now - ahead(now, 1) - behind(now, 1) - 2.0 * after
        total = total + now * image
    tile = place_pair(tile, ENERGY_AT[0], (ENERGY_AT[1], None, None), whole(fold(total)))
    node = requests[0:1, :]
    entries = node.shape[1]
    found = nodes_values(
        [lambda c, k=k: basis_tile(k, c) for k in range(SITERS)], table, picked_nodes(node), node >> 10
    )
    answer = [values[c * 8 : c * 8 + 8] for c in range(3) for values in (found, fixed)]
    answer = jnp.concatenate(answer, 0)
    lane16 = lax.broadcasted_iota(jnp.int32, (16, 128), 1)
    row16 = lax.broadcasted_iota(jnp.int32, (16, 128), 0)
    extra = jnp.concatenate(
        [answer[c * 16 + 12 : c * 16 + 14] for c in range(3)] + [jnp.zeros((10, entries), F32)], 0
    )
    for p in range(ranks):
        columns = slice(p // 4 * 128, p // 4 * 128 + 128)
        block = jnp.where(row16 < 6, pltpu.roll(extra[:, columns], (32 * (3 - p % 4)) % 128, 1), tile)
        for c in range(3):
            piece = answer[c * 16 : c * 16 + 16, columns]
            block = jnp.where(
                lane16 // 32 == c, pltpu.roll(piece, (32 * (c - p % 4)) % 128, 1), block
            )
        for t in range(3):
            payload[p, t] = block[t * 4 : t * 4 + 4]
    for copy in copies:
        copy.wait()


def combine_kernel(basis, factors, pressure):
    basis = basis()
    for x in range(pressure.shape[0]):
        total = 0.0
        for k in range(PITERS):
            total = total + factors[3 + k : 4 + k, 0:1] * basis[k, x]
        pressure[x] = total


def update_kernel(
    received, basis, displacement, solved_prev, solved_history, owner, slots,
    new_displacement, wall, *, ranks,
):
    summed = [sum(received[p, t] for p in range(ranks)) for t in range(3)]
    summed = jnp.concatenate(summed + [jnp.zeros((4, 128), F32)], 0)
    matrix = second_gram(summed)
    gram = [column_of(matrix, k) for k in range(SITERS + 5)]
    energy = summed[ENERGY_AT[0] : ENERGY_AT[0] + 1, ENERGY_AT[1] : ENERGY_AT[1] + 1]
    system = galerkin(gram[:SITERS], 0, S_SHIFT, S_BACK, energy)
    steps = eliminate(system, gram[0], 0)
    down = lax.broadcasted_iota(jnp.int32, (16, 1), 0)
    steps = jnp.where(down < SITERS, steps, 0.0)
    base, count = SITERS, 1 + solved_history.shape[0]
    with_moved = jnp.sum(matrix * steps, 0, keepdims=True)
    diagonal = at(matrix, 0) == at(matrix, 1)
    with_moved = jnp.sum(
        jnp.where(diagonal, jnp.broadcast_to(with_moved, matrix.shape), 0.0), 1, keepdims=True
    )
    with_newest = with_moved - gram[base]
    newest_moved = jnp.sum(steps * with_newest, 0, keepdims=True)
    newest_newest = newest_moved - with_newest[base : base + 1]
    columns = [jnp.where(down == base, newest_newest, with_newest)]
    for k in range(1, count):
        columns.append(jnp.where(down == base, with_newest[base + k : base + k + 1], gram[base + k]))
    right = jnp.where(down == base, newest_moved, with_moved)
    coefficients = -eliminate(columns, right, base)
    newest = row_of(coefficients, base)
    factors = jnp.where(
        down < base,
        (1.0 + newest) * steps,
        jnp.where(
            down == base,
            1.0 + newest,
            jnp.where(down < base + count, coefficients, jnp.where(down == base + count, -newest, 0.0)),
        ),
    )
    for c in range(3):
        total = row_of(factors, base) * displacement[c]
        for k in range(SITERS):
            total = total + row_of(factors, k) * basis[k, c]
        for k in range(count - 1):
            total = total + row_of(factors, base + 1 + k) * solved_history[k, c]
        total = total + row_of(factors, base + count) * solved_prev[c]
        new_displacement[c] = total
    row, group = at(summed, 0), at(summed, 1) // 32
    spare = jnp.where(row % 2 == 0, factors[12:13], factors[13:14])
    stacked = []
    for c in range(3):
        scales = jnp.where(group == c, factors, jnp.where((group == 3) & (row // 2 == c), spare, 0.0))
        scales = [scales[t * 4 : t * 4 + 4] for t in range(3)]
        for p in range(ranks):
            stacked.append(jnp.sum(sum(received[p, t] * scales[t] for t in range(3)), 0, keepdims=True))
    stacked = jnp.concatenate(stacked, 0)
    slot_row = lax.broadcasted_iota(jnp.int32, (128, 256), 0) & 31
    rank = lax.broadcasted_iota(jnp.int32, (ranks, 256), 0)
    for x in range(owner.shape[0]):
        pick = jnp.where(slot_row == slots[x : x + 1, :], 1.0, 0.0).astype(BF16)
        spread = split_dot(stacked, pick, 3)
        mine = rank == owner[x : x + 1, :]
        for c in range(3):
            wall[c : c + 1, x * 256 : x * 256 + 256] = jnp.sum(
                jnp.where(mine, spread[c * ranks : (c + 1) * ranks], 0.0), 0, keepdims=True
            )


def on_device(
    velocity,
    pressure_shift,
    owner_rank,
    node_index,
    map_weight,
    shell_load,
    shell_stiffness,
    displacement,
    residual_prev,
    solved_prev,
    residual_history,
    solved_history,
):
    ranks = lax.axis_size("slab")
    layers = velocity.shape[1]
    kept = residual_history.shape[0]

    def with_mate(values):
        return lax.ppermute(values, "slab", [(i, i ^ 1) for i in range(ranks)])

    def with_other(values):
        pairs = [(i, i + 1) for i in range(1, ranks - 1, 2)]
        return lax.ppermute(values, "slab", pairs + [(j, i) for i, j in pairs])

    node = node_index.reshape(layers, -1)
    weight = map_weight.reshape(layers, -1)
    plane = shape(*velocity.shape[2:])

    to_mate, to_other, own_left, own_right = call(
        edge_kernel,
        (shape(HALO_ROWS, 128), shape(HALO_ROWS, 128), plane, plane),
        (velocity, displacement),
        outer=(0, 1),
        stored=(0, 1),
        scratch=(
            pltpu.VMEM(velocity.shape, F32),
            pltpu.VMEM(displacement.shape, F32),
            pltpu.SemaphoreType.DMA((4, max(layers, 1))),
        ),
    )
    halo_other, halo_mate = with_other(to_other), with_mate(to_mate)
    shift_other, shift_mate = with_other(pressure_shift), with_mate(pressure_shift)
    source, wall = call(fluid_kernel, (shape(*velocity.shape[1:]), shape(8, 256)), (velocity,))
    slots, owner = call(
        lambda *refs: slots_kernel(*refs, ranks=ranks),
        (shape(layers, 256, dtype=jnp.int32), shape(layers, 256, dtype=jnp.int32)),
        (owner_rank.T,),
    )
    fields, first, shell, wall = call(
        lambda *refs: source_kernel(*refs),
        (shape(FIELD_ROWS, 128), shape(128, 128), shape(SHELL_ROWS, 128), shape(8, 256)),
        (
            source, wall, own_left, own_right, halo_mate, halo_other,
            displacement, shell_load, shell_stiffness,
        ),
        pairs=(4,),
    )
    beyond = lax.ppermute(first, "slab", [(i, i - 2) for i in range(2, ranks)])
    fields_other, fields_mate = with_other(fields), with_mate(fields)
    shell_other, shell_mate = with_other(shell), with_mate(shell)
    payload, pressure_basis = call(
        lambda *refs: pressure_kernel(*refs, ranks=ranks),
        (shape(ranks, 8, 128), pltpu.HBM((PITERS, *pressure_shift.shape), F32)),
        (
            fields, fields_mate, fields_other, beyond, pressure_shift, shift_mate, shift_other,
            wall, owner, slots, node, weight,
        ),
        direct=(1,),
        scratch=(
            pltpu.VMEM((PITERS, 13, 64, 256), F32),
            pltpu.SemaphoreType.DMA((PITERS,)),
        ),
    )
    received = lax.all_to_all(payload, "slab", split_axis=0, concat_axis=0, tiled=True)
    entries = ranks * CAP
    forces, requests, fixed, factors = call(
        lambda *refs: force_kernel(*refs, ranks=ranks),
        (
            shape(3, 3 * displacement.shape[1], displacement.shape[2]),
            shape(8, entries, dtype=jnp.int32), shape(24, entries), shape(8, 128),
        ),
        (received, displacement, solved_prev, solved_history),
        scratch=(pltpu.VMEM((8, 8 * 24, 128), F32),),
    )
    payload, shell_basis = call(
        lambda *refs: shell_kernel(*refs, ranks=ranks),
        (shape(ranks, 3, 4, 128), pltpu.HBM((SITERS, *displacement.shape), F32)),
        (
            forces, requests, fixed, shell, shell_mate, shell_other, residual_prev, residual_history,
        ),
        direct=(1,),
        scratch=(
            pltpu.VMEM((SITERS, 3, 24, 1024), F32),
            pltpu.VMEM((72, 1024), F32),
            pltpu.VMEM((8, 8 * 24, 128), F32),
            pltpu.SemaphoreType.DMA((SITERS,)),
        ),
    )
    answers = lax.all_to_all(payload, "slab", split_axis=0, concat_axis=0, tiled=True)
    (pressure,) = call(
        combine_kernel,
        (shape(*pressure_shift.shape),),
        (pressure_basis, factors),
        late=(0,),
        stored=(0,),
    )
    new_displacement, wall_displacement = call(
        lambda *refs: update_kernel(*refs, ranks=ranks),
        (shape(*displacement.shape), shape(3, owner_rank.shape[0])),
        (answers, shell_basis, displacement, solved_prev, solved_history, owner, slots),
    )
    return (pressure, new_displacement, wall_displacement)


def solution(mesh):
    in_specs = (
        P(None, ("groups", "slab"), None, None),
        P(("groups", "slab"), None, None),
        P(("groups", "slab"), None),
        P(("groups", "slab")),
        P(("groups", "slab")),
        P(None, ("groups", "slab"), None),
        P(("groups", "slab"), None),
        P(None, ("groups", "slab"), None),
        P(None, ("groups", "slab"), None),
        P(None, ("groups", "slab"), None),
        P(None, None, ("groups", "slab"), None),
        P(None, None, ("groups", "slab"), None),
    )
    out_specs = (
        P(("groups", "slab"), None, None),
        P(None, ("groups", "slab"), None),
        P(None, ("groups", "slab")),
    )
    return jax.shard_map(
        on_device, mesh=mesh, in_specs=in_specs, out_specs=out_specs, check_vma=False
    )
```

```python
import jax
import jax.numpy as jnp
from jax import lax
from jax.experimental import pallas as pl
from jax.experimental.pallas import tpu as pltpu
from jax.sharding import PartitionSpec as P

CAP = 32
PITERS = 5
SITERS = 8

NU = 0.15
MU = 0.5
WALL = 4.0

P_SHIFT, P_BACK = (4.93, 7.29, 5.13, 7.05, 5.38), (10.17, 6.01, 8.86, 8.24)
S_SHIFT = (5.7, 5.09, 4.26, 4.26, 4.08, 4.17, 4.1, 4.18)
S_BACK = (2.53, 3.17, 4.07, 3.95, 4.22, 4.01, 4.14)
TINY = 1e-7
LEAST_SHARE = 0.01

VMEM = pl.BlockSpec(memory_space=pltpu.VMEM)
F32 = jnp.float32
BF16 = jnp.bfloat16

H2_AT, ROW_AT, DISP_AT, HALO_ROWS = 128, 256, 264, 288
FIELD_ROWS, STIFF_AT, SHELL_ROWS = 512, 192, 256


def even_device():
    return lax.rem(lax.axis_index("slab"), 2) == 0


class Late:
    def __init__(self, source, place, semaphore):
        self.place = place
        self.copy = pltpu.make_async_copy(source, place, semaphore)
        self.copy.start()
        self.pending = True

    def __call__(self):
        if self.pending:
            self.copy.wait()
            self.pending = False
        return self.place


class Sides:
    def __init__(self, to_mate, to_other, left, right, semaphores):
        even = even_device()
        self.copies = [
            pltpu.make_async_copy(to_mate, left, semaphores.at[0]),
            pltpu.make_async_copy(to_other, right, semaphores.at[1]),
        ]
        self.places = (left, right)

        @pl.when(even)
        def _():
            pltpu.make_async_copy(to_other, left, semaphores.at[0]).start()
            pltpu.make_async_copy(to_mate, right, semaphores.at[1]).start()

        @pl.when(jnp.logical_not(even))
        def _():
            for copy in self.copies:
                copy.start()

        self.pending = True

    def __call__(self):
        if self.pending:
            for copy in self.copies:
                copy.wait()
            self.pending = False
        return self.places


class Either:
    def __init__(self, which, first, second):
        self.which, self.first, self.second = which, first, second

    def __getitem__(self, index):
        return jnp.where(self.which, self.first[index], self.second[index])


def sides(to_mate, to_other):
    even = even_device()
    return Either(even, to_other, to_mate), Either(even, to_mate, to_other)


def call(
    kernel, outs, args, late=(), outer=(), pairs=(), direct=(), stored=(), scratch=(),
    flops=1000000000, limit=48.0,
):
    count, made = len(args), len(outs)

    def body(*refs):
        operands = list(refs[:count])
        at_end = count + made + len(scratch)
        places = iter(refs[at_end:-1])
        wanted = []
        used = 0
        for i in late:
            operands[i] = Late(operands[i], next(places), refs[-1].at[used])
            wanted.append(operands[i])
            used += 1
        for i in pairs:
            operands[i] = Sides(
                operands[i], operands[i + 1], next(places), next(places), refs[-1].at[pl.ds(used, 2)]
            )
            wanted.append(operands[i])
            used += 2
        operands = [value for i, value in enumerate(operands) if i - 1 not in pairs]
        kernel(*operands, *refs[count:at_end])
        for value in wanted:
            value()

    outside = [i for i in late] + [i + k for i in pairs for k in (0, 1)]
    extra = [pltpu.VMEM(args[i].shape, args[i].dtype) for i in outside]
    extra.append(pltpu.SemaphoreType.DMA((max(1, len(outside)),)))
    args = [
        pltpu.with_memory_space_constraint(value, pltpu.HBM) if i in stored else value
        for i, value in enumerate(args)
    ]
    any_space = pl.BlockSpec(memory_space=pl.ANY)
    return pl.pallas_call(
        body,
        out_shape=outs,
        in_specs=[any_space if i in outside or i in outer else VMEM for i in range(count)],
        out_specs=tuple(any_space if i in direct else VMEM for i in range(made)),
        scratch_shapes=list(scratch) + extra,
        compiler_params=pltpu.CompilerParams(vmem_limit_bytes=int(limit * 1024 * 1024)),
        cost_estimate=pl.CostEstimate(flops=flops, bytes_accessed=0, transcendentals=0),
    )(*args)


def shape(*dims, dtype=F32):
    return jax.ShapeDtypeStruct(dims, dtype)


def at(values, axis):
    return lax.broadcasted_iota(jnp.int32, values.shape, axis)


def without_edge(values, axis, index):
    width = (8, 128)[axis]
    size = values.shape[axis]
    edge = 0 if index == 0 else size - width
    tile = lax.slice_in_dim(values, edge, edge + width, axis=axis)
    tile = jnp.where(at(tile, axis) == index - edge, 0.0, tile)
    if index == 0:
        rest = lax.slice_in_dim(values, width, size, axis=axis)
        return jnp.concatenate([tile, rest], axis)
    return jnp.concatenate([lax.slice_in_dim(values, 0, edge, axis=axis), tile], axis)


def ahead(values, axis):
    size = values.shape[axis]
    return without_edge(pltpu.roll(values, size - 1, axis), axis, size - 1)


def behind(values, axis):
    return without_edge(pltpu.roll(values, 1, axis), axis, 0)


def plane_sum(plane):
    return ahead(plane, 0) + behind(plane, 0) + ahead(plane, 1) + behind(plane, 1)


def difference(plane, axis):
    return ahead(plane, axis) - behind(plane, axis)


def halves(ref, start):
    return jnp.concatenate([ref[start : start + 64, :], ref[start + 64 : start + 128, :]], axis=1)


def put_halves(ref, start, plane):
    ref[start : start + 64, :] = plane[:, :128]
    ref[start + 64 : start + 128, :] = plane[:, 128:]


def parts(values, count):
    pieces = []
    for _ in range(count - 1):
        piece = values.astype(BF16)
        pieces.append(piece)
        values = values - piece.astype(F32)
    pieces.append(values.astype(BF16))
    return pieces


def dot(left, right, transposed=False):
    dims = (((1,), (1 if transposed else 0,)), ((), ()))
    return lax.dot_general(left, right, dims, preferred_element_type=F32)


def pieces_of(values, count):
    pieces = []
    for _ in range(count):
        pieces.append(values.astype(BF16).astype(F32))
        values = values - pieces[-1]
    return pieces


def added(product, count):
    rows = product.shape[0] // count
    return sum(product[i * rows : (i + 1) * rows] for i in range(count))


def split_dot(left, right, count, transposed=False):
    rows = left.shape[0]
    product = dot(jnp.concatenate(parts(left, count), 0), right, transposed)
    return sum(product[i * rows : (i + 1) * rows] for i in range(count))


def plane_part(plane):
    return (1.0 - 6.0 * NU) * plane + NU * plane_sum(plane)


def edge_kernel(
    velocity_in, displacement_in, to_mate, to_other, own_left, own_right,
    velocity, displacement, arrived,
):
    layers = velocity.shape[1]
    last = layers - 1
    copies = [pltpu.make_async_copy(velocity_in.at[0], velocity.at[0], arrived.at[0, 0])]
    for c in (1, 2):
        for x in (0, last):
            copies.append(
                pltpu.make_async_copy(velocity_in.at[c, x], velocity.at[c, x], arrived.at[c, x])
            )
    copies.append(pltpu.make_async_copy(displacement_in, displacement, arrived.at[3, 0]))
    for copy in copies:
        copy.start()
    for copy in copies:
        copy.wait()
    even = even_device()
    spread = {
        x: NU * (difference(velocity[1, x], 0) + difference(velocity[2, x], 1)) for x in (0, last)
    }
    lefts = (plane_part(velocity[0, 0]) + NU * velocity[0, 1] + spread[0], NU * velocity[0, 0])
    rights = (
        spread[last] - plane_part(velocity[0, last]) - NU * velocity[0, last - 1],
        NU * velocity[0, last],
    )
    own_left[...] = lefts[1]
    own_right[...] = rights[1]
    edges = [
        (MU * NU) * (velocity[2, x, 1:2, :] - velocity[2, x, 0:1, :]) for x in (0, last)
    ]
    for ref, first, second in ((to_mate, rights, lefts), (to_other, lefts, rights)):
        put_halves(ref, 0, jnp.where(even, first[0], second[0]))
        put_halves(ref, H2_AT, jnp.where(even, first[1], second[1]))
        ref[ROW_AT : DISP_AT, :] = jnp.zeros((8, 128), F32)
        ref[ROW_AT + 2 : ROW_AT + 3, :] = jnp.ones((1, 128), F32)
        edge = jnp.where(even, edges[int(first is rights)], edges[int(second is rights)])
        ref[ROW_AT : ROW_AT + 1, :] = edge[:, :128]
        ref[ROW_AT + 1 : ROW_AT + 2, :] = edge[:, 128:]
        for c in range(3):
            rows = (displacement[c, 0:1, :], displacement[c, 7:8, :])
            row = jnp.where(even, rows[int(first is rights)], rows[int(second is rights)])
            for k in range(8):
                place = DISP_AT + c * 8 + k
                ref[place : place + 1, :] = row[:, k * 128 : k * 128 + 128]


def fluid_kernel(velocity, source, wall):
    layers = velocity.shape[1]
    last = layers - 1
    field = [[velocity[c, x] for x in range(layers)] for c in range(3)]
    own = [[plane_part(f) for f in rows] for rows in field]
    zero = jnp.zeros_like(field[0][0])
    predicted = [
        [
            own[c][x]
            + NU
            * (
                (field[c][x + 1] if x < last else zero)
                + (field[c][x - 1] if x > 0 else zero)
            )
            for x in range(layers)
        ]
        for c in range(3)
    ]
    for x in range(layers):
        after = predicted[0][x + 1] if x < last else zero
        before = predicted[0][x - 1] if x > 0 else zero
        source[x] = -0.5 * (
            after - before + difference(predicted[1][x], 0) + difference(predicted[2][x], 1)
        )
        wall[x : x + 1, :] = MU * (predicted[0][x][1:2, :] - predicted[0][x][0:1, :])
        wall[4 + x : 5 + x, :] = MU * (predicted[2][x][1:2, :] - predicted[2][x][0:1, :])


def shell_beside(field):
    rows = field.shape[0]
    beside = pltpu.roll(field, rows - 1, 0) + pltpu.roll(field, 1, 0)
    return beside + ahead(field, 1) + behind(field, 1)


def source_kernel(
    source, wall, own_left, own_right, halo, displacement, load, stiffness,
    fields, first, shell, wall_out,
):
    from_left, from_right = halo()
    layers = source.shape[0]
    last = layers - 1
    left1, left2 = halves(from_left, 0), halves(from_left, H2_AT)
    right1, right2 = halves(from_right, 0), halves(from_right, H2_AT)
    has_left = from_left[ROW_AT + 2 : ROW_AT + 3, 0:1]
    has_right = from_right[ROW_AT + 2 : ROW_AT + 3, 0:1]
    left1 = left1 - has_left * own_left[...]
    right1 = right1 + has_right * own_right[...]
    for x in range(layers):
        plane = source[x]
        if x == 0:
            plane = plane - 0.5 * left1
        if x == 1:
            plane = plane + 0.5 * left2
        if x == last - 1:
            plane = plane - 0.5 * right2
        if x == last:
            plane = plane - 0.5 * right1
        put_halves(fields, x * 128, plane)
        if x == 0:
            put_halves(first, 0, plane)
    wall_out[...] = wall[...]
    for x, ref, plane in ((0, from_left, left2), (last, from_right, right2)):
        edge = jnp.concatenate([ref[ROW_AT : ROW_AT + 1, :], ref[ROW_AT + 1 : ROW_AT + 2, :]], 1)
        wall_out[x : x + 1, :] = wall[x : x + 1, :] + MU * (plane[1:2, :] - plane[0:1, :])
        wall_out[4 + x : 5 + x, :] = wall[4 + x : 5 + x, :] + edge
    for c in range(3):
        field = displacement[c]
        above = jnp.concatenate(
            [from_left[DISP_AT + c * 8 + k : DISP_AT + c * 8 + k + 1, :] for k in range(8)], 1
        )
        below = jnp.concatenate(
            [from_right[DISP_AT + c * 8 + k : DISP_AT + c * 8 + k + 1, :] for k in range(8)], 1
        )
        row = at(field, 0)
        beside = jnp.where(row == 0, above, pltpu.roll(field, 1, 0))
        beside = beside + jnp.where(row == 7, below, pltpu.roll(field, 7, 0))
        beside = beside + ahead(field, 1) + behind(field, 1)
        start = load[c] - ((4.0 + stiffness[...]) * field - beside)
        for k in range(8):
            place = (c * 8 + k) * 8
            shell[place : place + 8, :] = start[:, k * 128 : k * 128 + 128]
    for k in range(8):
        place = STIFF_AT + k * 8
        shell[place : place + 8, :] = stiffness[:, k * 128 : k * 128 + 128]


def slots_kernel(owners, slots, owner, *, ranks):
    width = owner.shape[1]
    for x in range(owner.shape[0]):
        owner[x : x + 1, :] = owners[:, x * width : x * width + width]
    down = lax.broadcasted_iota(jnp.int32, (width, width), 0)
    across = lax.broadcasted_iota(jnp.int32, (width, width), 1)
    earlier = jnp.where(down < across, 1.0, 0.0).astype(BF16)
    rank = lax.broadcasted_iota(jnp.int32, (ranks, width), 0)
    seen = jnp.zeros((ranks, 1), F32)
    for x in range(owner.shape[0]):
        member = jnp.where(rank == owner[x : x + 1, :], 1.0, 0.0)
        before = dot(member.astype(BF16), earlier) + seen
        slots[x : x + 1, :] = jnp.sum(before * member, 0, keepdims=True).astype(jnp.int32)
        seen = seen + jnp.sum(member, 1, keepdims=True)


def fold(product):
    rows, columns = product.shape
    tall = product[0:8]
    for a in range(1, rows // 8):
        tall = tall + product[a * 8 : a * 8 + 8]
    total = tall[:, :128]
    for b in range(1, columns // 128):
        total = total + tall[:, b * 128 : b * 128 + 128]
    return total


def whole(tile):
    return jnp.sum(jnp.sum(tile, 0, keepdims=True), 1, keepdims=True)


def place_pair(tile, i, j, value):
    row, lane = at(tile, 0), at(tile, 1)
    here = (row == i) & (lane == j[0])
    if j[1] is not None:
        here = here | ((row == j[1]) & (lane == j[2]))
    return jnp.where(here, value, tile)


def pressure_kernel(
    own, mate, other, beyond, shift, shift_mate, shift_other,
    wall, owner, slots, node, weight,
    payload, basis, work, sent, *, ranks,
):
    left, right = sides(mate, other)
    shift_left, shift_right = sides(shift_mate, shift_other)
    layers = shift.shape[0]
    for x in range(layers):
        work[0, x] = halves(left, x * 128)
        work[0, x + 4] = halves(own, x * 128)
        work[0, x + 8] = halves(right, x * 128)
    work[0, 12] = halves(beyond, 0)
    inside = [jnp.where(side[3 * end][0:1, 0:1] > 0.0, 1.0, 0.0) for side, end in ((shift_left, 1), (shift_right, 0))]
    copies = [
        pltpu.make_async_copy(work.at[k, pl.ds(4, layers)], basis.at[k], sent.at[k])
        for k in range(PITERS)
    ]
    copies[0].start()
    for step in range(1, PITERS):
        for x in range(step, 13 - step):
            now = work[step - 1, x]
            beside = work[step - 1, x - 1] + work[step - 1, x + 1] + plane_sum(now)
            if x < 4 or x >= 8:
                beside = inside[x // 8] * beside
            diagonal = (shift_left, shift, shift_right)[x // 4][x % 4] + (6.0 - P_SHIFT[step - 1])
            value = diagonal * now - beside
            if step > 1:
                value = value - P_BACK[step - 2] * work[step - 2, x]
            work[step, x] = value
        copies[step].start()
    tile = jnp.zeros((8, 128), F32)
    pairs = [(i, j) for i in range(PITERS) for j in range(i, PITERS)]
    totals = [0.0] * len(pairs)
    for x in range(4, 8):
        for y in range(0, 64, 8):
            for z in (0, 128):
                tiles = [work[k, x, y : y + 8, z : z + 128] for k in range(PITERS)]
                totals = [total + tiles[i] * tiles[j] for total, (i, j) in zip(totals, pairs)]
    for total, (i, j) in zip(totals, pairs):
        tile = place_pair(tile, 3 + i, (96 + j, 3 + j, 96 + i), whole(total))
    top = PITERS - 1
    total = 0.0
    for x in range(4, 8):
        now = work[top, x]
        image = (6.0 + shift[x - 4]) * now - plane_sum(now) - 2.0 * work[top, x + 1]
        total = total + now * image
    tile = place_pair(tile, 3 + top, (96 + PITERS, None, None), whole(fold(total)))
    lanes = lax.broadcasted_iota(jnp.int32, (128, 256), 0)
    field_row = lax.broadcasted_iota(jnp.int32, (8, 256), 0)
    packed = jnp.zeros((ranks * 8, 128), F32)
    weights = jnp.zeros((ranks * 8, 128), F32)
    for x in range(layers):
        scale = weight[x : x + 1, :].astype(F32)
        rows = [wall[x : x + 1, :] * scale, wall[4 + x : 5 + x, :] * scale]
        rows.append(node[x : x + 1, :].astype(F32))
        rows += [work[k, x + 4][0:1, :] * scale for k in range(PITERS)]
        values = jnp.concatenate(rows, 0)
        who = owner[x : x + 1, :]
        here = jnp.where((lanes & 31) == slots[x : x + 1, :], 1.0, 0.0)
        place = jnp.where(lanes < 96, here, 0.0).astype(BF16)
        end = jnp.where(lanes >= 96, here, 0.0).astype(BF16)
        left_rows = jnp.concatenate(
            [jnp.where(who == d, piece, 0.0) for piece in pieces_of(values, 3) for d in range(ranks)], 0
        )
        packed = packed + added(dot(left_rows.astype(BF16), place, True), 3)
        weight_rows = jnp.concatenate(
            [
                jnp.where((who == d - 1 + field_row) & (field_row < 3), scale, 0.0)
                for d in range(ranks)
            ],
            0,
        )
        weights = weights + dot(weight_rows.astype(BF16), end, True)
    lane = lax.broadcasted_iota(jnp.int32, (8, 128), 1)
    zero = jnp.zeros((8, 128), F32)
    for d in range(ranks):
        mine = packed[d * 8 : d * 8 + 8]
        before = packed[d * 8 - 8 : d * 8] if d > 0 else zero
        after = packed[d * 8 + 8 : d * 8 + 16] if d < ranks - 1 else zero
        block = jnp.where(lane < 32, before, jnp.where(lane < 64, mine, after))
        block = jnp.where(lane < 96, block, 0.0) + weights[d * 8 : d * 8 + 8]
        payload[d] = block + tile
    for copy in copies:
        copy.wait()


def second_spot(i, j):
    if i < SITERS:
        return 6 + i % 4, 96 + 16 * (i // 4) + j
    return 10 + (i - SITERS) // 4, 96 + 8 * ((i - SITERS) % 4) + j - SITERS


ENERGY_AT = (11, 112)


def place_second(tile, i, j, value):
    row, lane = second_spot(i, j)
    if i < SITERS <= j:
        return place_pair(tile, row, (lane, None, None), value)
    return place_pair(tile, row, (lane, *second_spot(j, i)), value)


def second_gram(summed):
    row, lane = at(summed, 0), at(summed, 1)
    first = pltpu.roll(pltpu.roll(summed, 32, 1), 10, 0)
    second = pltpu.roll(pltpu.roll(summed, 16, 1), 14, 0)
    gram = jnp.where(row < 4, first, second)
    gram = jnp.where((row < SITERS) & (lane < 16), gram, 0.0)
    for k in range(5):
        source, start = second_spot(SITERS + k, SITERS)
        moved = pltpu.roll(summed, (SITERS - start) % 128, 1)[source : source + 1]
        here = (row == SITERS + k) & (lane >= SITERS) & (lane < SITERS + 5)
        gram = jnp.where(here, jnp.broadcast_to(moved, gram.shape), gram)
    return gram


def row_of(matrix, k):
    return jnp.sum(jnp.where(at(matrix, 0) == k, matrix, 0.0), 0, keepdims=True)


def column_of(matrix, k):
    return jnp.sum(jnp.where(at(matrix, 1) == k, matrix, 0.0), 1, keepdims=True)


def eliminate(columns, right, first):
    row = at(right, 0)
    share = jnp.ones((1, 1), F32)
    lengths = [TINY * column[first + k : first + k + 1] for k, column in enumerate(columns)]
    for k in range(len(columns)):
        column = columns[k]
        here = first + k
        pivot = column[here : here + 1]
        good = pivot > lengths[k]
        share = jnp.minimum(share, jnp.where(good, pivot * TINY / jnp.where(good, lengths[k], 1.0), 0.0))
        inverse = jnp.where(good, 1.0 / jnp.where(good, pivot, 1.0), 0.0)
        factor = column * inverse

        def reduced(values):
            mine = values[here : here + 1]
            return jnp.where(row == here, mine * inverse, values - factor * mine)

        columns = columns[: k + 1] + [reduced(values) for values in columns[k + 1 :]]
        right = reduced(right)
    return right, share


def galerkin(gram, first, shifts, back, energy):
    count = len(shifts)
    images = []
    for k in range(count - 1):
        image = shifts[k] * gram[k] + gram[k + 1]
        if k > 0:
            image = image + back[k - 1] * gram[k - 1]
        images.append(image)
    last = jnp.broadcast_to(gram[count - 1], (gram[0].shape[0], 128))
    row = at(last, 0)
    shift, prior = 0.0, 0.0
    for k in range(count):
        shift = jnp.where(row == first + k, shifts[k], shift)
    for k in range(1, count):
        prior = jnp.where(row == first + k, back[k - 1], prior)
    size = last.shape[0]
    image = shift * last + pltpu.roll(last, size - 1, 0) + prior * pltpu.roll(last, 1, 0)
    image = jnp.where(row == first + count - 1, energy, image)
    images.append(image[:, 0:1])
    return images


def picked_nodes(node):
    column = lax.broadcasted_iota(jnp.int32, (1024, node.shape[1]), 0)
    return jnp.where(column == (node & 1023), 1.0, 0.0).astype(BF16)


def nodes_values(fields, table, pick, line):
    for c in range(3):
        for f in range(8):
            value = fields[f](c) if f < len(fields) else jnp.zeros((8, 1024), F32)
            for k in range(8):
                table[k, pl.ds(c * 8 + f, 8, stride=24), :] = value[:, k * 128 : k * 128 + 128]
    found = split_dot(jnp.concatenate([table[k] for k in range(8)], 1), pick, 2)
    values = found[0:24]
    for r in range(1, 8):
        values = jnp.where(line == r, found[r * 24 : r * 24 + 24], values)
    return values


def force_kernel(
    received, displacement, solved_prev, solved_history,
    forces, requests, fixed, factors, table, *, ranks,
):
    lane8 = lax.broadcasted_iota(jnp.int32, (8, 128), 1)
    summed = received[0]
    for p in range(1, ranks):
        summed = summed + received[p]
    gram = [column_of(summed, 96 + k) for k in range(PITERS + 1)]
    system = galerkin(gram[:PITERS], 3, P_SHIFT, P_BACK, gram[PITERS][7:8])
    solved, share = eliminate(system, gram[0], 3)
    solved = jnp.where(lax.broadcasted_iota(jnp.int32, (8, 1), 0) >= 3, solved, 0.0)
    first_row = lax.broadcasted_iota(jnp.int32, (8, 1), 0) == 0
    factors[...] = jnp.broadcast_to(jnp.where(first_row, share, solved), (8, 128))
    groups = [lane8 // 32 == q for q in range(4)]

    def gathered(j):
        chunks = []
        for k in range(ranks // 4):
            chunk = jnp.zeros((8, 128), F32)
            for q in range(4):
                chunk = jnp.where(
                    groups[q], pltpu.roll(received[4 * k + q], (32 * (q - j)) % 128, 1), chunk
                )
            chunks.append(chunk)
        return jnp.concatenate(chunks, 1)

    weights = gathered(3)
    entries = ranks * CAP
    target = lax.broadcasted_iota(jnp.int32, (64, entries), 0)
    low = lax.broadcasted_iota(jnp.int32, (128, entries), 0)
    node = None
    for j in range(3):
        values = gathered(j)
        numbers = values[2:3, :].astype(jnp.int32)
        if j == 1:
            node = numbers
        rows = (
            values[0:1, :],
            WALL * jnp.sum(values * solved, 0, keepdims=True),
            values[1:2, :],
        )
        code = ((numbers >> 7) & 7) * 8 + (numbers >> 10)
        spot = jnp.where(low == (numbers & 127), 1.0, 0.0).astype(BF16)
        match = target == code
        pieces = pieces_of(jnp.concatenate(rows, 0), 2)
        left_rows = jnp.concatenate(
            [jnp.where(match, piece[c : c + 1], 0.0) for piece in pieces for c in range(3)], 0
        )
        scattered = added(dot(left_rows.astype(BF16), spot, True), 2)
        total_weight = dot(jnp.where(match, weights[j : j + 1, :], 0.0).astype(BF16), spot, True)
        inverse = 1.0 / jnp.maximum(total_weight, 1.0)
        for c in range(3):
            force = scattered[c * 64 : c * 64 + 64] * inverse
            for k in range(8):
                forces[c, j * 8 : j * 8 + 8, k * 128 : k * 128 + 128] = force[k * 8 : k * 8 + 8]
    requests[...] = jnp.broadcast_to(node, (8, entries))
    pick = picked_nodes(node)
    fields = [lambda c: displacement[c]]
    fields += [lambda c, k=k: solved_history[k, c] for k in range(solved_history.shape[0])]
    fields.append(lambda c: solved_prev[c])
    fixed[...] = nodes_values(fields, table, pick, node >> 10)


def shell_kernel(
    forces, requests, fixed, own, mate, other, residual_prev, residual_history,
    payload, basis, work, diagonal, table, sent, *, ranks,
):
    left, right = sides(mate, other)
    inside = []
    for j, ref in enumerate((left, own, right)):
        stiff = []
        for k in range(8):
            columns = slice(k * 128, k * 128 + 128)
            stiff.append(ref[STIFF_AT + k * 8 : STIFF_AT + k * 8 + 8, :])
            for c in range(3):
                place = (c * 8 + k) * 8
                here = slice(j * 8, j * 8 + 8)
                work[0, c, here, columns] = forces[c, here, columns] + ref[place : place + 8, :]
        stiff = jnp.concatenate(stiff, 1)
        if j == 1:
            stiffness = stiff
        for c in range(3):
            diagonal[c * 24 + j * 8 : c * 24 + j * 8 + 8, :] = stiff
        inside.append(jnp.where(stiff[:, 0:1] > 0.0, 1.0, 0.0))
    inside = jnp.concatenate(inside * 3, 0)
    copies = [
        pltpu.make_async_copy(work.at[k, :, pl.ds(8, 8)], basis.at[k], sent.at[k])
        for k in range(SITERS)
    ]
    for step in range(1, SITERS):
        now = work[step - 1].reshape(72, 1024)
        value = (diagonal[...] + (4.0 - S_SHIFT[step - 1])) * now - inside * shell_beside(now)
        if step > 1:
            value = value - S_BACK[step - 2] * work[step - 2].reshape(72, 1024)
        work[step] = value.reshape(3, 24, 1024)
        copies[step - 1].start()
    copies[-1].start()
    def basis_tile(k, c, columns=slice(None)):
        return work[k, c, 8:16, columns]

    def tile_of(ref):
        return lambda c, columns=slice(None): ref[c, :, columns]

    vectors = [lambda c, columns=slice(None), k=k: basis_tile(k, c, columns) for k in range(SITERS)]
    vectors.append(tile_of(residual_prev))
    vectors += [tile_of(residual_history.at[k]) for k in range(residual_history.shape[0])]
    tile = jnp.zeros((16, 128), F32)
    pairs = [(i, j) for i in range(len(vectors)) for j in range(i, len(vectors))]
    for some in (pairs[:46], pairs[46:]):
        totals = [0.0] * len(some)
        used = sorted({v for pair in some for v in pair})
        for c in range(3):
            for k in range(8):
                tiles = {v: vectors[v](c, slice(k * 128, k * 128 + 128)) for v in used}
                totals = [total + tiles[i] * tiles[j] for total, (i, j) in zip(totals, some)]
        for total, (i, j) in zip(totals, some):
            tile = place_second(tile, i, j, whole(total))
    top = SITERS - 1
    total = 0.0
    for c in range(3):
        now = basis_tile(top, c)
        after = work[top, c, 9:17, :]
        image = (4.0 + stiffness) * now - ahead(now, 1) - behind(now, 1) - 2.0 * after
        total = total + now * image
    tile = place_pair(tile, ENERGY_AT[0], (ENERGY_AT[1], None, None), whole(fold(total)))
    node = requests[0:1, :]
    entries = node.shape[1]
    found = nodes_values(
        [lambda c, k=k: basis_tile(k, c) for k in range(SITERS)], table, picked_nodes(node), node >> 10
    )
    answer = [values[c * 8 : c * 8 + 8] for c in range(3) for values in (found, fixed)]
    answer = jnp.concatenate(answer, 0)
    lane16 = lax.broadcasted_iota(jnp.int32, (16, 128), 1)
    row16 = lax.broadcasted_iota(jnp.int32, (16, 128), 0)
    extra = jnp.concatenate(
        [answer[c * 16 + 12 : c * 16 + 14] for c in range(3)] + [jnp.zeros((10, entries), F32)], 0
    )
    for p in range(ranks):
        columns = slice(p // 4 * 128, p // 4 * 128 + 128)
        block = jnp.where(row16 < 6, pltpu.roll(extra[:, columns], (32 * (3 - p % 4)) % 128, 1), tile)
        for c in range(3):
            piece = answer[c * 16 : c * 16 + 16, columns]
            block = jnp.where(
                lane16 // 32 == c, pltpu.roll(piece, (32 * (c - p % 4)) % 128, 1), block
            )
        for t in range(3):
            payload[p, t] = block[t * 4 : t * 4 + 4]
    for copy in copies:
        copy.wait()


def combine_kernel(basis, factors, pressure):
    basis = basis()
    for x in range(pressure.shape[0]):
        total = 0.0
        for k in range(PITERS):
            total = total + factors[3 + k : 4 + k, 0:1] * basis[k, x]
        pressure[x] = total


def update_kernel(
    received, basis, displacement, solved_prev, solved_history, owner, slots, pressure_factors,
    new_displacement, wall, shares, *, ranks,
):
    summed = [sum(received[p, t] for p in range(ranks)) for t in range(3)]
    summed = jnp.concatenate(summed + [jnp.zeros((4, 128), F32)], 0)
    matrix = second_gram(summed)
    gram = [column_of(matrix, k) for k in range(SITERS + 5)]
    energy = summed[ENERGY_AT[0] : ENERGY_AT[0] + 1, ENERGY_AT[1] : ENERGY_AT[1] + 1]
    system = galerkin(gram[:SITERS], 0, S_SHIFT, S_BACK, energy)
    steps, share = eliminate(system, gram[0], 0)
    down = lax.broadcasted_iota(jnp.int32, (16, 1), 0)
    steps = jnp.where(down < SITERS, steps, 0.0)
    base, count = SITERS, 1 + solved_history.shape[0]
    with_moved = jnp.sum(matrix * steps, 0, keepdims=True)
    diagonal = at(matrix, 0) == at(matrix, 1)
    with_moved = jnp.sum(
        jnp.where(diagonal, jnp.broadcast_to(with_moved, matrix.shape), 0.0), 1, keepdims=True
    )
    with_newest = with_moved - gram[base]
    newest_moved = jnp.sum(steps * with_newest, 0, keepdims=True)
    newest_newest = newest_moved - with_newest[base : base + 1]
    columns = [jnp.where(down == base, newest_newest, with_newest)]
    for k in range(1, count):
        columns.append(jnp.where(down == base, with_newest[base + k : base + k + 1], gram[base + k]))
    right = jnp.where(down == base, newest_moved, with_moved)
    coefficients, newest_share = eliminate(columns, right, base)
    coefficients = -coefficients
    together = newest_moved + with_newest[base : base + 1] + 2.0 * gram[base][base : base + 1]
    kept = newest_newest / jnp.maximum(together, 1e-30)
    share = jnp.minimum(jnp.minimum(share, newest_share), jnp.minimum(kept, pressure_factors[0:1, 0:1]))
    shares[...] = jnp.broadcast_to(share, (8, 128))
    newest = row_of(coefficients, base)
    factors = jnp.where(
        down < base,
        (1.0 + newest) * steps,
        jnp.where(
            down == base,
            1.0 + newest,
            jnp.where(down < base + count, coefficients, jnp.where(down == base + count, -newest, 0.0)),
        ),
    )
    for c in range(3):
        total = row_of(factors, base) * displacement[c]
        for k in range(SITERS):
            total = total + row_of(factors, k) * basis[k, c]
        for k in range(count - 1):
            total = total + row_of(factors, base + 1 + k) * solved_history[k, c]
        total = total + row_of(factors, base + count) * solved_prev[c]
        new_displacement[c] = total
    row, group = at(summed, 0), at(summed, 1) // 32
    spare = jnp.where(row % 2 == 0, factors[12:13], factors[13:14])
    stacked = []
    for c in range(3):
        scales = jnp.where(group == c, factors, jnp.where((group == 3) & (row // 2 == c), spare, 0.0))
        scales = [scales[t * 4 : t * 4 + 4] for t in range(3)]
        for p in range(ranks):
            stacked.append(jnp.sum(sum(received[p, t] * scales[t] for t in range(3)), 0, keepdims=True))
    stacked = jnp.concatenate(stacked, 0)
    slot_row = lax.broadcasted_iota(jnp.int32, (128, 256), 0) & 31
    rank = lax.broadcasted_iota(jnp.int32, (ranks, 256), 0)
    for x in range(owner.shape[0]):
        pick = jnp.where(slot_row == slots[x : x + 1, :], 1.0, 0.0).astype(BF16)
        spread = split_dot(stacked, pick, 3)
        mine = rank == owner[x : x + 1, :]
        for c in range(3):
            wall[c : c + 1, x * 256 : x * 256 + 256] = jnp.sum(
                jnp.where(mine, spread[c * ranks : (c + 1) * ranks], 0.0), 0, keepdims=True
            )


def with_halo(cells, sides, width):
    for axis, dim in sides:
        count = lax.axis_size(axis)
        ends = count - 1
        head = lax.slice_in_dim(cells, 0, width, axis=dim)
        tail = lax.slice_in_dim(cells, cells.shape[dim] - width, cells.shape[dim], axis=dim)
        cells = jnp.concatenate(
            [
                lax.ppermute(tail, axis, [(i, (i + 1) % count) for i in range(ends)]),
                cells,
                lax.ppermute(head, axis, [((i + 1) % count, i) for i in range(ends)]),
            ],
            axis=dim,
        )
    return cells


def both_ways(core, axis):
    length = core.shape[axis]
    zero_slab = jnp.zeros_like(lax.slice_in_dim(core, 0, 1, axis=axis))
    ahead = jnp.concatenate([lax.slice_in_dim(core, 1, length, axis=axis), zero_slab], axis)
    behind = jnp.concatenate([zero_slab, lax.slice_in_dim(core, 0, length - 1, axis=axis)], axis)
    return (ahead, behind)


def grid_plane_sum(core):
    ahead_y, behind_y = both_ways(core, core.ndim - 2)
    ahead_z, behind_z = both_ways(core, core.ndim - 1)
    return ahead_y + behind_y + ahead_z + behind_z


def pressure_apply(field, shift):
    extended = with_halo(field, (("slab", 0),), 1)
    beside = extended[2:] + extended[:-2] + grid_plane_sum(field)
    return (6.0 + shift) * field - beside


def pressure_total(value):
    return lax.psum(value, "slab")


def grid_shell_apply(field, stiffness):
    extended = with_halo(field, (("slab", 1),), 1)
    ahead_c, behind_c = both_ways(field, 2)
    beside = extended[:, 2:] + extended[:, :-2] + ahead_c + behind_c
    return (4.0 + stiffness) * field - beside


def shell_total(value):
    return lax.psum(value, "slab")


def small_solve(gram, target):
    factor = jnp.linalg.cholesky(gram)
    gram_size = gram.shape[0]
    forward = []
    for across in range(gram_size):
        partial_sum = target[across] - sum(
            (factor[across, within] * forward[within] for within in range(across))
        )
        forward.append(partial_sum / factor[across, across])
    backward = [None] * gram_size
    for across in reversed(range(gram_size)):
        partial_sum = forward[across] - sum(
            (factor[within, across] * backward[within] for within in range(across + 1, gram_size))
        )
        backward[across] = partial_sum / factor[across, across]
    return jnp.stack(backward)


def step_by_step(
    velocity,
    pressure_shift,
    owner_rank,
    node_index,
    map_weight,
    shell_load,
    shell_stiffness,
    displacement,
    residual_prev,
    solved_prev,
    residual_history,
    solved_history,
):
    slab_count = lax.axis_size("slab")
    kept = residual_history.shape[0]
    shell_rows = displacement.shape[1]
    shell_cols = displacement.shape[2]
    node_count = shell_rows * shell_cols
    extended = with_halo(velocity, (("slab", 1),), 1)
    predicted = velocity + NU * (
        extended[:, 2:] + extended[:, :-2] + grid_plane_sum(velocity) - 6.0 * velocity
    )
    along_first = with_halo(predicted[0], (("slab", 0),), 1)
    ahead_y, behind_y = both_ways(predicted[1], 1)
    ahead_z, behind_z = both_ways(predicted[2], 2)
    spread = along_first[2:] - along_first[:-2] + ahead_y - behind_y + ahead_z - behind_z
    source = -0.5 * spread
    pressure = jnp.zeros_like(source)
    residual = source
    direction = source
    norm_now = pressure_total(jnp.sum(residual * residual))
    for sweep in range(PITERS):
        image = pressure_apply(direction, pressure_shift)
        step_size = norm_now / lax.psum(jnp.sum(direction * image), "slab")
        pressure = pressure + step_size * direction
        residual = residual - step_size * image
        norm_next = pressure_total(jnp.sum(residual * residual))
        direction = residual + norm_next / norm_now * direction
        norm_now = norm_next
    traction = jnp.stack(
        [
            MU * (predicted[0, :, 1, :] - predicted[0, :, 0, :]),
            WALL * pressure[:, 0, :],
            MU * (predicted[2, :, 1, :] - predicted[2, :, 0, :]),
        ]
    ).reshape(3, -1)
    owners = owner_rank[:, 0]
    ranks = jnp.arange(slab_count, dtype=jnp.int32)
    member = (owners[:, None] == ranks[None, :]).astype(jnp.int32)
    slots = jnp.sum((jnp.cumsum(member, 0) - 1) * member, 1)
    scaled = map_weight.astype(jnp.float32)
    packed = jnp.concatenate([traction * scaled[None, :], scaled[None, :]], 0).T
    send_values = (
        jnp.zeros((slab_count, 4, CAP), jnp.float32)
        .at[owners, :, slots]
        .set(packed)
        .reshape(slab_count, 4 * CAP)
    )
    send_nodes = (
        jnp.full((slab_count, CAP), node_count, jnp.int32).at[owners, slots].set(node_index)
    )
    got_values, got_nodes = (
        lax.all_to_all(send_values, "slab", split_axis=0, concat_axis=0, tiled=True),
        lax.all_to_all(send_nodes, "slab", split_axis=0, concat_axis=0, tiled=True),
    )
    flat_values = got_values.reshape(slab_count, 4, CAP).transpose(0, 2, 1).reshape(-1, 4)
    totals = jax.ops.segment_sum(flat_values, got_nodes.reshape(-1), num_segments=node_count + 1)[
        :node_count
    ]
    force = (totals[:, :3] / jnp.maximum(totals[:, 3], 1.0)[:, None]).T.reshape(
        3, shell_rows, shell_cols
    )
    shell_source = force + shell_load
    solved = displacement
    residual = shell_source - grid_shell_apply(solved, shell_stiffness)
    direction = residual
    norm_now = shell_total(jnp.sum(residual * residual))
    for sweep in range(SITERS):
        image = grid_shell_apply(direction, shell_stiffness)
        step_size = norm_now / lax.psum(jnp.sum(direction * image), "slab")
        solved = solved + step_size * direction
        residual = residual - step_size * image
        norm_next = shell_total(jnp.sum(residual * residual))
        direction = residual + norm_next / norm_now * direction
        norm_now = norm_next
    moved = solved - displacement
    newest_v = moved - residual_prev
    newest_w = solved - solved_prev
    columns = jnp.concatenate([newest_v[None], residual_history], 0).reshape(kept + 1, -1)
    outputs_w = jnp.concatenate([newest_w[None], solved_history], 0)
    moved_flat = moved.reshape(-1)
    gram_local = jnp.dot(columns, columns.T, precision=lax.Precision.HIGHEST)
    target_local = jnp.dot(columns, moved_flat, precision=lax.Precision.HIGHEST)
    gram, target = lax.psum((gram_local, target_local), "slab")
    coefficients = -small_solve(gram, target)
    new_displacement = solved + jnp.einsum(
        "k,kabc->abc", coefficients, outputs_w, precision=lax.Precision.HIGHEST
    )
    shell_flat = new_displacement.reshape(3, node_count)
    requested = jnp.minimum(got_nodes, node_count - 1)
    answers = shell_flat[:, requested].transpose(1, 0, 2)
    returned = lax.all_to_all(answers, "slab", split_axis=0, concat_axis=0, tiled=True)
    wall_displacement = returned[owners, :, slots].T
    return (pressure, new_displacement, wall_displacement)


def on_device(
    velocity,
    pressure_shift,
    owner_rank,
    node_index,
    map_weight,
    shell_load,
    shell_stiffness,
    displacement,
    residual_prev,
    solved_prev,
    residual_history,
    solved_history,
):
    ranks = lax.axis_size("slab")
    layers = velocity.shape[1]
    kept = residual_history.shape[0]

    def with_mate(values):
        return lax.ppermute(values, "slab", [(i, i ^ 1) for i in range(ranks)])

    def with_other(values):
        pairs = [(i, i + 1) for i in range(1, ranks - 1, 2)]
        return lax.ppermute(values, "slab", pairs + [(j, i) for i, j in pairs])

    node = node_index.reshape(layers, -1)
    weight = map_weight.reshape(layers, -1)
    plane = shape(*velocity.shape[2:])

    to_mate, to_other, own_left, own_right = call(
        edge_kernel,
        (shape(HALO_ROWS, 128), shape(HALO_ROWS, 128), plane, plane),
        (velocity, displacement),
        outer=(0, 1),
        stored=(0, 1),
        scratch=(
            pltpu.VMEM(velocity.shape, F32),
            pltpu.VMEM(displacement.shape, F32),
            pltpu.SemaphoreType.DMA((4, max(layers, 1))),
        ),
    )
    halo_other, halo_mate = with_other(to_other), with_mate(to_mate)
    shift_other, shift_mate = with_other(pressure_shift), with_mate(pressure_shift)
    source, wall = call(fluid_kernel, (shape(*velocity.shape[1:]), shape(8, 256)), (velocity,))
    slots, owner = call(
        lambda *refs: slots_kernel(*refs, ranks=ranks),
        (shape(layers, 256, dtype=jnp.int32), shape(layers, 256, dtype=jnp.int32)),
        (owner_rank.T,),
    )
    fields, first, shell, wall = call(
        lambda *refs: source_kernel(*refs),
        (shape(FIELD_ROWS, 128), shape(128, 128), shape(SHELL_ROWS, 128), shape(8, 256)),
        (
            source, wall, own_left, own_right, halo_mate, halo_other,
            displacement, shell_load, shell_stiffness,
        ),
        pairs=(4,),
    )
    beyond = lax.ppermute(first, "slab", [(i, i - 2) for i in range(2, ranks)])
    fields_other, fields_mate = with_other(fields), with_mate(fields)
    shell_other, shell_mate = with_other(shell), with_mate(shell)
    payload, pressure_basis = call(
        lambda *refs: pressure_kernel(*refs, ranks=ranks),
        (shape(ranks, 8, 128), pltpu.HBM((PITERS, *pressure_shift.shape), F32)),
        (
            fields, fields_mate, fields_other, beyond, pressure_shift, shift_mate, shift_other,
            wall, owner, slots, node, weight,
        ),
        direct=(1,),
        scratch=(
            pltpu.VMEM((PITERS, 13, 64, 256), F32),
            pltpu.SemaphoreType.DMA((PITERS,)),
        ),
    )
    received = lax.all_to_all(payload, "slab", split_axis=0, concat_axis=0, tiled=True)
    entries = ranks * CAP
    forces, requests, fixed, factors = call(
        lambda *refs: force_kernel(*refs, ranks=ranks),
        (
            shape(3, 3 * displacement.shape[1], displacement.shape[2]),
            shape(8, entries, dtype=jnp.int32), shape(24, entries), shape(8, 128),
        ),
        (received, displacement, solved_prev, solved_history),
        scratch=(pltpu.VMEM((8, 8 * 24, 128), F32),),
    )
    payload, shell_basis = call(
        lambda *refs: shell_kernel(*refs, ranks=ranks),
        (shape(ranks, 3, 4, 128), pltpu.HBM((SITERS, *displacement.shape), F32)),
        (
            forces, requests, fixed, shell, shell_mate, shell_other, residual_prev, residual_history,
        ),
        direct=(1,),
        scratch=(
            pltpu.VMEM((SITERS, 3, 24, 1024), F32),
            pltpu.VMEM((72, 1024), F32),
            pltpu.VMEM((8, 8 * 24, 128), F32),
            pltpu.SemaphoreType.DMA((SITERS,)),
        ),
    )
    answers = lax.all_to_all(payload, "slab", split_axis=0, concat_axis=0, tiled=True)
    (pressure,) = call(
        combine_kernel,
        (shape(*pressure_shift.shape),),
        (pressure_basis, factors),
        late=(0,),
        stored=(0,),
    )
    new_displacement, wall_displacement, shares = call(
        lambda *refs: update_kernel(*refs, ranks=ranks),
        (shape(*displacement.shape), shape(3, owner_rank.shape[0]), shape(8, 128)),
        (answers, shell_basis, displacement, solved_prev, solved_history, owner, slots, factors),
    )
    return lax.cond(
        shares[0, 0] > LEAST_SHARE,
        lambda: (pressure, new_displacement, wall_displacement),
        lambda: step_by_step(
            velocity, pressure_shift, owner_rank, node_index, map_weight, shell_load, shell_stiffness,
            displacement, residual_prev, solved_prev, residual_history, solved_history,
        ),
    )


def solution(mesh):
    in_specs = (
        P(None, ("groups", "slab"), None, None),
        P(("groups", "slab"), None, None),
        P(("groups", "slab"), None),
        P(("groups", "slab")),
        P(("groups", "slab")),
        P(None, ("groups", "slab"), None),
        P(("groups", "slab"), None),
        P(None, ("groups", "slab"), None),
        P(None, ("groups", "slab"), None),
        P(None, ("groups", "slab"), None),
        P(None, None, ("groups", "slab"), None),
        P(None, None, ("groups", "slab"), None),
    )
    out_specs = (
        P(("groups", "slab"), None, None),
        P(None, ("groups", "slab"), None),
        P(None, ("groups", "slab")),
    )
    return jax.shard_map(
        on_device, mesh=mesh, in_specs=in_specs, out_specs=out_specs, check_vma=False
    )
```
